32 devices in a mesh: fsdp: 8 (over z, x), ctx: 2 (over y), tp: 2 (over core).
Axes of the slice: x: 2, y: 2, z: 4, core: 2. Of those that a mesh axis runs over, the one named last changes fastest.
Arguments:
- inputs: bfloat16 [8, 640, 1536], P('fsdp', 'ctx'), may hold values from -6 to 6
- conditioning: bfloat16 [8, 130, 768], P('fsdp'), may hold values from -6 to 6
- query_matrix: bfloat16 [1536, 1536], P(('fsdp', 'ctx'), 'tp'), may hold values from -0.15625 to 0.15625
- key_matrix: bfloat16 [1536, 1536], P(('fsdp', 'ctx'), 'tp'), may hold values from -0.15625 to 0.15625
- value_matrix: bfloat16 [1536, 1536], P(('fsdp', 'ctx'), 'tp'), may hold values from -0.15625 to 0.15625
- output_matrix: bfloat16 [1536, 1536], P('tp', ('fsdp', 'ctx')), may hold values from -1.25 to 1.25
- cross_query: bfloat16 [1536, 1536], P(('fsdp', 'ctx'), 'tp'), may hold values from -0.15625 to 0.15625
- cross_key: bfloat16 [768, 1536], P(('fsdp', 'ctx'), 'tp'), may hold values from -0.21875 to 0.21875
- cross_value: bfloat16 [768, 1536], P(('fsdp', 'ctx'), 'tp'), may hold values from -0.21875 to 0.21875
- cross_output: bfloat16 [1536, 1536], P('tp', ('fsdp', 'ctx')), may hold values from -0.625 to 0.625
- gate_matrix: bfloat16 [1536, 6144], P(('fsdp', 'ctx'), 'tp'), may hold values from -0.15625 to 0.15625
- up_matrix: bfloat16 [1536, 6144], P(('fsdp', 'ctx'), 'tp'), may hold values from -0.15625 to 0.15625
- down_matrix: bfloat16 [6144, 1536], P('tp', ('fsdp', 'ctx')), may hold values from -0.078125 to 0.078125
- first_gain: bfloat16 [1536], P(('fsdp', 'ctx')), may hold values from 0.099609375 to 1.8984375
- second_gain: bfloat16 [1536], P(('fsdp', 'ctx')), may hold values from 0.099609375 to 1.8984375
- third_gain: bfloat16 [1536], P(('fsdp', 'ctx')), may hold values from 0.099609375 to 1.8984375
- cotangent: bfloat16 [8, 640, 1536], P('fsdp', 'ctx'), may hold values from -6 to 6
Outputs:
- layer_output: float32 [8, 640, 1536], P('fsdp', 'ctx')
- inputs_gradient: float32 [8, 640, 1536], P('fsdp', 'ctx')
- conditioning_gradient: float32 [8, 130, 768], P('fsdp')
- query_gradient: float32 [1536, 1536], P(('fsdp', 'ctx'), 'tp')
- key_gradient: float32 [1536, 1536], P(('fsdp', 'ctx'), 'tp')
- value_gradient: float32 [1536, 1536], P(('fsdp', 'ctx'), 'tp')
- output_gradient: float32 [1536, 1536], P('tp', ('fsdp', 'ctx'))
- cross_query_gradient: float32 [1536, 1536], P(('fsdp', 'ctx'), 'tp')
- cross_key_gradient: float32 [768, 1536], P(('fsdp', 'ctx'), 'tp')
- cross_value_gradient: float32 [768, 1536], P(('fsdp', 'ctx'), 'tp')
- cross_output_gradient: float32 [1536, 1536], P('tp', ('fsdp', 'ctx'))
- gate_gradient: float32 [1536, 6144], P(('fsdp', 'ctx'), 'tp')
- up_gradient: float32 [1536, 6144], P(('fsdp', 'ctx'), 'tp')
- down_gradient: float32 [6144, 1536], P('tp', ('fsdp', 'ctx'))
- first_gain_gradient: float32 [1536], P(('fsdp', 'ctx'))
- second_gain_gradient: float32 [1536], P(('fsdp', 'ctx'))
- third_gain_gradient: float32 [1536], P(('fsdp', 'ctx'))
The draws below stay inside these ranges and needn't reach their ends.
All inputs are finite; a program needn't handle non-finite values.
Results may differ from the reference program's by a relative error of at most 0.02.
Values may be sent and summed in bfloat16 or wider, within the bound.
No kernel may reach another device: no remote copies, remote signals or barrier semaphores. Data moves between devices by JAX's collectives and lax.ppermute only.
A program may use at most 256 MiB of HBM per device.

```python
import math
import jax
import jax.numpy as jnp
from jax import lax

D = 1536
HEADS = 24
HDIM = 64
FF = 6144
CDIM = 768
CTOK = 130
SEQ_LEN = 640
SEQS = 8


def raised(values, stream_key, source, target, blocks, factor):
    owner, partner = [(jnp.arange(values.shape[dim]) // (values.shape[dim] // blocks)).reshape([-1 if axis == dim else 1 for axis in range(values.ndim)]) for dim in (source, target)]
    chosen = jax.random.permutation(stream_key, blocks)[partner]
    strong = (owner == chosen) | (owner == (partner + blocks // 2) % blocks)
    return jnp.where(strong, factor * values, values)


def level_of(key, dims, cuts, least, top_value):
    def one(dim, blocks):
        steps = jax.random.uniform(jax.random.fold_in(jax.random.fold_in(key, 6), dim), (blocks,), jnp.float32, least / len(cuts), top_value / len(cuts))
        return jnp.repeat(jnp.exp(steps), dims[dim] // blocks).reshape((-1,) + (1,) * (len(dims) - dim - 1))

    level = one(*cuts[0])
    for cut in cuts[1:]:
        level = level * one(*cut)
    return level


def normal_values(stream_key, extent, scale, bound, cuts=(), held_as=jnp.bfloat16):
    array = jax.random.normal(stream_key, extent, jnp.float32) * scale
    if len(cuts) > 0:
        array = level_of(stream_key, extent, cuts, -0.22, 0.18) * array
    return jnp.clip(array, min=-bound, max=bound).astype(held_as)


def heavy_noise(rng, dims, scale, limit, split, heavy, kind=jnp.bfloat16):
    array = scale * jax.random.normal(rng, dims, jnp.float32)
    if split:
        array = array * level_of(rng, dims, split, -0.22, 0.18)
    return jnp.clip(raised(array, jax.random.fold_in(rng, 3), *heavy), -limit, limit).astype(kind)


def setup_inputs(seed: int = 0) -> dict:
    key_of = jax.random.split(jax.random.key(seed), 18)
    inputs = heavy_noise(key_of[0], (SEQS, SEQ_LEN, D), 1.0, 6.0, ((0, 8), (1, 2)), (0, 2, 8, 2.0))
    conditioning = normal_values(key_of[1], (SEQS, CTOK, CDIM), 1.0, 6.0, ((0, 8),))
    query_matrix = normal_values(key_of[2], (D, D), D ** -0.5, 0.15625, ((0, 16), (1, 2)))
    key_matrix = normal_values(key_of[3], (D, D), D ** -0.5, 0.15625, ((0, 16), (1, 2)))
    value_matrix = normal_values(key_of[4], (D, D), D ** -0.5, 0.15625, ((0, 16), (1, 2)))
    output_matrix = normal_values(key_of[5], (D, D), (D // 64) ** -0.5, 1.25, ((0, 2), (1, 16)))
    cross_query = normal_values(key_of[6], (D, D), D ** -0.5, 0.15625, ((0, 16), (1, 2)))
    cross_key = normal_values(key_of[7], (CDIM, D), CDIM ** -0.5, 0.21875, ((0, 16), (1, 2)))
    cross_value = normal_values(key_of[8], (CDIM, D), CDIM ** -0.5, 0.21875, ((0, 16), (1, 2)))
    cross_output = normal_values(key_of[9], (D, D), (D // 16) ** -0.5, 0.625, ((0, 2), (1, 16)))
    gate_matrix = normal_values(key_of[10], (D, FF), D ** -0.5, 0.15625, ((0, 16), (1, 2)))
    up_matrix = normal_values(key_of[11], (D, FF), D ** -0.5, 0.15625, ((0, 16), (1, 2)))
    down_matrix = normal_values(key_of[12], (FF, D), FF ** -0.5, 0.078125, ((0, 2), (1, 16)))
    first_gain = jnp.clip(1.0 + 0.18 * jax.random.normal(key_of[13], (D,), jnp.float32), 0.099609375, 1.8984375).astype(jnp.bfloat16)
    second_gain = jnp.clip(1.0 + 0.18 * jax.random.normal(key_of[14], (D,), jnp.float32), 0.099609375, 1.8984375).astype(jnp.bfloat16)
    third_gain = jnp.clip(1.0 + 0.18 * jax.random.normal(key_of[15], (D,), jnp.float32), 0.099609375, 1.8984375).astype(jnp.bfloat16)
    cotangent = heavy_noise(key_of[16], (SEQS, SEQ_LEN, D), 1.0, 6.0, ((0, 8), (1, 2)), (0, 2, 8, 2.0))
    return {"inputs": inputs, "conditioning": conditioning, "query_matrix": query_matrix, "key_matrix": key_matrix, "value_matrix": value_matrix, "output_matrix": output_matrix, "cross_query": cross_query, "cross_key": cross_key, "cross_value": cross_value, "cross_output": cross_output, "gate_matrix": gate_matrix, "up_matrix": up_matrix, "down_matrix": down_matrix, "first_gain": first_gain, "second_gain": second_gain, "third_gain": third_gain, "cotangent": cotangent}


EPSILON = 1e-05
HIGHEST = lax.Precision.HIGHEST

@jax.custom_vjp
def low(v):
    return lax.optimization_barrier(v.astype(jnp.bfloat16)).astype(jnp.float32)

@jax.custom_vjp
def low_back(v):
    return v

def low_keep(v):
    return (low(v), None)

def low_pass(kept, grad):
    return (grad,)

def back_keep(v):
    return (v, None)

def back_low(kept, grad):
    return (low(grad),)
low.defvjp(low_keep, low_pass)
low_back.defvjp(back_keep, back_low)

def matmul(left, right):
    return jnp.dot(left, right, precision=HIGHEST, preferred_element_type=jnp.float32)

def layer_norm(values, norm_gain):
    center = values - lax.optimization_barrier(jnp.mean(values, axis=-1, keepdims=True))
    spread = lax.optimization_barrier(jnp.mean(center * center, axis=-1, keepdims=True))
    return center * lax.rsqrt(spread + EPSILON) * norm_gain

def rotary_tables(length, head_size):
    position = jnp.arange(length).astype(jnp.float32)
    rotated = head_size // 2
    middle = rotated // 2
    frequency = jnp.exp(-(2.0 * jnp.arange(middle).astype(jnp.float32) / rotated) * math.log(10000.0))
    angles = position[:, None] * frequency[None, :]
    return (jnp.cos(angles)[:, None, :], jnp.sin(angles)[:, None, :])

def rotate(values, cosine, sine_table):
    middle = cosine.shape[-1]
    first_half = values[..., :middle]
    second_half = values[..., middle:2 * middle]
    passing = values[..., 2 * middle:]
    return jnp.concatenate([first_half * cosine - second_half * sine_table, second_half * cosine + first_half * sine_table, passing], axis=-1)

def attend(queries, keys, values):
    query_heads = queries.reshape(queries.shape[0], HEADS, HDIM)
    key_heads = keys.reshape(keys.shape[0], HEADS, HDIM)
    value_heads = values.reshape(values.shape[0], HEADS, HDIM)
    scores = low_back(jnp.einsum('qhd,khd->hqk', query_heads, key_heads, precision=HIGHEST) * HDIM ** (-0.5))
    probability = low(jax.nn.softmax(scores, axis=-1))
    mixture = jnp.einsum('hqk,khd->qhd', probability, value_heads, precision=HIGHEST)
    return mixture.reshape(queries.shape[0], D)

def one_sequence(tokens, context, cosine, sine_table, query_matrix, key_matrix, value_matrix, output_matrix, cross_query, cross_key, cross_value, cross_output, gate_matrix, up_matrix, down_matrix, first_gain, second_gain, third_gain):
    length = tokens.shape[0]
    normed_one = low(layer_norm(tokens, first_gain))
    query_raw = low_back(matmul(normed_one, query_matrix)).reshape(length, HEADS, HDIM)
    key_raw = low_back(matmul(normed_one, key_matrix)).reshape(length, HEADS, HDIM)
    value_low = low_back(low(matmul(normed_one, value_matrix)))
    query_rot = low(rotate(query_raw, cosine, sine_table)).reshape(length, D)
    key_rot = low(rotate(key_raw, cosine, sine_table)).reshape(length, D)
    self_low = low_back(low(attend(query_rot, key_rot, value_low)))
    hidden_one = tokens + low_back(matmul(self_low, output_matrix))
    normed_two = low(layer_norm(hidden_one, second_gain))
    cross_query_low = low_back(low(matmul(normed_two, cross_query)))
    cross_key_low = low(matmul(context, cross_key))
    cross_value_low = low(matmul(context, cross_value))
    cross_low = low_back(low(attend(cross_query_low, cross_key_low, cross_value_low)))
    hidden_two = hidden_one + low_back(matmul(cross_low, cross_output))
    normed_three = low(layer_norm(hidden_two, third_gain))
    gate_value = low_back(matmul(normed_three, gate_matrix))
    up_value = low_back(matmul(normed_three, up_matrix))
    feed_low = low_back(low(jax.nn.silu(gate_value) * up_value))
    return hidden_two + low_back(matmul(feed_low, down_matrix))

def reference(inputs, conditioning, query_matrix, key_matrix, value_matrix, output_matrix, cross_query, cross_key, cross_value, cross_output, gate_matrix, up_matrix, down_matrix, first_gain, second_gain, third_gain, cotangent):
    cosine, sine_table = rotary_tables(SEQ_LEN, HDIM)
    params = tuple((item.astype(jnp.float32) for item in (query_matrix, key_matrix, value_matrix, output_matrix, cross_query, cross_key, cross_value, cross_output, gate_matrix, up_matrix, down_matrix, first_gain, second_gain, third_gain)))

    def forward(tokens, contexts, *weights):

        def per_sequence(items):
            return jax.checkpoint(one_sequence)(items[0], items[1], cosine, sine_table, *weights)
        return lax.map(per_sequence, (tokens, contexts))
    outputs, pullback = jax.vjp(forward, inputs.astype(jnp.float32), conditioning.astype(jnp.float32), *params)
    grads = pullback(cotangent.astype(jnp.float32))
    return (outputs, grads[0], grads[1], grads[2], grads[3], grads[4], grads[5], grads[6], grads[7], grads[8], grads[9], grads[10], grads[11], grads[12], grads[13], grads[14], grads[15])
```

```python
import functools
import math

import jax
import jax.numpy as jnp
from jax import lax
from jax.experimental import pallas as pl
from jax.experimental.pallas import tpu as pltpu
from jax.sharding import PartitionSpec as P

HDIM = 64
EPSILON = 1e-05
F32 = jnp.float32
BF16 = jnp.bfloat16
SCALE = HDIM ** (-0.5)
PAIR = 2 * HDIM
VMEM_LIMIT = 48 * 1024 * 1024


def mm(left, right):
    return lax.dot_general(left, right, (((1,), (0,)), ((), ())), preferred_element_type=F32)


def mm_tn(left, right):
    return lax.dot_general(left, right, (((0,), (0,)), ((), ())), preferred_element_type=F32)


def mm_nt(left, right):
    return lax.dot_general(left, right, (((1,), (1,)), ((), ())), preferred_element_type=F32)


def norm_stats(values):
    center = values - jnp.mean(values, axis=-1, keepdims=True)
    rate = lax.rsqrt(jnp.mean(center * center, axis=-1, keepdims=True) + EPSILON)
    return center * rate, rate


def norm_low(values, gain):
    return (norm_stats(values)[0] * gain).astype(BF16)


def norm_backward(values, gain, upstream):
    unit, rate = norm_stats(values)
    scaled = upstream * gain
    back = rate * (
        scaled
        - jnp.mean(scaled, axis=-1, keepdims=True)
        - unit * jnp.mean(scaled * unit, axis=-1, keepdims=True)
    )
    return back, jnp.sum(upstream * unit, axis=0)


def turned(values, cosine, upper, lower):
    width = values.shape[1]
    return (
        values * cosine
        + pltpu.roll(values, width - HDIM // 4, 1) * upper
        + pltpu.roll(values, HDIM // 4, 1) * lower
    )


def chunk_of(rows):
    return 128 if rows % 128 == 0 else rows


def scores_of(query, key, valid):
    scores = mm_nt(query, key) * SCALE
    if valid < key.shape[0]:
        column = lax.broadcasted_iota(jnp.int32, scores.shape, 1)
        scores = jnp.where(column < valid, scores, -1e30)
    return scores


def forward_heads(q_ref, k_ref, v_ref, o_ref, lse_ref, valid):
    rows = q_ref.shape[0]
    step = chunk_of(rows)
    for head in range(2):
        cols = slice(head * HDIM, (head + 1) * HDIM)
        key, value = k_ref[:, cols], v_ref[:, cols]
        for first in range(0, rows, step):
            part = slice(first, first + step)
            scores = scores_of(q_ref[part, cols], key, valid)
            peak = jnp.max(scores, axis=-1, keepdims=True)
            shifted = jnp.exp(scores - peak)
            total = jnp.sum(shifted, axis=-1, keepdims=True)
            probability = (shifted * (1.0 / total)).astype(BF16)
            o_ref[part, cols] = mm(probability, value).astype(BF16)
            lse_ref[part, cols] = jnp.broadcast_to(peak + jnp.log(total), (step, HDIM))


def self_forward_kernel(
    q_ref, k_ref, v_ref, cos_ref, up_ref, low_ref, qr_ref, kr_ref, o_ref, lse_ref
):
    tables = cos_ref[...], up_ref[...], low_ref[...]
    qr_ref[...] = turned(q_ref[...], *tables).astype(BF16)
    kr_ref[...] = turned(k_ref[...], *tables).astype(BF16)
    forward_heads(qr_ref, kr_ref, v_ref, o_ref, lse_ref, kr_ref.shape[0])


def cross_forward_kernel(valid, q_ref, k_ref, v_ref, o_ref, lse_ref):
    forward_heads(q_ref, k_ref, v_ref, o_ref, lse_ref, valid)


def backward_heads(q_ref, k_ref, v_ref, do_ref, lse_ref, dq_ref, dk_ref, dv_ref, valid):
    rows = q_ref.shape[0]
    step = chunk_of(rows)
    for head in range(2):
        cols = slice(head * HDIM, (head + 1) * HDIM)
        key, value = k_ref[:, cols], v_ref[:, cols]
        for first in range(0, rows, step):
            part = slice(first, first + step)
            query, grad = q_ref[part, cols], do_ref[part, cols]
            scores = scores_of(query, key, valid)
            probability = jnp.exp(scores - lse_ref[part, cols][:, :1])
            prob_grad = mm_nt(grad, value)
            mean_grad = jnp.sum(probability * prob_grad, axis=-1, keepdims=True)
            score_grad = (probability * (prob_grad - mean_grad)).astype(BF16)
            dq_ref[part, cols] = mm(score_grad, key) * SCALE
            key_term = mm_tn(score_grad, query) * SCALE
            value_term = mm_tn(probability.astype(BF16), grad)
            if first == 0:
                dk_ref[:, cols] = key_term
                dv_ref[:, cols] = value_term
            else:
                dk_ref[:, cols] += key_term
                dv_ref[:, cols] += value_term


def self_backward_kernel(
    q_ref, k_ref, v_ref, do_ref, lse_ref, cos_ref, up_ref, low_ref,
    dq_ref, dk_ref, dv_ref, dq_acc, dk_acc, dv_acc,
):
    backward_heads(
        q_ref, k_ref, v_ref, do_ref, lse_ref, dq_acc, dk_acc, dv_acc, k_ref.shape[0]
    )
    tables = cos_ref[...], -up_ref[...], -low_ref[...]
    dq_ref[...] = turned(dq_acc[...], *tables).astype(BF16)
    dk_ref[...] = turned(dk_acc[...], *tables).astype(BF16)
    dv_ref[...] = dv_acc[...].astype(BF16)


def cross_backward_kernel(
    valid, q_ref, k_ref, v_ref, do_ref, lse_ref, dq_ref, dk_ref, dv_ref, dq_acc
):
    backward_heads(q_ref, k_ref, v_ref, do_ref, lse_ref, dq_acc, dk_ref, dv_ref, valid)
    dq_ref[...] = dq_acc[...].astype(BF16)


def pair_block(rows):
    return pl.BlockSpec((rows, PAIR), lambda pair: (0, pair))


def fixed_block(rows):
    return pl.BlockSpec((rows, PAIR), lambda pair: (0, 0))


def shape(rows, cols, kind):
    return jax.ShapeDtypeStruct((rows, cols), kind)


def attention_call(kernel, cols, rows_in, fixed, outs, scratch=(), flops=0):
    return pl.pallas_call(
        kernel,
        grid=(cols // PAIR,),
        in_specs=[pair_block(r) for r in rows_in] + [fixed_block(r) for r in fixed],
        out_specs=[pair_block(r) for r, _ in outs],
        out_shape=[shape(r, cols, kind) for r, kind in outs],
        scratch_shapes=[pltpu.VMEM((r, PAIR), F32) for r in scratch],
        compiler_params=pltpu.CompilerParams(vmem_limit_bytes=VMEM_LIMIT),
        cost_estimate=pl.CostEstimate(
            flops=flops, bytes_accessed=sum(r * cols * 4 for r in rows_in), transcendentals=flops // 256
        ),
    )


def self_forward(query, key, value, tables):
    rows, cols = query.shape
    return attention_call(
        self_forward_kernel, cols, (rows,) * 3, (rows,) * 3,
        ((rows, BF16), (rows, BF16), (rows, BF16), (rows, F32)),
        flops=4 * rows * rows * cols,
    )(query, key, value, *tables)


def self_backward(query, key, value, grad, lse, tables):
    rows, cols = query.shape
    return attention_call(
        self_backward_kernel, cols, (rows,) * 5, (rows,) * 3,
        ((rows, BF16),) * 3, (rows,) * 3, flops=10 * rows * rows * cols,
    )(query, key, value, grad, lse, *tables)


def cross_forward(query, key, value, valid):
    rows, cols = query.shape
    keys = key.shape[0]
    return attention_call(
        functools.partial(cross_forward_kernel, valid), cols, (rows, keys, keys), (),
        ((rows, BF16), (rows, F32)), flops=4 * rows * keys * cols,
    )(query, key, value)


def cross_backward(query, key, value, grad, lse, valid):
    rows, cols = query.shape
    keys = key.shape[0]
    return attention_call(
        functools.partial(cross_backward_kernel, valid), cols, (rows, keys, keys, rows, rows), (),
        ((rows, BF16), (keys, F32), (keys, F32)), (rows,), flops=10 * rows * keys * cols,
    )(query, key, value, grad, lse)


def rotary_tables(position):
    quarter = HDIM // 4
    frequency = jnp.exp(
        -(2.0 * jnp.arange(quarter).astype(F32) / (2 * quarter)) * math.log(10000.0)
    )
    angles = position.astype(F32)[:, None] * frequency[None, :]
    cosine, sine = jnp.cos(angles), jnp.sin(angles)
    none = jnp.zeros_like(sine)
    rest = jnp.zeros((position.shape[0], HDIM // 2), F32)
    return tuple(
        jnp.concatenate(parts + parts, axis=1)
        for parts in (
            [cosine, cosine, rest + 1.0],
            [-sine, none, rest],
            [none, sine, rest],
        )
    )


class Links:
    def __init__(self, mesh):
        self.fsdp = mesh.shape["fsdp"]
        self.ring = 4 if self.fsdp % 4 == 0 else 1
        self.width = self.fsdp // self.ring
        index = lax.axis_index("fsdp")
        self.at = index // self.width
        self.lane = index % self.width
        self.half = lax.axis_index("ctx")
        self.core = lax.axis_index("tp")

    def over_ring(self, value, hops=1):
        z, r = self.ring, self.width
        pairs = [(a * r + b, (a + hops) % z * r + b) for a in range(z) for b in range(r)]
        return lax.ppermute(value, "fsdp", pairs)

    def over_lanes(self, value, hops=1):
        z, r = self.ring, self.width
        pairs = [(a * r + b, a * r + (b + hops) % r) for a in range(z) for b in range(r)]
        return lax.ppermute(value, "fsdp", pairs)

    def over_half(self, value):
        return lax.ppermute(value, "ctx", [(0, 1), (1, 0)])

    def over_core(self, value):
        return lax.ppermute(value, "tp", [(0, 1), (1, 0)])

    def ring_at(self, back):
        return (self.at - back) % self.ring

    def lane_at(self, back):
        return (self.lane - back) % self.width


    def share(self, own):
        pair = jnp.concatenate([own, self.over_half(own)], axis=0)
        return jnp.concatenate([pair, self.over_core(pair)], axis=0)

    def reduce(self, partial):
        rows = partial.shape[0] // 2
        mine = partial[:rows] + self.over_core(partial[rows:].astype(BF16)).astype(F32)
        rows //= 2
        return mine[:rows] + self.over_half(mine[rows:].astype(BF16)).astype(F32)

    def both_cores(self, own):
        other = self.over_core(own)
        first = jnp.where(self.core == 0, own, other)
        second = jnp.where(self.core == 0, other, own)
        return jnp.concatenate([first, second], axis=0)


    def share_ring(self, own):
        parts = [own]
        for _ in range(self.ring - 1):
            parts.append(self.over_ring(parts[-1]))
        mine = jnp.concatenate(parts, axis=0)
        return jnp.concatenate([mine, self.over_core(mine)], axis=0)

    def reduce_ring(self, partial):
        rows = partial.shape[0] // 2
        mine = partial[:rows] + self.over_core(partial[rows:].astype(BF16)).astype(F32)
        rows //= self.ring
        parts = [mine[k * rows : (k + 1) * rows] for k in range(self.ring)]
        total = None
        for back in list(range(1, self.ring)) + [0]:
            total = parts[back] if total is None else total + parts[back]
            if back:
                total = self.over_ring(total.astype(BF16)).astype(F32)
        return total


    def gather_pack(self, shards):
        m, rows, cols = shards.shape
        cols //= 2
        halves = shards.reshape(m, rows, 2, cols)
        keep = lax.dynamic_index_in_dim(halves, self.half, 2, keepdims=False)
        send = lax.dynamic_index_in_dim(halves, 1 - self.half, 2, keepdims=False)
        recv = self.over_half(send)
        unit = jnp.where(
            self.half == 0, jnp.stack([keep, recv], 1), jnp.stack([recv, keep], 1)
        ).reshape(m, 1, 2 * rows, cols)
        whole = jnp.zeros((m, self.fsdp, 2 * rows, cols), shards.dtype)
        for back in range(self.ring):
            piece = unit
            for turn in range(self.width):
                place = self.ring_at(back) * self.width + self.lane_at(turn)
                whole = lax.dynamic_update_slice(whole, piece, (0, place, 0, 0))
                if turn < self.width - 1:
                    piece = self.over_lanes(piece)
            if back < self.ring - 1:
                unit = self.over_ring(unit)
        return whole

    def scatter_pack(self, grads):
        m, _, rows, cols = grads.shape

        def block(back, turn):
            place = self.ring_at(back) * self.width + self.lane_at(turn)
            return lax.dynamic_slice(grads, (0, place, 0, 0), (m, 1, rows, cols))

        def over_width(back):
            total = None
            for turn in list(range(1, self.width)) + [0]:
                term = block(back, turn)
                total = term if total is None else total.astype(F32) + term.astype(F32)
                if turn:
                    total = self.over_lanes(total.astype(BF16))
            return total.astype(F32)

        sums = {back: over_width(back) for back in list(range(1, self.ring)) + [0]}
        total = None
        for back in list(range(1, self.ring)) + [0]:
            total = sums[back] if total is None else total + sums[back]
            if back:
                total = self.over_ring(total.astype(BF16)).astype(F32)
        total = total.reshape(m, 2, rows // 2, cols)
        keep = lax.dynamic_index_in_dim(total, self.half, 1, keepdims=False)
        send = lax.dynamic_index_in_dim(total, 1 - self.half, 1, keepdims=False).astype(BF16)
        recv = self.over_half(send).astype(F32)
        return jnp.where(
            self.half == 0,
            jnp.concatenate([keep, recv], -1),
            jnp.concatenate([recv, keep], -1),
        )


    def gather_feed(self, shards):
        m, rows, cols = shards.shape
        cols //= self.ring
        parts = shards.reshape(m, rows, self.ring, cols)

        def part(ahead):
            index = (self.at + ahead) % self.ring
            return lax.dynamic_index_in_dim(parts, index, 2, keepdims=False)

        pieces = [part(0)] + [self.over_ring(part(k), k) for k in range(1, self.ring)]
        group = max(1, self.ring // 2)
        whole = jnp.zeros((m, self.ring, self.width, 2, rows, cols), shards.dtype)

        def put(whole, values, backs, turn, half):
            for n, back in enumerate(backs):
                spot = (0, self.ring_at(back), self.lane_at(turn), half, 0, 0)
                whole = lax.dynamic_update_slice(whole, values[n][:, None, None, None], spot)
            return whole

        for first in range(0, self.ring, group):
            backs = list(range(first, first + group))
            values = jnp.stack([pieces[b] for b in backs])
            if first == 0:
                for turn in range(self.width):
                    whole = put(whole, values, backs, turn, self.half)
                    whole = put(whole, self.over_half(values), backs, turn, 1 - self.half)
                    if turn < self.width - 1:
                        values = self.over_lanes(values)
            else:
                for half in (self.half, 1 - self.half):
                    there = values
                    for turn in range(self.width):
                        whole = put(whole, there, backs, turn, half)
                        if turn < self.width - 1:
                            there = self.over_lanes(there)
                    values = self.over_half(values)
        return whole.reshape(m, self.ring * self.width * 2 * rows, cols)

    def scatter_feed(self, grads):
        m, rows, cols = grads.shape
        rows //= self.fsdp * 2
        blocks = grads.reshape(m, self.ring, self.width, 2, rows, cols)
        group = max(1, self.ring // 2)

        def over_width(values):
            total = None
            for turn in list(range(1, self.width)) + [0]:
                term = lax.dynamic_index_in_dim(values, self.lane_at(turn), 2, keepdims=False)
                total = term if total is None else total.astype(F32) + term.astype(F32)
                if turn:
                    total = self.over_lanes(total.astype(BF16))
            return total.astype(F32)

        def over_halves(values, dim):
            keep = lax.dynamic_index_in_dim(values, self.half, dim, keepdims=False)
            send = lax.dynamic_index_in_dim(values, 1 - self.half, dim, keepdims=False)
            return keep.astype(F32) + self.over_half(send.astype(BF16)).astype(F32)

        sums = []
        for first in range(0, self.ring, group):
            values = blocks[:, first : first + group]
            if first == 0:
                sums.append(over_halves(over_width(values), 2))
            else:
                sums.append(over_width(over_halves(values, 3)))
        mine = jnp.concatenate(sums, 1).astype(BF16)
        result = jnp.zeros((m, rows, self.ring, cols), F32)
        for k in range(self.ring):
            piece = lax.dynamic_index_in_dim(mine, (self.at + k) % self.ring, 1, keepdims=False)
            if k:
                piece = self.over_ring(piece, k)
            result = lax.dynamic_update_slice(
                result, piece.astype(F32)[:, :, None], (0, 0, self.ring_at(k), 0)
            )
        return result.reshape(m, rows, self.ring * cols)

    def scatter_gains(self, grads):
        grads = grads + self.over_core(grads)
        count, width = grads.shape
        blocks = grads.reshape(count, self.ring, self.width, 2, width // (self.fsdp * 2))
        keep = lax.dynamic_index_in_dim(blocks, self.half, 3, keepdims=False)
        send = lax.dynamic_index_in_dim(blocks, 1 - self.half, 3, keepdims=False)
        blocks = keep + self.over_half(send)
        total = None
        for turn in list(range(1, self.width)) + [0]:
            term = lax.dynamic_index_in_dim(blocks, self.lane_at(turn), 2, keepdims=False)
            total = term if total is None else total + term
            if turn:
                total = self.over_lanes(total)
        blocks, total = total, None
        for back in list(range(1, self.ring)) + [0]:
            term = lax.dynamic_index_in_dim(blocks, self.ring_at(back), 1, keepdims=False)
            total = term if total is None else total + term
            if back:
                total = self.over_ring(total)
        return total

    def gather_gains(self, gains):
        count, part = gains.shape
        other = self.over_half(gains)
        unit = jnp.where(
            self.half == 0,
            jnp.concatenate([gains, other], 1),
            jnp.concatenate([other, gains], 1),
        )[:, None]
        whole = jnp.zeros((count, self.fsdp, 2 * part), gains.dtype)
        for back in range(self.ring):
            piece = unit
            for turn in range(self.width):
                place = self.ring_at(back) * self.width + self.lane_at(turn)
                whole = lax.dynamic_update_slice(whole, piece, (0, place, 0))
                if turn < self.width - 1:
                    piece = self.over_lanes(piece)
            if back < self.ring - 1:
                unit = self.over_ring(unit)
        return whole.reshape(count, self.fsdp * 2 * part)


def on_device(
    mesh,
    inputs,
    conditioning,
    query_matrix,
    key_matrix,
    value_matrix,
    output_matrix,
    cross_query,
    cross_key,
    cross_value,
    cross_output,
    gate_matrix,
    up_matrix,
    down_matrix,
    first_gain,
    second_gain,
    third_gain,
    cotangent,
):
    links = Links(mesh)
    core, half = links.core, links.half
    rows = inputs.shape[1]
    own_rows = rows // 2
    width = inputs.shape[2]

    gains = links.gather_gains(jnp.stack([first_gain, second_gain, third_gain])).astype(F32)
    first_norm, second_norm, third_norm = gains[0], gains[1], gains[2]
    early = links.gather_pack(jnp.stack([query_matrix, key_matrix, value_matrix]))
    late = links.gather_pack(
        jnp.stack(
            [
                output_matrix.T,
                cross_query,
                cross_output.T,
                jnp.concatenate([cross_key, cross_value], axis=0),
            ]
        )
    )
    cols = early.shape[-1]
    query_full, key_full, value_full = (early[n].reshape(width, cols) for n in range(3))
    output_full, cross_query_full, cross_output_full = (
        late[n].reshape(width, cols) for n in range(3)
    )
    context_rows = cross_key.shape[0]
    context_pack = late[3].reshape(2 * links.fsdp, 2, context_rows, cols)
    cross_key_full = context_pack[:, 0].reshape(-1, cols)
    cross_value_full = context_pack[:, 1].reshape(-1, cols)
    feed = links.gather_feed(jnp.stack([gate_matrix, up_matrix, down_matrix.T]))
    gate_full, up_full, down_full = feed[0], feed[1], feed[2]

    own = lax.dynamic_slice_in_dim(inputs[0], core * own_rows, own_rows, 0)
    sequence = links.share(own)
    tokens = own.astype(F32)
    upstream = lax.dynamic_slice_in_dim(cotangent[0], core * own_rows, own_rows, 0)
    row = lax.iota(jnp.int32, own_rows)
    position = jnp.concatenate(
        [
            row + (half ^ there) * rows + (core ^ other) * own_rows
            for other in (0, 1)
            for there in (0, 1)
        ]
    )
    tables = rotary_tables(position)

    normed_one = norm_low(sequence.astype(F32), first_norm)
    query_rot, key_rot, value_low, self_low = None, None, None, None
    value_low = mm(normed_one, value_full).astype(BF16)
    query_rot, key_rot, self_low, self_logsum = self_forward(
        mm(normed_one, query_full), mm(normed_one, key_full), value_low, tables
    )
    hidden_one = tokens + links.reduce(mm_nt(self_low, output_full))

    normed_two = links.share(norm_low(hidden_one, second_norm))
    cross_query_low = mm(normed_two, cross_query_full).astype(BF16)
    context_count = conditioning.shape[1]
    padded = -(-context_count // 128) * 128
    context = jnp.pad(conditioning[0], ((0, padded - context_count), (0, 0)))
    cross_key_low = mm(context, cross_key_full).astype(BF16)
    cross_value_low = mm(context, cross_value_full).astype(BF16)
    cross_low, cross_logsum = cross_forward(
        cross_query_low, cross_key_low, cross_value_low, context_count
    )
    hidden_two = hidden_one + links.reduce(mm_nt(cross_low, cross_output_full))

    normed_three = links.share_ring(norm_low(hidden_two, third_norm))
    upstream_all = links.share_ring(upstream)
    gate_value = mm(normed_three, gate_full)
    up_value = mm(normed_three, up_full)
    sigmoid_gate = jax.nn.sigmoid(gate_value)
    silu_gate = gate_value * sigmoid_gate
    feed_low = (silu_gate * up_value).astype(BF16)
    feed_grad = mm_nt_down(upstream_all, down_full)
    gate_grad = (
        feed_grad * up_value * sigmoid_gate * (1.0 + gate_value * (1.0 - sigmoid_gate))
    ).astype(BF16)
    up_grad = (feed_grad * silu_gate).astype(BF16)
    third_grad = links.reduce_ring(mm_nt(gate_grad, gate_full) + mm_nt(up_grad, up_full))
    layer_result = hidden_two + links.reduce_ring(mm_nt(feed_low, down_full))
    feed_grads = jnp.stack(
        [
            mm_tn(normed_three, gate_grad).astype(BF16),
            mm_tn(normed_three, up_grad).astype(BF16),
            mm_tn(upstream_all, feed_low).astype(BF16),
        ]
    )
    gate_sum, up_sum, down_sum = links.scatter_feed(feed_grads)

    norm_three_back, third_gain_grad = norm_backward(hidden_two, third_norm, third_grad)
    hidden_two_grad = upstream.astype(F32) + norm_three_back
    branch_two = links.share(hidden_two_grad.astype(BF16))
    cross_out_grad = mm(branch_two, cross_output_full).astype(BF16)
    cross_query_round, cross_key_back, cross_value_back = cross_backward(
        cross_query_low, cross_key_low, cross_value_low, cross_out_grad, cross_logsum, context_count
    )
    second_grad = links.reduce(mm_nt(cross_query_round, cross_query_full))
    cross_key_low_back = cross_key_back.astype(BF16)
    cross_value_low_back = cross_value_back.astype(BF16)
    context_term = (
        mm_nt(cross_key_low_back, cross_key_full) + mm_nt(cross_value_low_back, cross_value_full)
    )[:context_count]
    context_term = context_term + links.over_core(context_term.astype(BF16)).astype(F32)
    context_low = context_term.astype(BF16)
    context_grad = context_low.astype(F32) + links.over_half(context_low).astype(F32)

    norm_two_back, second_gain_grad = norm_backward(hidden_one, second_norm, second_grad)
    hidden_one_grad = hidden_two_grad + norm_two_back
    branch_one = links.share(hidden_one_grad.astype(BF16))
    self_out_grad = mm(branch_one, output_full).astype(BF16)
    context_grads = jnp.stack(
        [
            mm_tn(context, cross_key_low_back).reshape(-1, context_rows, cols),
            mm_tn(context, cross_value_low_back).reshape(-1, context_rows, cols),
        ],
        axis=1,
    )
    late_grads = jnp.stack(
        [
            mm_tn(branch_one, self_low).astype(BF16),
            mm_tn(normed_two, cross_query_round).astype(BF16),
            mm_tn(branch_two, cross_low).astype(BF16),
            context_grads.reshape(width, cols).astype(BF16),
        ]
    )
    unit_rows = width // links.fsdp
    late_sums = links.scatter_pack(late_grads.reshape(4, links.fsdp, unit_rows, cols))
    query_round, key_round, value_round = self_backward(
        query_rot, key_rot, value_low, self_out_grad, self_logsum, tables
    )
    first_grad = links.reduce(
        mm_nt(query_round, query_full)
        + mm_nt(key_round, key_full)
        + mm_nt(value_round, value_full)
    )
    early_grads = jnp.stack(
        [
            mm_tn(normed_one, query_round).astype(BF16),
            mm_tn(normed_one, key_round).astype(BF16),
            mm_tn(normed_one, value_round).astype(BF16),
        ]
    )
    early_sums = links.scatter_pack(early_grads.reshape(3, links.fsdp, unit_rows, cols))
    norm_one_back, first_gain_grad = norm_backward(tokens, first_norm, first_grad)
    inputs_grad = hidden_one_grad + norm_one_back
    gain_sums = links.scatter_gains(
        jnp.stack([first_gain_grad, second_gain_grad, third_gain_grad])
    )
    return (
        links.both_cores(layer_result)[None],
        links.both_cores(inputs_grad)[None],
        context_grad[None],
        early_sums[0],
        early_sums[1],
        early_sums[2],
        late_sums[0].T,
        late_sums[1],
        late_sums[3][:context_rows],
        late_sums[3][context_rows:],
        late_sums[2].T,
        gate_sum,
        up_sum,
        down_sum.T,
        gain_sums[0],
        gain_sums[1],
        gain_sums[2],
    )


def mm_nt_down(upstream, down_rows):
    return mm(upstream, down_rows).astype(BF16).astype(F32)


def solution(mesh):
    row = P(("fsdp", "ctx"), "tp")
    col = P("tp", ("fsdp", "ctx"))
    gain = P(("fsdp", "ctx"))
    token = P("fsdp", "ctx", None)
    context = P("fsdp", None, None)
    weights = (row, row, row, col, row, row, row, col, row, row, col, gain, gain, gain)
    return jax.shard_map(
        functools.partial(on_device, mesh),
        mesh=mesh,
        in_specs=(token, context) + weights + (token,),
        out_specs=(token, token, context) + weights,
        check_vma=False,
    )
```

```python
import functools
import math

import jax
import jax.numpy as jnp
from jax import lax
from jax.experimental import pallas as pl
from jax.experimental.pallas import tpu as pltpu
from jax.sharding import PartitionSpec as P

HDIM = 64
EPSILON = 1e-05
F32 = jnp.float32
BF16 = jnp.bfloat16
SCALE = HDIM ** (-0.5)
PAIR = 2 * HDIM
VMEM_LIMIT = 48 * 1024 * 1024


def mm(left, right):
    return lax.dot_general(left, right, (((1,), (0,)), ((), ())), preferred_element_type=F32)


def mm_tn(left, right):
    return lax.dot_general(left, right, (((0,), (0,)), ((), ())), preferred_element_type=F32)


def mm_nt(left, right):
    return lax.dot_general(left, right, (((1,), (1,)), ((), ())), preferred_element_type=F32)


def norm_stats(values):
    center = values - jnp.mean(values, axis=-1, keepdims=True)
    rate = lax.rsqrt(jnp.mean(center * center, axis=-1, keepdims=True) + EPSILON)
    return center * rate, rate


def params():
    return pltpu.CompilerParams(vmem_limit_bytes=VMEM_LIMIT)


def norm_forward_kernel(base_ref, near_ref, far_ref, gain_ref, x_ref, n_ref):
    values = base_ref[...].astype(F32) + near_ref[...] + far_ref[...].astype(F32)
    x_ref[...] = values
    n_ref[...] = (norm_stats(values)[0] * gain_ref[...]).astype(BF16)


def norm_forward(base, near, far, gain):
    rows, width = base.shape
    return pl.pallas_call(
        norm_forward_kernel,
        out_shape=(
            jax.ShapeDtypeStruct((rows, width), F32),
            jax.ShapeDtypeStruct((rows, width), BF16),
        ),
        compiler_params=params(),
    )(base, near, far, gain)


def norm_backward_kernel(
    x_ref, gain_ref, skip_ref, *refs
):
    *terms, dx_ref, low_ref, dg_ref = refs
    rows = x_ref.shape[0]
    upstream = terms[0][:rows, :].astype(F32)
    for term in terms[1:]:
        upstream = upstream + term[:rows, :].astype(F32)
    unit, rate = norm_stats(x_ref[...].astype(F32))
    scaled = upstream * gain_ref[...]
    back = rate * (
        scaled
        - jnp.mean(scaled, axis=-1, keepdims=True)
        - unit * jnp.mean(scaled * unit, axis=-1, keepdims=True)
    )
    total = skip_ref[...].astype(F32) + back
    dx_ref[...] = total
    low_ref[...] = total.astype(BF16)
    dg_ref[...] = jnp.sum(upstream * unit, axis=0, keepdims=True)


def norm_backward(values, gain, skip, *terms):
    rows, width = values.shape
    return pl.pallas_call(
        norm_backward_kernel,
        out_shape=(
            jax.ShapeDtypeStruct((rows, width), F32),
            jax.ShapeDtypeStruct((rows, width), BF16),
            jax.ShapeDtypeStruct((1, width), F32),
        ),
        compiler_params=params(),
    )(values, gain, skip, *terms)


def turned(values, cosine, upper, lower):
    width = values.shape[1]
    return (
        values * cosine
        + pltpu.roll(values, width - HDIM // 4, 1) * upper
        + pltpu.roll(values, HDIM // 4, 1) * lower
    )


def chunk_of(rows):
    return 128 if rows % 128 == 0 else rows


def low_half(shape):
    return lax.broadcasted_iota(jnp.int32, shape, len(shape) - 1) < HDIM


def of_head(values, head):
    first = low_half(values.shape)
    keep = first if head == 0 else jnp.logical_not(first)
    return jnp.where(keep, values, jnp.zeros((), values.dtype))


def forward_heads(q_ref, k_ref, v_ref, o_ref, lse_ref, valid):
    rows = q_ref.shape[0]
    step = chunk_of(rows)
    key, value = k_ref[...], v_ref[...]
    first_half = low_half(value.shape)
    ones = jnp.ones((), BF16)
    extended = jnp.where(first_half, value, ones), jnp.where(first_half, ones, value)
    for first in range(0, rows, step):
        part = slice(first, first + step)
        query = q_ref[part, :]
        results = []
        for head in range(2):
            scores = mm_nt(of_head(query, head), key)
            if valid < key.shape[0]:
                column = lax.broadcasted_iota(jnp.int32, scores.shape, 1)
                scores = jnp.where(column < valid, scores, -1e30)
            peak = jnp.max(scores, axis=-1, keepdims=True)
            mixed = mm(jnp.exp(scores - peak).astype(BF16), extended[head])
            total = pltpu.roll(mixed, HDIM, 1)
            results.append((mixed * (1.0 / total), peak + jnp.log(total)))
        lanes = low_half((step, PAIR))
        o_ref[part, :] = jnp.where(lanes, results[0][0], results[1][0]).astype(BF16)
        lse_ref[part, :] = jnp.where(lanes, results[0][1], results[1][1])


def thirds(ref):
    return ref.at[:, :PAIR], ref.at[:, PAIR : 2 * PAIR], ref.at[:, 2 * PAIR :]


def self_forward_kernel(qkv_ref, cos_ref, up_ref, low_ref, turned_ref, o_ref, lse_ref):
    tables = cos_ref[...], up_ref[...], low_ref[...]
    q_ref, k_ref, v_ref = thirds(turned_ref)
    q_ref[...] = turned(qkv_ref[:, :PAIR], *tables).astype(BF16) * jnp.asarray(SCALE, BF16)
    k_ref[...] = turned(qkv_ref[:, PAIR : 2 * PAIR], *tables).astype(BF16)
    v_ref[...] = qkv_ref[:, 2 * PAIR :].astype(BF16)
    forward_heads(q_ref, k_ref, v_ref, o_ref, lse_ref, k_ref.shape[0])


def cross_forward_kernel(valid, q_ref, k_ref, v_ref, o_ref, lse_ref):
    forward_heads(q_ref, k_ref, v_ref, o_ref, lse_ref, valid)


def backward_heads(q_ref, k_ref, v_ref, o_ref, do_ref, lse_ref, dq_ref, dk_ref, dv_ref, valid):
    rows = q_ref.shape[0]
    step = chunk_of(rows)
    key, value = k_ref[...], v_ref[...]
    for first in range(0, rows, step):
        part = slice(first, first + step)
        query, grad = q_ref[part, :], do_ref[part, :]
        lse = lse_ref[part, :].T
        delta = (grad.astype(F32) * o_ref[part, :].astype(F32)).T
        query_terms = []
        for head in range(2):
            query_head, grad_head = of_head(query, head), of_head(grad, head)
            lanes = slice(head * HDIM, (head + 1) * HDIM)
            mean_grad = jnp.sum(delta[lanes, :], axis=0, keepdims=True)
            probability = jnp.exp(mm_nt(key, query_head) - lse[head * HDIM : head * HDIM + 1, :])
            if valid < key.shape[0]:
                line = lax.broadcasted_iota(jnp.int32, probability.shape, 0)
                probability = jnp.where(line < valid, probability, 0.0)
            score_grad = (probability * (mm_nt(value, grad_head) - mean_grad)).astype(BF16)
            query_terms.append(mm_tn(score_grad, key))
            key_term = mm(score_grad, query_head)
            value_term = mm(probability.astype(BF16), grad_head)
            if first == 0 and head == 0:
                dk_ref[...] = key_term
                dv_ref[...] = value_term
            else:
                dk_ref[...] += key_term
                dv_ref[...] += value_term
        dq_ref[part, :] = jnp.where(low_half((step, PAIR)), *query_terms) * SCALE


def self_backward_kernel(
    turned_ref, o_ref, do_ref, lse_ref, cos_ref, up_ref, low_ref, out_ref, dq_acc, dk_acc, dv_acc
):
    q_ref, k_ref, v_ref = thirds(turned_ref)
    backward_heads(
        q_ref, k_ref, v_ref, o_ref, do_ref, lse_ref, dq_acc, dk_acc, dv_acc, k_ref.shape[0]
    )
    tables = cos_ref[...], -up_ref[...], -low_ref[...]
    dq_ref, dk_ref, dv_ref = thirds(out_ref)
    dq_ref[...] = turned(dq_acc[...], *tables).astype(BF16)
    dk_ref[...] = turned(dk_acc[...], *tables).astype(BF16)
    dv_ref[...] = dv_acc[...].astype(BF16)


def cross_backward_kernel(
    valid, q_ref, k_ref, v_ref, o_ref, do_ref, lse_ref, dq_ref, dk_ref, dv_ref, dq_acc, dk_acc, dv_acc
):
    some = -(-valid // 16) * 16
    backward_heads(
        q_ref, k_ref.at[:some, :], v_ref.at[:some, :], o_ref, do_ref, lse_ref,
        dq_acc, dk_acc.at[:some, :], dv_acc.at[:some, :], valid,
    )
    dq_ref[...] = dq_acc[...].astype(BF16)
    for ref, acc in ((dk_ref, dk_acc), (dv_ref, dv_acc)):
        ref[:some, :] = acc[:some, :].astype(BF16)
        if some < ref.shape[0]:
            ref[some:, :] = jnp.zeros((ref.shape[0] - some, PAIR), BF16)


def attention_call(kernel, pairs, ins, outs, scratch, flops):
    return pl.pallas_call(
        kernel,
        grid=(pairs,),
        in_specs=[
            pl.BlockSpec((rows, width), functools.partial(lambda place, pair: (0, place(pair)), place))
            for rows, width, place in ins
        ],
        out_specs=[pl.BlockSpec((rows, width), lambda pair: (0, pair)) for rows, width, _ in outs],
        out_shape=[
            jax.ShapeDtypeStruct((rows, width * pairs), kind) for rows, width, kind in outs
        ],
        scratch_shapes=[pltpu.VMEM((rows, PAIR), F32) for rows in scratch],
        compiler_params=params(),
        cost_estimate=pl.CostEstimate(
            flops=flops,
            bytes_accessed=4 * pairs * sum(rows * width for rows, width, _ in ins),
            transcendentals=flops // 256,
        ),
    )


def here(pair):
    return pair


def always(pair):
    return 0


def self_forward(qkv, tables):
    rows, pairs = qkv.shape[0], qkv.shape[1] // (3 * PAIR)
    return attention_call(
        self_forward_kernel,
        pairs,
        [(rows, 3 * PAIR, here)] + [(rows, PAIR, always)] * 3,
        [(rows, 3 * PAIR, BF16), (rows, PAIR, BF16), (rows, PAIR, F32)],
        (),
        4 * rows * rows * pairs * PAIR,
    )(qkv, *tables)


def self_backward(qkv, out, grad, lse, tables):
    rows, pairs = qkv.shape[0], qkv.shape[1] // (3 * PAIR)
    return attention_call(
        self_backward_kernel,
        pairs,
        [(rows, 3 * PAIR, here)] + [(rows, PAIR, here)] * 3 + [(rows, PAIR, always)] * 3,
        [(rows, 3 * PAIR, BF16)],
        (rows,) * 3,
        10 * rows * rows * pairs * PAIR,
    )(qkv, out, grad, lse, *tables)[0]


def cross_forward(query, context, valid):
    rows, pairs, keys = query.shape[0], query.shape[1] // PAIR, context.shape[0]
    return attention_call(
        functools.partial(cross_forward_kernel, valid),
        pairs,
        [(rows, PAIR, here), (keys, PAIR, here), (keys, PAIR, lambda pair: pairs + pair)],
        [(rows, PAIR, BF16), (rows, PAIR, F32)],
        (),
        4 * rows * keys * pairs * PAIR,
    )(query, context, context)


def cross_backward(query, context, out, grad, lse, valid):
    rows, pairs, keys = query.shape[0], query.shape[1] // PAIR, context.shape[0]
    return attention_call(
        functools.partial(cross_backward_kernel, valid),
        pairs,
        [(rows, PAIR, here), (keys, PAIR, here), (keys, PAIR, lambda pair: pairs + pair)]
        + [(rows, PAIR, here)] * 3,
        [(rows, PAIR, BF16), (keys, PAIR, BF16), (keys, PAIR, BF16)],
        (rows, keys, keys),
        10 * rows * keys * pairs * PAIR,
    )(query, context, context, out, grad, lse)


def rotary_tables(position):
    quarter = HDIM // 4
    lane = lax.broadcasted_iota(jnp.int32, (position.shape[0], PAIR), 1) & (HDIM - 1)
    turn = (lane & (quarter - 1)).astype(F32)
    frequency = jnp.exp(-(2.0 * turn / (2 * quarter)) * math.log(10000.0))
    angles = position.astype(F32)[:, None] * frequency
    cosine, sine = jnp.cos(angles), jnp.sin(angles)
    return (
        jnp.where(lane < 2 * quarter, cosine, 1.0),
        jnp.where(lane < quarter, -sine, 0.0),
        jnp.where((lane >= quarter) & (lane < 2 * quarter), sine, 0.0),
    )


def place_kernel(plan, n_pieces, place_ref, *refs):
    pieces, outs = refs[:n_pieces], refs[n_pieces:]
    for piece, spot, src_row, rows, src_col, cols, out, dst_col in plan:
        row = pl.multiple_of(place_ref[spot] * rows, rows)
        outs[out][pl.ds(row, rows), dst_col : dst_col + cols] = pieces[piece][
            src_row : src_row + rows, src_col : src_col + cols
        ]


def place_pieces(pieces, plan, place, outs):
    if any(entry[2] % 16 or entry[3] % 16 for entry in plan):
        whole = [jnp.zeros(out, BF16) for out in outs]
        for piece, spot, src_row, rows, src_col, cols, out, dst_col in plan:
            part = pieces[piece][src_row : src_row + rows, src_col : src_col + cols]
            whole[out] = lax.dynamic_update_slice(whole[out], part, (place[spot] * rows, dst_col))
        return whole
    vmem = pl.BlockSpec(memory_space=pltpu.VMEM)
    return pl.pallas_call(
        functools.partial(place_kernel, tuple(plan), len(pieces)),
        in_specs=[pl.BlockSpec(memory_space=pltpu.SMEM)] + [vmem] * len(pieces),
        out_specs=[vmem] * len(outs),
        out_shape=[jax.ShapeDtypeStruct(out, BF16) for out in outs],
        compiler_params=params(),
        cost_estimate=pl.CostEstimate(
            flops=0, transcendentals=0, bytes_accessed=4 * sum(math.prod(out) for out in outs)
        ),
    )(place, *pieces)


def early_kernel(shard, place_ref, *refs):
    *pieces, a_ref, b_ref, c_ref, d_ref, qkv_ref, output_ref, gain_ref, normed_ref = refs
    gains = pieces[0][2 * shard :, :].astype(F32)
    for piece in pieces[1:]:
        gains = gains + piece[2 * shard :, :].astype(F32)
    gain_ref[...] = gains
    first = 0
    for ref in (a_ref, b_ref, c_ref, d_ref):
        unit, _ = norm_stats(ref[...].astype(F32))
        normed_ref[first : first + ref.shape[0], :] = (unit * gains[:1]).astype(BF16)
        first += ref.shape[0]
    cols = qkv_ref.shape[1]
    for n, piece in enumerate(pieces):
        for there in (0, 1):
            row = pl.ds(pl.multiple_of(place_ref[2 * n + there] * shard, shard), shard)
            lines = slice(there * shard, (there + 1) * shard)
            qkv_ref[row, :] = piece[lines, :cols]
            output_ref[row, :] = piece[lines, cols:]


def early_full(pieces, place, tokens, shard):
    width, cols = tokens[0].shape[1], pieces[0].shape[1] // 4
    rows = sum(part.shape[0] for part in tokens)
    vmem = pl.BlockSpec(memory_space=pltpu.VMEM)
    return pl.pallas_call(
        functools.partial(early_kernel, shard),
        in_specs=[pl.BlockSpec(memory_space=pltpu.SMEM)] + [vmem] * (len(pieces) + 4),
        out_specs=[vmem] * 4,
        out_shape=[
            jax.ShapeDtypeStruct((width, 3 * cols), BF16),
            jax.ShapeDtypeStruct((width, cols), BF16),
            jax.ShapeDtypeStruct((pieces[0].shape[0] - 2 * shard, width), F32),
            jax.ShapeDtypeStruct((rows, width), BF16),
        ],
        compiler_params=params(),
    )(place, *pieces, *tokens)


def spread_kernel(place_ref, *refs):
    pieces, (down_out, gate_out, up_out) = refs[:RING], refs[RING:]
    cols = pieces[0].shape[1] // 3
    for n, piece in enumerate(pieces):
        spot = pl.ds(pl.multiple_of(place_ref[n] * cols, cols), cols)
        for m, out in enumerate((down_out, gate_out, up_out)):
            out[:, spot] = piece[:, m * cols : (m + 1) * cols].astype(F32)


def spread(pieces, place):
    rows, cols = pieces[0].shape
    vmem = pl.BlockSpec(memory_space=pltpu.VMEM)
    down, gate, up = pl.pallas_call(
        spread_kernel,
        in_specs=[pl.BlockSpec(memory_space=pltpu.SMEM)] + [vmem] * RING,
        out_specs=[vmem] * 3,
        out_shape=[jax.ShapeDtypeStruct((rows, cols // 3 * RING), F32)] * 3,
        compiler_params=params(),
    )(place, *pieces)
    return gate, up, down


def pack_early_kernel(half_ref, q_ref, k_ref, v_ref, o_ref, send_ref, keep_ref):
    cols = o_ref.shape[1] // 2
    for out, index in ((send_ref, 1 - half_ref[0]), (keep_ref, half_ref[0])):
        first = pl.multiple_of(index * cols, PAIR)
        for pair in range(cols // PAIR):
            for n, ref in enumerate((q_ref, k_ref, v_ref)):
                spot = (3 * pair + n) * PAIR
                out[:, spot : spot + PAIR] = ref[:, pl.ds(first + pair * PAIR, PAIR)]
        out[:, 3 * cols :] = o_ref[:, pl.ds(first, cols)]


def pack_early(query, key, value, output, half, cols):
    rows = query.shape[0]
    vmem = pl.BlockSpec(memory_space=pltpu.VMEM)
    return pl.pallas_call(
        pack_early_kernel,
        in_specs=[pl.BlockSpec(memory_space=pltpu.SMEM)] + [vmem] * 4,
        out_specs=[vmem] * 2,
        out_shape=[jax.ShapeDtypeStruct((rows, 4 * cols), BF16)] * 2,
        compiler_params=params(),
    )(half.reshape(1), query, key, value, output)


RING = 4


class Links:
    def __init__(self, mesh):
        self.fsdp = mesh.shape["fsdp"]
        self.width = self.fsdp // RING
        index = lax.axis_index("fsdp")
        self.at = lax.div(index, self.width)
        self.lane = index - self.at * self.width
        self.half = lax.axis_index("ctx")
        self.core = lax.axis_index("tp")
        self.step = jnp.zeros((8, 128), F32)

    def sync(self, *values):
        flat, tree = jax.tree.flatten(values)
        self.step, *flat = lax.optimization_barrier([self.step, *flat])
        return jax.tree.unflatten(tree, flat)

    def begun(self, value):
        return lax.optimization_barrier([value, self.step])[0]

    def ring(self, value, hops):
        z, r = RING, self.width
        pairs = [(a * r + b, (a + hops) % z * r + b) for a in range(z) for b in range(r)]
        return lax.ppermute(self.begun(value), "fsdp", pairs)

    def lanes(self, value):
        z, r = RING, self.width
        pairs = [(a * r + b, a * r + (b + 1) % r) for a in range(z) for b in range(r)]
        return lax.ppermute(self.begun(value), "fsdp", pairs)

    def over_half(self, value):
        return lax.ppermute(self.begun(value), "ctx", [(0, 1), (1, 0)])

    def over_core(self, value):
        return lax.ppermute(self.begun(value), "tp", [(0, 1), (1, 0)])

    def ring_at(self, back):
        return (self.at + (RING - back)) & (RING - 1)

    def lane_at(self, turn):
        return lax.rem(self.lane + (self.width - turn), self.width) if turn else self.lane

    def place(self, back, turn):
        return self.ring_at(back) * self.width + self.lane_at(turn)

    def block_places(self):
        n = lax.iota(jnp.int32, RING * self.width * 2)
        back = lax.div(n, 2 * self.width)
        turn = lax.rem(lax.div(n, 2), self.width)
        ring = (self.at + RING - back) & (RING - 1)
        lane = lax.rem(self.lane + self.width - turn, self.width)
        return (ring * self.width + lane) * 2 + (self.half ^ (n & 1))

    def all_lanes(self, value):
        values = [value]
        while len(values) < self.width:
            values.append(self.lanes(values[-1]))
        return values

    def sum_lanes(self, terms):
        total, *rest = terms
        for term in rest:
            total = (self.lanes(total).astype(F32) + term.astype(F32)).astype(BF16)
        return self.lanes(total)

    def both_cores(self, own):
        other = self.over_core(own)
        first = jnp.where(self.core == 0, own, other)
        second = jnp.where(self.core == 0, other, own)
        return jnp.concatenate([first, second], axis=0)

    def swap_halves(self, total):
        keep = lax.dynamic_index_in_dim(total, self.half, 0, keepdims=False)
        send = lax.dynamic_index_in_dim(total, 1 - self.half, 0, keepdims=False)
        return keep, self.over_half(send.astype(BF16)).astype(F32)

    def side_by_side(self, keep, recv):
        return jnp.concatenate(
            [jnp.where(self.half == 0, keep, recv), jnp.where(self.half == 0, recv, keep)], axis=-1
        )


def slot(values, count, index):
    size = values.shape[1] // count
    return lax.dynamic_slice_in_dim(values, index * size, size, 1)


def in_order(values, index):
    count = len(values)
    ahead = jnp.concatenate(values[::-1], axis=1)
    size = ahead.shape[1]
    first = lax.rem(2 * count - 1 - index, count)
    twice = jnp.concatenate([ahead, ahead], axis=1)
    return lax.dynamic_slice_in_dim(twice, first * (size // count), size, 1)


def on_device(
    mesh,
    inputs,
    conditioning,
    query_matrix,
    key_matrix,
    value_matrix,
    output_matrix,
    cross_query,
    cross_key,
    cross_value,
    cross_output,
    gate_matrix,
    up_matrix,
    down_matrix,
    first_gain,
    second_gain,
    third_gain,
    cotangent,
):
    links = Links(mesh)
    ring, lanes, all_lanes = links.ring, links.lanes, links.all_lanes
    over_half, over_core = links.over_half, links.over_core
    sync = links.sync
    core, half, lane_count = links.core, links.half, links.width
    rows = inputs.shape[1]
    own_rows = rows // 2
    width = inputs.shape[2]
    shard = query_matrix.shape[0]
    cols = query_matrix.shape[1] // 2
    pairs = cols // PAIR
    context_shard = cross_key.shape[0]
    context_width = conditioning.shape[2]
    context_count = conditioning.shape[1]
    hidden = gate_matrix.shape[1] // RING
    blocks = links.fsdp * 2
    places = links.block_places()

    def half_cols(values, index):
        return lax.dynamic_slice_in_dim(values, index * cols, cols, 1)

    def early_part(index):
        parts = [half_cols(w, index) for w in (query_matrix, key_matrix, value_matrix)]
        return jnp.concatenate(
            [p[:, n * PAIR : (n + 1) * PAIR] for n in range(pairs) for p in parts]
            + [half_cols(output_matrix.T, index)],
            axis=1,
        )

    def late_part(index):
        return jnp.concatenate(
            [
                half_cols(w, index)
                for w in (cross_query, cross_output.T, cross_key, cross_value)
            ],
            axis=0,
        )

    def feed_part(index):
        return jnp.concatenate(
            [
                lax.dynamic_slice_in_dim(w, index * hidden, hidden, 1)
                for w in (gate_matrix, up_matrix, down_matrix.T)
            ],
            axis=1,
        )

    def halves_of(left, weights):
        pair = 2 * own_rows
        return mm_nt(left[:pair], weights), mm_nt(left[pair:], weights).astype(BF16)

    def with_core(mine, recv):
        total = mine + recv.astype(F32)
        return total[:own_rows], total[own_rows:].astype(BF16)

    def spread_cores(own, over):
        pair = jnp.concatenate([own, over], axis=0)
        return jnp.concatenate([pair, over_core(pair)], axis=0)

    own = lax.dynamic_slice_in_dim(inputs[0], core * own_rows, own_rows, 0)
    other = lax.dynamic_slice_in_dim(inputs[0], (1 - core) * own_rows, own_rows, 0)
    upstream = lax.dynamic_slice_in_dim(cotangent[0], core * own_rows, own_rows, 0)
    row = lax.iota(jnp.int32, own_rows)
    position = jnp.concatenate(
        [
            row + (half ^ there) * rows + (core ^ beside) * own_rows
            for beside in (0, 1)
            for there in (0, 1)
        ]
    )
    mark = lax.broadcasted_iota(jnp.int32, (16, width), 1)
    place = (lax.axis_index("fsdp") * 2 + half) * shard
    gains = jnp.pad(jnp.stack([first_gain, second_gain, third_gain]), ((0, 13), (0, 0)))
    gains = jnp.where(
        (mark >= place) & (mark < place + shard), jnp.tile(gains, (1, blocks)), jnp.zeros((), BF16)
    )
    early_send, early_keep = pack_early(
        query_matrix, key_matrix, value_matrix, output_matrix.T, half, cols
    )

    early_recv, gains_over = over_half(early_send), over_half(gains)
    early_keep, early_recv, gains_over = sync(early_keep, early_recv, gains_over)

    early0 = jnp.concatenate([early_keep, early_recv, gains + gains_over], axis=0)
    early1, lanes0, own_over = ring(early0, 1), all_lanes(early0), over_half(own)
    early1, lanes0, own_over, late_send, late_keep = sync(
        early1, lanes0, own_over, late_part(1 - half), late_part(half)
    )

    early3, lanes1, late_recv = ring(lanes0[0], -1), all_lanes(early1), over_half(late_send)
    other_over = over_core(own_over)
    early3, lanes1, late_recv, other_over, tables, feed0, feed_send = sync(
        early3,
        lanes1,
        late_recv,
        other_over,
        rotary_tables(position),
        feed_part(links.at),
        feed_part(links.ring_at(RING - 1)),
    )

    early2, lanes3, feed0_over = ring(lanes1[0], 1), all_lanes(early3), over_half(feed0)
    late0 = jnp.concatenate([late_keep, late_recv], axis=0)
    early2, lanes3, feed0_over, late0 = sync(early2, lanes3, feed0_over, late0)

    feed1, lanes2 = ring(feed_send, 1), all_lanes(early2)
    context = jnp.pad(conditioning[0], ((0, -context_count % 128), (0, 0)))
    feed1, lanes2, context, feed_send = sync(
        feed1, lanes2, context, feed_part(links.ring_at(1))
    )

    late1, late_lanes0, feed1_over = ring(late0, 1), all_lanes(late0), over_half(feed1)
    qkv_full, output_full, gains, normed_one = early_full(
        lanes0 + lanes1 + lanes2 + lanes3, places, (own, own_over, other, other_over), shard
    )
    first_norm_gain, second_norm_gain, third_norm_gain = gains[0:1], gains[1:2], gains[2:3]
    qkv = mm(normed_one, qkv_full)
    qkv, late1, late_lanes0, feed1_over = sync(qkv, late1, late_lanes0, feed1_over)

    late3, late2 = ring(late0, -1), ring(late1, 1)
    late_lanes1, feed0_lanes = all_lanes(late1), all_lanes(feed0)
    qkv_low, self_low, self_logsum = self_forward(qkv, tables)
    partial, send = halves_of(self_low, output_full)
    partial, send, late3, late2, late_lanes1, feed0_lanes = sync(
        partial, send, late3, late2, late_lanes1, feed0_lanes
    )

    terms = with_core(partial, over_core(send))
    far_term, feed3, late_lanes3 = over_half(terms[1]), ring(feed_send, -1), all_lanes(late3)
    far_term, feed3, late_lanes3, feed_send = sync(
        far_term, feed3, late_lanes3, feed_part(links.ring_at(2))
    )

    hidden_one, normed = norm_forward(own, terms[0], far_term, second_norm_gain)
    normed_over, cotangent1, late_lanes2 = over_half(normed), ring(upstream, 1), all_lanes(late2)
    normed_over, cotangent1, late_lanes2 = sync(normed_over, cotangent1, late_lanes2)

    feed2, feed0_over_lanes, feed3_over = (
        ring(feed_send, 2),
        all_lanes(feed0_over),
        over_half(feed3),
    )
    plan = []
    for n in range(blocks):
        first = (n % 2) * 2 * (shard + context_shard)
        for out in range(2):
            plan.append((n // 2, n, first + out * shard, shard, 0, cols, out, 0))
        for out in range(2):
            start = first + 2 * shard + out * context_shard
            plan.append((n // 2, n, start, context_shard, 0, cols, 2, out * cols))
    cross_query_full, cross_output_full, context_full = place_pieces(
        late_lanes0 + late_lanes1 + late_lanes2 + late_lanes3,
        plan,
        places,
        [(width, cols)] * 2 + [(context_width, 2 * cols)],
    )
    context_low = mm(context, context_full).astype(BF16)
    normed_two = spread_cores(normed, normed_over)
    cross_query_low = mm(normed_two, cross_query_full).astype(BF16) * jnp.asarray(SCALE, BF16)
    cross_low, cross_logsum = cross_forward(cross_query_low, context_low, context_count)
    partial, send = halves_of(cross_low, cross_output_full)
    partial, send, feed2, feed0_over_lanes, feed3_over = sync(
        partial, send, feed2, feed0_over_lanes, feed3_over
    )

    terms = with_core(partial, over_core(send))
    far_term, cotangent3, feed1_lanes = over_half(terms[1]), ring(upstream, -1), all_lanes(feed1)
    far_term, cotangent3, feed1_lanes = sync(far_term, cotangent3, feed1_lanes)

    hidden_two, normed0 = norm_forward(hidden_one, terms[0], far_term, third_norm_gain)
    normed1, feed3_lanes, feed2_over = ring(normed0, 1), all_lanes(feed3), over_half(feed2)
    normed1, feed3_lanes, feed2_over = sync(normed1, feed3_lanes, feed2_over)

    normed2, feed2_lanes = ring(normed1, 1), all_lanes(feed2)
    feed3_lanes_over = [feed3_over] + [over_half(value) for value in feed3_lanes[1:]]
    normed2, feed2_lanes, feed3_lanes_over = sync(normed2, feed2_lanes, feed3_lanes_over)

    normed3, feed1_over_lanes = ring(normed2, 1), all_lanes(feed1_over)
    feed2_lanes_over = [feed2_over] + [over_half(value) for value in feed2_lanes[1:]]
    normed3, feed1_over_lanes, feed2_lanes_over = sync(normed3, feed1_over_lanes, feed2_lanes_over)

    normed_mine = jnp.concatenate([normed0, normed1, normed2, normed3], axis=0)
    normed_three = jnp.concatenate([normed_mine, over_core(normed_mine)], axis=0)
    cotangent2 = ring(cotangent1, 1)
    plan = []
    pieces = []
    for back, groups in (
        (0, (feed0_lanes, feed0_over_lanes)),
        (1, (feed1_lanes, feed1_over_lanes)),
        (2, (feed2_lanes, feed2_lanes_over)),
        (3, (feed3_lanes, feed3_lanes_over)),
    ):
        for there, group in enumerate(groups):
            for turn, piece in enumerate(group):
                spot = (back * lane_count + turn) * 2 + there
                for out in range(3):
                    plan.append((len(pieces), spot, 0, shard, out * hidden, hidden, out, 0))
                pieces.append(piece)
    gate_full, up_full, down_full = place_pieces(pieces, plan, places, [(width, hidden)] * 3)
    gate_value = mm(normed_three, gate_full)
    up_value = mm(normed_three, up_full)
    sigmoid_gate = jax.nn.sigmoid(gate_value)
    silu_gate = gate_value * sigmoid_gate
    feed_low = (silu_gate * up_value).astype(BF16)
    gate_value, up_value, feed_low, cotangent2 = sync(gate_value, up_value, feed_low, cotangent2)

    def ring_halves(left, weights):
        count = RING * own_rows
        return mm_nt(left[:count], weights), mm_nt(left[count:], weights).astype(BF16)

    def block_of(mine, recv, back):
        part = slice(back * own_rows, (back + 1) * own_rows)
        return mine[part] + recv[part].astype(F32)

    def lanes_block(grads, turn):
        place = links.lane_at(turn)
        return jnp.concatenate(
            [
                lax.dynamic_slice_in_dim(grads, (z * lane_count + place) * 2 * shard, 2 * shard, 0)
                for z in (0, 1)
            ],
            axis=0,
        )

    def halves_block(grads, index):
        return jnp.concatenate(
            [
                lax.dynamic_slice_in_dim(
                    grads, ((z * lane_count + n) * 2 + index) * shard, shard, 0
                )
                for z in (2, 3)
                for n in range(lane_count)
            ],
            axis=0,
        )

    def lanes_terms(grads):
        return [lanes_block(grads, turn) for turn in range(1, lane_count)]

    def lanes_second(grads, recv):
        total = (lanes_block(grads, 0).astype(F32) + recv.astype(F32)).reshape(2, 2, shard, hidden)
        keep = lax.dynamic_index_in_dim(total, half, 1, keepdims=False)
        send = lax.dynamic_index_in_dim(total, 1 - half, 1, keepdims=False)
        return keep, send.astype(BF16)

    def halves_second(grads, recv):
        total = (halves_block(grads, half).astype(F32) + recv.astype(F32)).reshape(
            2, lane_count, shard, hidden
        )
        keep, *send = [
            lax.dynamic_index_in_dim(total, links.lane_at(turn), 1, keepdims=False)
            for turn in range(lane_count)
        ]
        return keep, [term.astype(BF16) for term in send]

    def joined(*terms):
        keep, recv, keep_late, recv_late = terms
        return jnp.concatenate(
            [
                (keep + recv.astype(F32)).astype(BF16),
                (keep_late + recv_late.astype(F32)).astype(BF16),
            ],
            axis=0,
        )

    mine = jnp.concatenate([upstream, cotangent1, cotangent2, cotangent3], axis=0)
    upstream_all = jnp.concatenate([mine, over_core(mine)], axis=0)
    out_mine, out_send = ring_halves(feed_low, down_full)
    upstream_all, out_mine, out_send = sync(upstream_all, out_mine, out_send)

    out_recv = over_core(out_send)
    down_grad = mm_tn(upstream_all, feed_low).astype(BF16)
    down_grad, out_recv, down_lanes, down_halves = sync(
        down_grad, out_recv, lanes_terms(down_grad), halves_block(down_grad, 1 - half)
    )

    out_two = ring(block_of(out_mine, out_recv, 2).astype(BF16), -1)
    down_lanes, down_halves = links.sum_lanes(down_lanes), over_half(down_halves)
    feed_grad = mm(upstream_all, down_full).astype(BF16).astype(F32)
    gate_low = (
        feed_grad * up_value * sigmoid_gate * (1.0 + gate_value * (1.0 - sigmoid_gate))
    ).astype(BF16)
    up_low = (feed_grad * silu_gate).astype(BF16)
    gate_low, up_low, out_two, down_lanes, down_halves = sync(
        gate_low, up_low, out_two, down_lanes, down_halves
    )

    count = RING * own_rows
    send = (mm_nt(gate_low[count:], gate_full) + mm_nt(up_low[count:], up_full)).astype(BF16)
    (send,) = sync(send)
    recv = over_core(send)
    mine = mm_nt(gate_low[:count], gate_full) + mm_nt(up_low[:count], up_full)
    recv, mine = sync(recv, mine)

    two = ring(block_of(mine, recv, 2).astype(BF16), -1)
    gate_grad = mm_tn(normed_three, gate_low).astype(BF16)
    up_grad = mm_tn(normed_three, up_low).astype(BF16)
    two, gate_grad, up_grad, gate_lanes, up_halves = sync(
        two, gate_grad, up_grad, lanes_terms(gate_grad), halves_block(up_grad, 1 - half)
    )

    one = ring((block_of(mine, recv, 1) + two.astype(F32)).astype(BF16), -1)
    gate_lanes, up_halves = links.sum_lanes(gate_lanes), over_half(up_halves)
    lanes_keep, lanes_move = lanes_second(down_grad, down_lanes)
    halves_keep, halves_move = halves_second(down_grad, down_halves)
    three_send = block_of(mine, recv, 3).astype(BF16)
    one, gate_lanes, up_halves, gate_halves, up_lanes, lanes_move, halves_move, three_send = sync(
        one,
        gate_lanes,
        up_halves,
        halves_block(gate_grad, 1 - half),
        lanes_terms(up_grad),
        lanes_move,
        halves_move,
        three_send,
    )

    three = ring(three_send, 1)
    up_lanes, gate_halves = links.sum_lanes(up_lanes), over_half(gate_halves)
    gate_keep, gate_move = lanes_second(gate_grad, gate_lanes)
    up_late_keep, up_late_move = halves_second(up_grad, up_halves)
    three, up_lanes, gate_halves, gate_keep, gate_move, up_late_keep, up_late_move = sync(
        three, up_lanes, gate_halves, gate_keep, gate_move, up_late_keep, up_late_move
    )

    hidden_two_grad, low, third_gain_grad = norm_backward(
        hidden_two, third_norm_gain, upstream, mine, recv, one, three
    )
    low_over = over_half(low)
    out_one = ring((block_of(out_mine, out_recv, 1) + out_two.astype(F32)).astype(BF16), -1)
    up_late_move, halves_move = links.sum_lanes(up_late_move), links.sum_lanes(halves_move)
    out_send = block_of(out_mine, out_recv, 3).astype(BF16)
    low_over, out_one, up_late_move, halves_move, out_send = sync(
        low_over, out_one, up_late_move, halves_move, out_send
    )

    lanes_move, gate_move, out_three = over_half(lanes_move), over_half(gate_move), ring(out_send, 1)
    branch_two = spread_cores(low, low_over)
    cross_out_grad = mm(branch_two, cross_output_full).astype(BF16)
    cross_query_round, cross_key_back, cross_value_back = cross_backward(
        cross_query_low, context_low, cross_low, cross_out_grad, cross_logsum, context_count
    )
    partial, send = halves_of(cross_query_round, cross_query_full)
    partial, send, lanes_move, gate_move, out_three, branch_two = sync(
        partial, send, lanes_move, gate_move, out_three, branch_two
    )
    (recv,) = sync(over_core(send))

    def part_of(grads, place):
        count = grads.shape[0] // links.fsdp
        return lax.dynamic_slice_in_dim(grads, place * count, count, 0)

    def lanes_total(block, back, recv):
        return block(links.place(back, 0)).astype(F32) + recv.astype(F32)

    def lanes_send(block, back):
        return links.sum_lanes(lambda turn: block(links.place(back, turn)))

    def cross_block(place):
        return jnp.concatenate([part_of(g, place) for g in cross_grads], axis=0)

    def lanes_blocks(block, back):
        return [block(links.place(back, turn)) for turn in range(1, lane_count)]

    def out_of(values, back):
        return lax.dynamic_index_in_dim(values, links.ring_at(back), 0, keepdims=False)

    terms = with_core(partial, recv)
    far_term = over_half(terms[1])
    up_keep, up_move = lanes_second(up_grad, up_lanes)
    gate_late_keep, gate_late_move = halves_second(gate_grad, gate_halves)
    cross_grads = [
        mm_tn(branch_two, cross_low).astype(BF16),
        mm_tn(normed_two, cross_query_round).astype(BF16),
        mm_tn(context, cross_key_back).astype(BF16),
        mm_tn(context, cross_value_back).astype(BF16),
    ]
    far_term, cross_grads, up_move, gate_late_move, cross2 = sync(
        far_term, cross_grads, up_move, gate_late_move, lanes_blocks(cross_block, 2)
    )

    hidden_one_grad, low, second_gain_grad = norm_backward(
        hidden_one, second_norm_gain, hidden_two_grad, terms[0], far_term
    )
    low_over = over_half(low)
    up_move, gate_late_move = over_half(up_move), links.sum_lanes(gate_late_move)
    cross2 = links.sum_lanes(cross2)
    low_over, cross2, up_move, gate_late_move, cross3, cross1 = sync(
        low_over,
        cross2,
        up_move,
        gate_late_move,
        lanes_blocks(cross_block, 3),
        lanes_blocks(cross_block, 1),
    )

    feed_mine = jnp.concatenate(
        [
            joined(lanes_keep, lanes_move, halves_keep, halves_move),
            joined(gate_keep, gate_move, gate_late_keep, gate_late_move),
            joined(up_keep, up_move, up_late_keep, up_late_move),
        ],
        axis=2,
    )
    feed1_sum, feed3_sum = ring(out_of(feed_mine, 3), 1), ring(out_of(feed_mine, 1), -1)
    cross3, cross1 = links.sum_lanes(cross3), links.sum_lanes(cross1)
    branch_one = spread_cores(low, low_over)
    self_out_grad = mm(branch_one, output_full).astype(BF16)
    qkv_round = self_backward(qkv_low, self_low, self_out_grad, self_logsum, tables)
    partial, send = halves_of(qkv_round, qkv_full)
    feed_mine, branch_one, qkv_round, partial, send, feed1_sum, feed3_sum, cross3, cross1 = sync(
        feed_mine, branch_one, qkv_round, partial, send, feed1_sum, feed3_sum, cross3, cross1
    )
    (recv,) = sync(over_core(send))

    def self_block(place):
        return jnp.concatenate([part_of(output_grad, place), part_of(qkv_grad, place)], axis=1)

    terms = with_core(partial, recv)
    far_term = over_half(terms[1])
    cross_two = ring(lanes_total(cross_block, 2, cross2).astype(BF16), -1)
    cross0 = links.sum_lanes(lanes_blocks(cross_block, 0))
    output_grad = mm_tn(branch_one, self_low).astype(BF16)
    qkv_grad = mm_tn(normed_one, qkv_round).astype(BF16)
    context_term = (
        mm_nt(cross_key_back, context_full[:, :cols])
        + mm_nt(cross_value_back, context_full[:, cols:])
    )[:context_count]
    far_term, cross0, cross_two, output_grad, qkv_grad, self2, context_send = sync(
        far_term,
        cross0,
        cross_two,
        output_grad,
        qkv_grad,
        lanes_blocks(self_block, 2),
        context_term.astype(BF16),
    )

    self2 = links.sum_lanes(self2)
    feed2_sum = ring(out_of(feed_mine, 2), 2)
    context_recv = over_core(context_send)
    inputs_grad, _, first_gain_grad = norm_backward(
        own, first_norm_gain, hidden_one_grad, terms[0], far_term
    )
    context_low_sum = (context_term + context_recv.astype(F32)).astype(BF16)
    gain_grads = jnp.concatenate([first_gain_grad, second_gain_grad, third_gain_grad], axis=0)
    self2, feed2_sum, context_low_sum, gain_grads, inputs_grad, self3 = sync(
        self2, feed2_sum, context_low_sum, gain_grads, inputs_grad, lanes_blocks(self_block, 3)
    )

    self3 = links.sum_lanes(self3)
    self_two = ring(lanes_total(self_block, 2, self2).astype(BF16), -1)
    context_over = over_half(context_low_sum)
    gain_grads = gain_grads + over_core(gain_grads)
    gate_sum, up_sum, down_sum = spread(
        [out_of(feed_mine, 0), feed1_sum, feed2_sum, feed3_sum],
        jnp.stack([links.ring_at(back) for back in range(RING)]),
    )
    layer_result = links.both_cores(
        hidden_two + block_of(out_mine, out_recv, 0) + out_one.astype(F32) + out_three.astype(F32)
    )
    self3, self_two, context_over, gain_grads, layer_result, self1, cross_sends = sync(
        self3,
        self_two,
        context_over,
        gain_grads,
        layer_result,
        lanes_blocks(self_block, 1),
        [
            lanes_total(cross_block, 3, cross3).astype(BF16),
            (lanes_total(cross_block, 1, cross1) + cross_two.astype(F32)).astype(BF16),
        ],
    )

    self1 = links.sum_lanes(self1)
    cross_three, cross_one = ring(cross_sends[0], 1), ring(cross_sends[1], -1)
    context_grad = context_low_sum.astype(F32) + context_over.astype(F32)
    inputs_result = links.both_cores(inputs_grad)
    gain_over = over_half(gain_grads)
    self1, cross_three, cross_one, gain_over, inputs_result, self0 = sync(
        self1, cross_three, cross_one, gain_over, inputs_result, lanes_blocks(self_block, 0)
    )

    self0 = links.sum_lanes(self0)
    self_one = ring((lanes_total(self_block, 1, self1) + self_two.astype(F32)).astype(BF16), -1)
    self_three = ring(lanes_total(self_block, 3, self3).astype(BF16), 1)
    cross_total = (
        lanes_total(cross_block, 0, cross0) + cross_one.astype(F32) + cross_three.astype(F32)
    )
    sizes = (shard, shard, context_shard, context_shard)
    starts = [2 * sum(sizes[:n]) for n in range(4)]
    cross_total = jnp.concatenate(
        [
            cross_total[start : start + 2 * size].reshape(2, size, cols)
            for start, size in zip(starts, sizes)
        ],
        axis=1,
    )
    cross_keep, cross_recv = links.swap_halves(cross_total)
    gain_grads = gain_grads + gain_over
    gain_ring = [slot(gain_grads, RING, links.ring_at(back)) for back in range(RING)]
    gain_two, gain_three = ring(gain_ring[2], -1), ring(gain_ring[3], 1)
    self0, self_one, self_three, cross_recv, gain_two, gain_three = sync(
        self0, self_one, self_three, cross_recv, gain_two, gain_three
    )

    gain_one = ring(gain_ring[1] + gain_two, -1)
    cross_sums = links.side_by_side(cross_keep, cross_recv)
    self_total = (
        lanes_total(self_block, 0, self0) + self_one.astype(F32) + self_three.astype(F32)
    )
    keep, recv = links.swap_halves(self_total.reshape(2, shard, 4 * cols))
    gain_grads = gain_ring[0] + gain_one + gain_three
    gain_total = slot(gain_grads, lane_count, links.lane_at(1))
    for turn in list(range(2, lane_count)) + [0]:
        gain_total = links.lanes(gain_total) + slot(gain_grads, lane_count, links.lane_at(turn))
    gain_sums = slot(gain_total, 2, half)

    def of_self(values, n):
        if n == 3:
            return values[:, :cols]
        return jnp.concatenate(
            [
                values[:, cols + (3 * pair + n) * PAIR : cols + (3 * pair + n + 1) * PAIR]
                for pair in range(pairs)
            ],
            axis=1,
        )

    query_sum, key_sum, value_sum, output_sum = (
        links.side_by_side(of_self(keep, n), of_self(recv, n)) for n in range(4)
    )
    return (
        layer_result[None],
        inputs_result[None],
        context_grad[None],
        query_sum,
        key_sum,
        value_sum,
        output_sum.T,
        cross_sums[shard : 2 * shard],
        cross_sums[2 * shard : 2 * shard + context_shard],
        cross_sums[2 * shard + context_shard :],
        cross_sums[:shard].T,
        gate_sum,
        up_sum,
        down_sum.T,
        gain_sums[0],
        gain_sums[1],
        gain_sums[2],
    )


def solution(mesh):
    row = P(("fsdp", "ctx"), "tp")
    col = P("tp", ("fsdp", "ctx"))
    gain = P(("fsdp", "ctx"))
    token = P("fsdp", "ctx", None)
    context = P("fsdp", None, None)
    weights = (row, row, row, col, row, row, row, col, row, row, col, gain, gain, gain)
    return jax.shard_map(
        functools.partial(on_device, mesh),
        mesh=mesh,
        in_specs=(token, context) + weights + (token,),
        out_specs=(token, token, context) + weights,
        check_vma=False,
    )
```

```python
import functools
import math

import jax
import jax.numpy as jnp
from jax import lax
from jax.experimental import pallas as pl
from jax.experimental.pallas import tpu as pltpu
from jax.sharding import PartitionSpec as P

HDIM = 64
EPSILON = 1e-05
F32 = jnp.float32
BF16 = jnp.bfloat16
SCALE = HDIM ** (-0.5)
PAIR = 2 * HDIM
VMEM_LIMIT = 48 * 1024 * 1024
VMEM_MOST = 60 * 1024 * 1024


def mm(left, right):
    return lax.dot_general(left, right, (((1,), (0,)), ((), ())), preferred_element_type=F32)


def mm_tn(left, right):
    return lax.dot_general(left, right, (((0,), (0,)), ((), ())), preferred_element_type=F32)


def mm_nt(left, right):
    return lax.dot_general(left, right, (((1,), (1,)), ((), ())), preferred_element_type=F32)


def norm_stats(values):
    center = values - jnp.mean(values, axis=-1, keepdims=True)
    rate = lax.rsqrt(jnp.mean(center * center, axis=-1, keepdims=True) + EPSILON)
    return center * rate, rate


def params(limit=VMEM_LIMIT):
    return pltpu.CompilerParams(vmem_limit_bytes=limit)


def norm_call(kernel, rows, outs, *operands):
    width = operands[0].shape[1]

    def block(count):
        return pl.BlockSpec((count, width), lambda step: (0, 0))

    return pl.pallas_call(
        kernel,
        grid=(1,),
        in_specs=[block(min(rows, operand.shape[0])) for operand in operands],
        out_specs=[block(count) for count, _ in outs],
        out_shape=[jax.ShapeDtypeStruct((count, width), kind) for count, kind in outs],
        compiler_params=params(),
    )(*operands)


def norm_forward_kernel(gain_ref, base_ref, *refs):
    *terms, x_ref, n_ref = refs
    values = base_ref[...].astype(F32)
    for term in terms:
        values = values + term[...].astype(F32)
    x_ref[...] = values
    n_ref[...] = (norm_stats(values)[0] * gain_ref[...]).astype(BF16)


def norm_forward(rows, base, gain, *terms):
    return norm_call(norm_forward_kernel, rows, ((rows, F32), (rows, BF16)), gain, base, *terms)


def pair_forward_kernel(gain_ref, own_ref, over_ref, near_ref, core_ref, far_ref, x_ref, n_ref):
    rows = own_ref.shape[0]
    for base, first in ((own_ref, 0), (over_ref, rows)):
        part, other = slice(first, first + rows), slice(rows - first, 2 * rows - first)
        values = base[...].astype(F32) + near_ref[part, :]
        values = values + core_ref[part, :].astype(F32) + far_ref[other, :].astype(F32)
        x_ref[part, :] = values
        n_ref[part, :] = (norm_stats(values)[0] * gain_ref[...]).astype(BF16)


def pair_forward(gain, own, over, near, core, far):
    rows, width = near.shape
    return pl.pallas_call(
        pair_forward_kernel,
        out_shape=(
            jax.ShapeDtypeStruct((rows, width), F32),
            jax.ShapeDtypeStruct((rows, width), BF16),
        ),
        compiler_params=params(),
    )(gain, own, over, near, core, far)


def pair_backward_kernel(
    gain_ref, x_ref, skip_ref, over_ref, near_ref, core_ref, far_ref, dx_ref, low_ref, dg_ref
):
    rows = skip_ref.shape[0]
    for skip, first in ((skip_ref, 0), (over_ref, rows)):
        part, other = slice(first, first + rows), slice(rows - first, 2 * rows - first)
        upstream = near_ref[part, :] + core_ref[part, :].astype(F32) + far_ref[other, :].astype(F32)
        unit, rate = norm_stats(x_ref[part, :])
        scaled = upstream * gain_ref[...]
        back = rate * (
            scaled
            - jnp.mean(scaled, axis=-1, keepdims=True)
            - unit * jnp.mean(scaled * unit, axis=-1, keepdims=True)
        )
        total = skip[...].astype(F32) + back
        low_ref[part, :] = total.astype(BF16)
        if first == 0:
            dx_ref[...] = total
            dg_ref[...] = jnp.sum(upstream * unit, axis=0, keepdims=True)


def pair_backward(gain, values, skip, over, near, core, far):
    rows, width = values.shape
    return pl.pallas_call(
        pair_backward_kernel,
        out_shape=(
            jax.ShapeDtypeStruct((rows // 2, width), F32),
            jax.ShapeDtypeStruct((rows, width), BF16),
            jax.ShapeDtypeStruct((1, width), F32),
        ),
        compiler_params=params(),
    )(gain, values, skip, over, near, core, far)


def norm_backward_kernel(gain_ref, x_ref, skip_ref, *refs):
    *terms, dx_ref, low_ref, dg_ref = refs
    upstream = terms[0][...].astype(F32)
    for term in terms[1:]:
        upstream = upstream + term[...].astype(F32)
    unit, rate = norm_stats(x_ref[...].astype(F32))
    scaled = upstream * gain_ref[...]
    back = rate * (
        scaled
        - jnp.mean(scaled, axis=-1, keepdims=True)
        - unit * jnp.mean(scaled * unit, axis=-1, keepdims=True)
    )
    total = skip_ref[...].astype(F32) + back
    dx_ref[...] = total
    low_ref[...] = total.astype(BF16)
    dg_ref[...] = jnp.sum(upstream * unit, axis=0, keepdims=True)


def norm_backward(values, gain, skip, *terms):
    rows = values.shape[0]
    outs = (rows, F32), (rows, BF16), (1, F32)
    return norm_call(norm_backward_kernel, rows, outs, gain, values, skip, *terms)


def turned(values, cosine, upper, lower):
    width = values.shape[1]
    return (
        values * cosine
        + pltpu.roll(values, width - HDIM // 4, 1) * upper
        + pltpu.roll(values, HDIM // 4, 1) * lower
    )


def chunk_of(rows):
    return 128 if rows % 128 == 0 else rows


def low_half(shape):
    return lax.broadcasted_iota(jnp.int32, shape, len(shape) - 1) < HDIM


def of_head(values, head):
    first = low_half(values.shape)
    keep = first if head == 0 else jnp.logical_not(first)
    return jnp.where(keep, values, jnp.zeros((), values.dtype))


def forward_heads(q_ref, k_ref, v_ref, o_ref, lse_ref, valid):
    rows = q_ref.shape[0]
    step = chunk_of(rows)
    key, value = k_ref[...], v_ref[...]
    first_half = low_half(value.shape)
    ones = jnp.ones((), BF16)
    extended = jnp.where(first_half, value, ones), jnp.where(first_half, ones, value)
    for first in range(0, rows, step):
        part = slice(first, first + step)
        query = q_ref[part, :]
        results = []
        for head in range(2):
            scores = mm_nt(of_head(query, head), key)
            if valid < key.shape[0]:
                column = lax.broadcasted_iota(jnp.int32, scores.shape, 1)
                scores = jnp.where(column < valid, scores, -1e30)
            peak = jnp.max(scores, axis=-1, keepdims=True)
            mixed = mm(jnp.exp(scores - peak).astype(BF16), extended[head])
            total = pltpu.roll(mixed, HDIM, 1)
            results.append((mixed * (1.0 / total), peak + jnp.log(total)))
        lanes = low_half((step, PAIR))
        o_ref[part, :] = jnp.where(lanes, results[0][0], results[1][0]).astype(BF16)
        lse_ref[part, :] = jnp.where(lanes, results[0][1], results[1][1])


def thirds(ref):
    return ref.at[:, :PAIR], ref.at[:, PAIR : 2 * PAIR], ref.at[:, 2 * PAIR :]


def self_forward_kernel(shard, place_ref, *refs):
    n_pieces = len(refs) - 23
    pieces, refs = refs[:n_pieces], refs[n_pieces:]
    parts, refs = refs[:4], refs[4:]
    cos_ref, up_ref, low_ref, *refs = refs
    turned_ref, o_ref, lse_ref, mine_ref, send_ref, gain_ref, *refs = refs
    qkv_out, output_out, normed_out, *refs = refs
    qkv_all, output_all, normed_all, gain_all, o_all = refs[:-2]
    sems, out_sems = refs[-2:]
    pair, cols = pl.program_id(0), qkv_all.shape[1]
    gain_rows = gain_all.shape[0] // n_pieces

    @pl.when(pair == 0)
    def _():
        copies = []
        for n, piece in enumerate(pieces):
            mark = pl.ds(n * gain_rows, gain_rows)
            copies.append((piece.at[pl.ds(2 * shard, gain_rows), pl.ds(0, gain_all.shape[1])], gain_all.at[mark, :]))
        for n, piece in enumerate(pieces):
            for there in (0, 1):
                row = pl.ds(pl.multiple_of(place_ref[2 * n + there] * shard, shard), shard)
                lines = pl.ds(there * shard, shard)
                copies.append((piece.at[lines, pl.ds(0, cols)], qkv_all.at[row, :]))
                copies.append((piece.at[lines, pl.ds(cols, output_all.shape[1])], output_all.at[row, :]))
        copies = [
            pltpu.make_async_copy(source, target, sems.at[n])
            for n, (source, target) in enumerate(copies)
        ]
        for copy in copies:
            copy.start()
        for copy in copies[:n_pieces]:
            copy.wait()
        gains = jnp.zeros((gain_rows, gain_all.shape[1]), F32)
        for n in range(n_pieces):
            gains = gains + gain_all[n * gain_rows : (n + 1) * gain_rows, :].astype(F32)
        gain_ref[...] = gains
        first = 0
        for part in parts:
            unit, _ = norm_stats(part[...].astype(F32))
            normed_all[first : first + part.shape[0], :] = (unit * gains[:1]).astype(BF16)
            first += part.shape[0]
        for copy in copies[n_pieces:]:
            copy.wait()

    exports = [
        pltpu.make_async_copy(source, target, out_sems.at[n])
        for n, (source, target) in enumerate(
            ((qkv_all, qkv_out), (output_all, output_out), (normed_all, normed_out))
        )
    ]

    @pl.when(pair == 0)
    def _():
        for export in exports:
            export.start()

    tables = cos_ref[...], up_ref[...], low_ref[...]
    q_ref, k_ref, v_ref = thirds(turned_ref)
    first = pl.multiple_of(pair * 3 * PAIR, PAIR)
    qkv = mm(normed_all[...], qkv_all[:, pl.ds(first, 3 * PAIR)])
    q_ref[...] = turned(qkv[:, :PAIR], *tables).astype(BF16) * jnp.asarray(SCALE, BF16)
    k_ref[...] = turned(qkv[:, PAIR : 2 * PAIR], *tables).astype(BF16)
    v_ref[...] = qkv[:, 2 * PAIR :].astype(BF16)
    forward_heads(q_ref, k_ref, v_ref, o_ref, lse_ref, k_ref.shape[0])
    o_all[:, pl.ds(pl.multiple_of(pair * PAIR, PAIR), PAIR)] = o_ref[...]

    @pl.when(pair == pl.num_programs(0) - 1)
    def _():
        half = o_all.shape[0] // 2
        mine_ref[...] = mm_nt(o_all[:half, :], output_all[...])
        send_ref[...] = mm_nt(o_all[half:, :], output_all[...]).astype(BF16)
        for export in exports:
            export.wait()


def self_forward(pieces, place, parts, tables, shard):
    width, cols = parts[0].shape[1], pieces[0].shape[1] // 4
    rows, pairs = sum(part.shape[0] for part in parts), cols // PAIR
    gain_rows = pieces[0].shape[0] - 2 * shard
    vmem, anywhere = pl.BlockSpec(memory_space=pltpu.VMEM), pl.BlockSpec(memory_space=pl.ANY)

    def paired(width):
        return pl.BlockSpec((rows, width), lambda pair: (0, pair))

    def whole(shape):
        return pl.BlockSpec(shape, lambda pair: (0, 0))

    return pl.pallas_call(
        functools.partial(self_forward_kernel, shard),
        grid=(pairs,),
        in_specs=[pl.BlockSpec(memory_space=pltpu.SMEM)]
        + [anywhere] * len(pieces)
        + [whole(part.shape) for part in parts]
        + [whole((rows, PAIR))] * 3,
        out_specs=[paired(3 * PAIR), paired(PAIR), paired(PAIR)]
        + [whole((rows // 2, width))] * 2
        + [whole((gain_rows, width))]
        + [anywhere] * 3,
        out_shape=[
            jax.ShapeDtypeStruct((rows, 3 * cols), BF16),
            jax.ShapeDtypeStruct((rows, cols), BF16),
            jax.ShapeDtypeStruct((rows, cols), F32),
            jax.ShapeDtypeStruct((rows // 2, width), F32),
            jax.ShapeDtypeStruct((rows // 2, width), BF16),
            jax.ShapeDtypeStruct((gain_rows, width), F32),
            jax.ShapeDtypeStruct((width, 3 * cols), BF16),
            jax.ShapeDtypeStruct((width, cols), BF16),
            jax.ShapeDtypeStruct((rows, width), BF16),
        ],
        scratch_shapes=[
            pltpu.VMEM((width, 3 * cols), BF16),
            pltpu.VMEM((width, cols), BF16),
            pltpu.VMEM((rows, width), BF16),
            pltpu.VMEM((len(pieces) * gain_rows, width), BF16),
            pltpu.VMEM((rows, cols), BF16),
            pltpu.SemaphoreType.DMA((5 * len(pieces),)),
            pltpu.SemaphoreType.DMA((3,)),
        ],
        compiler_params=params(VMEM_MOST),
        cost_estimate=pl.CostEstimate(
            flops=4 * rows * rows * cols + 2 * rows * width * 4 * cols,
            bytes_accessed=8 * width * cols + 2 * rows * width,
            transcendentals=rows * rows * cols // HDIM,
        ),
    )(place, *pieces, *parts, *tables)


def cross_forward_kernel(valid, q_ref, k_ref, v_ref, o_ref, lse_ref):
    forward_heads(q_ref, k_ref, v_ref, o_ref, lse_ref, valid)


def backward_heads(q_ref, k_ref, v_ref, o_ref, do_ref, lse_ref, dq_ref, dk_ref, dv_ref, valid):
    rows = q_ref.shape[0]
    step = chunk_of(rows)
    key, value = k_ref[...], v_ref[...]
    for first in range(0, rows, step):
        part = slice(first, first + step)
        query, grad = q_ref[part, :], do_ref[part, :]
        lse = lse_ref[part, :].T
        delta = (grad.astype(F32) * o_ref[part, :].astype(F32)).T
        query_terms = []
        for head in range(2):
            query_head, grad_head = of_head(query, head), of_head(grad, head)
            lanes = slice(head * HDIM, (head + 1) * HDIM)
            mean_grad = jnp.sum(delta[lanes, :], axis=0, keepdims=True)
            probability = jnp.exp(mm_nt(key, query_head) - lse[head * HDIM : head * HDIM + 1, :])
            if valid < key.shape[0]:
                line = lax.broadcasted_iota(jnp.int32, probability.shape, 0)
                probability = jnp.where(line < valid, probability, 0.0)
            score_grad = (probability * (mm_nt(value, grad_head) - mean_grad)).astype(BF16)
            query_terms.append(mm_tn(score_grad, key))
            key_term = mm(score_grad, query_head)
            value_term = mm(probability.astype(BF16), grad_head)
            if first == 0 and head == 0:
                dk_ref[...] = key_term
                dv_ref[...] = value_term
            else:
                dk_ref[...] += key_term
                dv_ref[...] += value_term
        dq_ref[part, :] = jnp.where(low_half((step, PAIR)), *query_terms) * SCALE


def self_backward_kernel(
    turned_ref, o_ref, do_ref, lse_ref, cos_ref, up_ref, low_ref, out_ref, dq_acc, dk_acc, dv_acc
):
    q_ref, k_ref, v_ref = thirds(turned_ref)
    backward_heads(
        q_ref, k_ref, v_ref, o_ref, do_ref, lse_ref, dq_acc, dk_acc, dv_acc, k_ref.shape[0]
    )
    tables = cos_ref[...], -up_ref[...], -low_ref[...]
    dq_ref, dk_ref, dv_ref = thirds(out_ref)
    dq_ref[...] = turned(dq_acc[...], *tables).astype(BF16)
    dk_ref[...] = turned(dk_acc[...], *tables).astype(BF16)
    dv_ref[...] = dv_acc[...].astype(BF16)


def cross_backward_kernel(
    valid, q_ref, k_ref, v_ref, o_ref, do_ref, lse_ref, dq_ref, dk_ref, dv_ref, dq_acc, dk_acc, dv_acc
):
    some = -(-valid // 16) * 16
    backward_heads(
        q_ref, k_ref.at[:some, :], v_ref.at[:some, :], o_ref, do_ref, lse_ref,
        dq_acc, dk_acc.at[:some, :], dv_acc.at[:some, :], valid,
    )
    dq_ref[...] = dq_acc[...].astype(BF16)
    for ref, acc in ((dk_ref, dk_acc), (dv_ref, dv_acc)):
        ref[:some, :] = acc[:some, :].astype(BF16)
        if some < ref.shape[0]:
            ref[some:, :] = jnp.zeros((ref.shape[0] - some, PAIR), BF16)


def attention_call(kernel, pairs, ins, outs, scratch, flops):
    return pl.pallas_call(
        kernel,
        grid=(pairs,),
        in_specs=[
            pl.BlockSpec((rows, width), functools.partial(lambda place, pair: (0, place(pair)), place))
            for rows, width, place in ins
        ],
        out_specs=[pl.BlockSpec((rows, width), lambda pair: (0, pair)) for rows, width, _ in outs],
        out_shape=[
            jax.ShapeDtypeStruct((rows, width * pairs), kind) for rows, width, kind in outs
        ],
        scratch_shapes=[pltpu.VMEM((rows, PAIR), F32) for rows in scratch],
        compiler_params=params(),
        cost_estimate=pl.CostEstimate(
            flops=flops,
            bytes_accessed=4 * pairs * sum(rows * width for rows, width, _ in ins),
            transcendentals=flops // 256,
        ),
    )


def here(pair):
    return pair


def always(pair):
    return 0


def self_backward(qkv, out, grad, lse, tables):
    rows, pairs = qkv.shape[0], qkv.shape[1] // (3 * PAIR)
    return attention_call(
        self_backward_kernel,
        pairs,
        [(rows, 3 * PAIR, here)] + [(rows, PAIR, here)] * 3 + [(rows, PAIR, always)] * 3,
        [(rows, 3 * PAIR, BF16)],
        (rows,) * 3,
        10 * rows * rows * pairs * PAIR,
    )(qkv, out, grad, lse, *tables)[0]


def cross_forward(query, context, valid):
    rows, pairs, keys = query.shape[0], query.shape[1] // PAIR, context.shape[0]
    return attention_call(
        functools.partial(cross_forward_kernel, valid),
        pairs,
        [(rows, PAIR, here), (keys, PAIR, here), (keys, PAIR, lambda pair: pairs + pair)],
        [(rows, PAIR, BF16), (rows, PAIR, F32)],
        (),
        4 * rows * keys * pairs * PAIR,
    )(query, context, context)


def cross_backward(query, context, out, grad, lse, valid):
    rows, pairs, keys = query.shape[0], query.shape[1] // PAIR, context.shape[0]
    return attention_call(
        functools.partial(cross_backward_kernel, valid),
        pairs,
        [(rows, PAIR, here), (keys, PAIR, here), (keys, PAIR, lambda pair: pairs + pair)]
        + [(rows, PAIR, here)] * 3,
        [(rows, PAIR, BF16), (keys, PAIR, BF16), (keys, PAIR, BF16)],
        (rows, keys, keys),
        10 * rows * keys * pairs * PAIR,
    )(query, context, context, out, grad, lse)


def rotary_tables(position):
    quarter = HDIM // 4
    lane = lax.broadcasted_iota(jnp.int32, (position.shape[0], PAIR), 1) & (HDIM - 1)
    turn = (lane & (quarter - 1)).astype(F32)
    frequency = jnp.exp(-(2.0 * turn / (2 * quarter)) * math.log(10000.0))
    angles = position.astype(F32)[:, None] * frequency
    cosine, sine = jnp.cos(angles), jnp.sin(angles)
    return (
        jnp.where(lane < 2 * quarter, cosine, 1.0),
        jnp.where(lane < quarter, -sine, 0.0),
        jnp.where((lane >= quarter) & (lane < 2 * quarter), sine, 0.0),
    )


def place_kernel(plan, n_pieces, place_ref, *refs):
    pieces, outs = refs[:n_pieces], refs[n_pieces:]
    for piece, spot, src_row, rows, src_col, cols, out, dst_col in plan:
        row = pl.multiple_of(place_ref[spot] * rows, rows)
        outs[out][pl.ds(row, rows), dst_col : dst_col + cols] = pieces[piece][
            src_row : src_row + rows, src_col : src_col + cols
        ]


def place_pieces(pieces, plan, place, outs):
    if any(entry[2] % 16 or entry[3] % 16 for entry in plan):
        whole = [jnp.zeros(out, BF16) for out in outs]
        for piece, spot, src_row, rows, src_col, cols, out, dst_col in plan:
            part = pieces[piece][src_row : src_row + rows, src_col : src_col + cols]
            whole[out] = lax.dynamic_update_slice(whole[out], part, (place[spot] * rows, dst_col))
        return whole
    vmem = pl.BlockSpec(memory_space=pltpu.VMEM)
    return pl.pallas_call(
        functools.partial(place_kernel, tuple(plan), len(pieces)),
        in_specs=[pl.BlockSpec(memory_space=pltpu.SMEM)] + [vmem] * len(pieces),
        out_specs=[vmem] * len(outs),
        out_shape=[jax.ShapeDtypeStruct(out, BF16) for out in outs],
        compiler_params=params(),
        cost_estimate=pl.CostEstimate(
            flops=0, transcendentals=0, bytes_accessed=4 * sum(math.prod(out) for out in outs)
        ),
    )(place, *pieces)


def feed_kernel(shard, own, n_held, plan, place_ref, *refs):
    n_pieces = len(refs) - 13 - n_held
    pieces, held, refs = refs[:n_pieces], refs[n_pieces : n_pieces + n_held], refs[n_pieces + n_held :]
    tokens, cotangents = [
        [held[n].at[pl.ds(part * own, own), :] for n, part in parts] for parts in plan
    ]
    hid_ref, low_ref, send_ref, mine_ref, n_out, ct_out, down_out, *refs = refs
    gate_up, down, n_all, ct_all, sems, out_sems = refs
    step, steps = pl.program_id(0), pl.num_programs(0)
    hidden = down.shape[1]
    block = n_all.shape[0] // steps
    each = 8 // steps

    def row(n):
        return pl.ds(pl.multiple_of(place_ref[n] * shard, shard), shard)

    def copies_of(sources, target, first):
        return [
            pltpu.make_async_copy(source, target.at[pl.ds(n * own, own), :], sems.at[first + n])
            for n, source in enumerate(sources)
        ]

    inward = copies_of(tokens, n_all, 0), copies_of(cotangents, ct_all, 8)
    weights = [
        pltpu.make_async_copy(piece.at[:, pl.ds(0, 2 * hidden)], gate_up.at[row(n), :], sems.at[16 + n])
        for n, piece in enumerate(pieces)
    ]
    downs = [
        pltpu.make_async_copy(
            piece.at[:, pl.ds(2 * hidden, hidden)], down.at[row(n), :], sems.at[16 + n_pieces + n]
        )
        for n, piece in enumerate(pieces)
    ]

    @pl.when(step == 0)
    def _():
        for copy in inward[0][:each] + weights + inward[1][:each] + downs:
            copy.start()
        for copy in inward[0][each:] + inward[1][each:]:
            copy.start()
        for copy in weights:
            copy.wait()

    @pl.when(step == 0)
    def _():
        for copy in inward[0][:each]:
            copy.wait()

    @pl.when(step == 1)
    def _():
        for copy in inward[0][each:]:
            copy.wait()

    part = pl.ds(pl.multiple_of(step * block, block), block)
    both = mm(n_all[part, :], gate_up[...])
    gate, up = both[:, :hidden], both[:, hidden:]
    sigmoid = 1.0 / (1.0 + jnp.exp(-gate))
    silu = gate * sigmoid
    hid_ref[...] = (silu * up).astype(BF16)
    slope = up * sigmoid * (1.0 + gate * (1.0 - sigmoid))

    @pl.when(step == 0)
    def _():
        for copy in downs:
            copy.wait()

    @pl.when(step == 0)
    def _():
        for copy in inward[1][:each]:
            copy.wait()

    exports = [
        pltpu.make_async_copy(source, target, out_sems.at[n])
        for n, (source, target) in enumerate(((n_all, n_out), (ct_all, ct_out), (down, down_out)))
    ]

    @pl.when(step == 1)
    def _():
        for copy in inward[1][each:]:
            copy.wait()
        for export in exports:
            export.start()

    back = mm(ct_all[part, :], down[...]).astype(BF16).astype(F32)
    gate_low = (back * slope).astype(BF16)
    up_low = (back * silu).astype(BF16)
    low_ref[:, :hidden] = gate_low
    low_ref[:, hidden:] = up_low
    result = mm_nt(low_ref[...], gate_up[...])

    @pl.when(step < steps // 2)
    def _():
        send_ref[...] = result.astype(BF16)

    @pl.when(step >= steps // 2)
    def _():
        mine_ref[...] = result

    @pl.when(step == steps - 1)
    def _():
        for export in exports:
            export.wait()


def feed_forward(pieces, place, held, tokens, cotangents, shard, own):
    width = held[0].shape[1]
    hidden = pieces[0].shape[1] // 3
    rows = 8 * own
    steps = 4
    block = rows // steps
    vmem, anywhere = pl.BlockSpec(memory_space=pltpu.VMEM), pl.BlockSpec(memory_space=pl.ANY)
    half = steps // 2

    def blocks(cols):
        return pl.BlockSpec((block, cols), lambda step: (step, 0))

    return pl.pallas_call(
        functools.partial(
            feed_kernel, shard, own, len(held), (tuple(tokens), tuple(cotangents))
        ),
        grid=(steps,),
        in_specs=[pl.BlockSpec(memory_space=pltpu.SMEM)] + [anywhere] * (len(pieces) + len(held)),
        out_specs=[blocks(hidden), blocks(2 * hidden)]
        + [
            pl.BlockSpec((block, width), lambda step: (jnp.minimum(step, half - 1), 0)),
            pl.BlockSpec((block, width), lambda step: (jnp.maximum(step - half, 0), 0)),
        ]
        + [anywhere] * 3,
        out_shape=[
            jax.ShapeDtypeStruct((rows, hidden), BF16),
            jax.ShapeDtypeStruct((rows, 2 * hidden), BF16),
            jax.ShapeDtypeStruct((rows // 2, width), BF16),
            jax.ShapeDtypeStruct((rows // 2, width), F32),
            jax.ShapeDtypeStruct((rows, width), BF16),
            jax.ShapeDtypeStruct((rows, width), BF16),
            jax.ShapeDtypeStruct((width, hidden), BF16),
        ],
        scratch_shapes=[
            pltpu.VMEM((width, 2 * hidden), BF16),
            pltpu.VMEM((width, hidden), BF16),
            pltpu.VMEM((rows, width), BF16),
            pltpu.VMEM((rows, width), BF16),
            pltpu.SemaphoreType.DMA((16 + 2 * len(pieces),)),
            pltpu.SemaphoreType.DMA((3,)),
        ],
        compiler_params=params(VMEM_MOST),
        cost_estimate=pl.CostEstimate(
            flops=10 * rows * width * hidden,
            bytes_accessed=6 * width * hidden + 8 * rows * width,
            transcendentals=rows * hidden,
        ),
    )(place, *pieces, *held)


def spread_kernel(place_ref, *refs):
    pieces, (down_out, gate_out, up_out) = refs[:RING], refs[RING:]
    cols = pieces[0].shape[1] // 3
    for n, piece in enumerate(pieces):
        spot = pl.ds(pl.multiple_of(place_ref[n] * cols, cols), cols)
        for m, out in enumerate((down_out, gate_out, up_out)):
            out[:, spot] = piece[:, m * cols : (m + 1) * cols].astype(F32)


def spread(pieces, place):
    rows, cols = pieces[0].shape
    vmem = pl.BlockSpec(memory_space=pltpu.VMEM)
    down, gate, up = pl.pallas_call(
        spread_kernel,
        in_specs=[pl.BlockSpec(memory_space=pltpu.SMEM)] + [vmem] * RING,
        out_specs=[vmem] * 3,
        out_shape=[jax.ShapeDtypeStruct((rows, cols // 3 * RING), F32)] * 3,
        compiler_params=params(),
    )(place, *pieces)
    return gate, up, down


def split_kernel(down, place_ref, *refs):
    grads, outs = refs[: len(down)], refs[len(down) :]
    for n, out in enumerate(outs):
        row = col = 0
        for grad, below in zip(grads, down):
            count, cols = grad.shape[0] // len(outs), grad.shape[1]
            line = pl.ds(pl.multiple_of(place_ref[n] * count, count), count)
            out[row : row + count, col : col + cols] = grad[line, :]
            if below:
                row += count
            else:
                col += cols


def split_blocks(grads, place, below):
    count = place.shape[0]
    rows = [grad.shape[0] // count for grad in grads]
    cols = [grad.shape[1] for grad in grads]
    shape = (sum(rows), cols[0]) if below else (rows[0], sum(cols))
    vmem = pl.BlockSpec(memory_space=pltpu.VMEM)
    return pl.pallas_call(
        functools.partial(split_kernel, (below,) * len(grads)),
        in_specs=[pl.BlockSpec(memory_space=pltpu.SMEM)] + [vmem] * len(grads),
        out_specs=[vmem] * count,
        out_shape=[jax.ShapeDtypeStruct(shape, BF16)] * count,
        compiler_params=params(),
    )(place, *grads)


def pack_early_kernel(half_ref, q_any, k_any, v_any, o_any, gain_ref, send_ref, keep_ref, *scratch):
    *held, sems = scratch
    copies = [
        pltpu.make_async_copy(source, target, sems.at[n])
        for n, (source, target) in enumerate(zip((q_any, k_any, v_any, o_any), held))
    ]
    for copy in copies:
        copy.start()
    for copy in copies:
        copy.wait()
    q_ref, k_ref, v_ref, o_ref = held
    rows, cols = o_ref.shape[0], o_ref.shape[1] // 2
    for out, index in ((send_ref, 1 - half_ref[0]), (keep_ref, half_ref[0])):
        first = pl.multiple_of(index * cols, PAIR)
        for pair in range(cols // PAIR):
            for n, ref in enumerate((q_ref, k_ref, v_ref)):
                spot = (3 * pair + n) * PAIR
                out[:rows, spot : spot + PAIR] = ref[:, pl.ds(first + pair * PAIR, PAIR)]
        out[:rows, 3 * cols :] = o_ref[:, pl.ds(first, cols)]
    send_ref[rows:, :] = gain_ref[...]


def pack_early(query, key, value, output, gains, half, cols):
    rows, full = query.shape
    vmem = pl.BlockSpec(memory_space=pltpu.VMEM)
    anywhere = pl.BlockSpec(memory_space=pl.ANY)
    return pl.pallas_call(
        pack_early_kernel,
        in_specs=[pl.BlockSpec(memory_space=pltpu.SMEM)] + [anywhere] * 4 + [vmem],
        out_specs=[vmem] * 2,
        out_shape=[
            jax.ShapeDtypeStruct((rows + gains.shape[0], 4 * cols), BF16),
            jax.ShapeDtypeStruct((rows, 4 * cols), BF16),
        ],
        scratch_shapes=[pltpu.VMEM((rows, full), BF16)] * 4 + [pltpu.SemaphoreType.DMA((4,))],
        compiler_params=params(VMEM_MOST),
    )(half.reshape(1), query, key, value, output, gains)


RING = 4


class Links:
    def __init__(self, mesh):
        self.fsdp = mesh.shape["fsdp"]
        self.width = self.fsdp // RING
        index = lax.axis_index("fsdp")
        self.at = lax.div(index, self.width)
        self.lane = index - self.at * self.width
        self.half = lax.axis_index("ctx")
        self.core = lax.axis_index("tp")
        self.step = jnp.zeros((8, 128), F32)

    def sync(self, *values):
        flat, tree = jax.tree.flatten(values)
        self.step, *flat = lax.optimization_barrier([self.step, *flat])
        return jax.tree.unflatten(tree, flat)

    def begun(self, value):
        return lax.optimization_barrier([value, self.step])[0]

    def ring(self, value, hops):
        z, r = RING, self.width
        pairs = [(a * r + b, (a + hops) % z * r + b) for a in range(z) for b in range(r)]
        return lax.ppermute(self.begun(value), "fsdp", pairs)

    def lanes(self, value):
        z, r = RING, self.width
        pairs = [(a * r + b, a * r + (b + 1) % r) for a in range(z) for b in range(r)]
        return lax.ppermute(self.begun(value), "fsdp", pairs)

    def over_half(self, value):
        return lax.ppermute(self.begun(value), "ctx", [(0, 1), (1, 0)])

    def over_core(self, value):
        return lax.ppermute(self.begun(value), "tp", [(0, 1), (1, 0)])

    def ring_at(self, back):
        return (self.at + (RING - back)) & (RING - 1)

    def lane_at(self, turn):
        return lax.rem(self.lane + (self.width - turn), self.width) if turn else self.lane

    def place(self, back, turn):
        return self.ring_at(back) * self.width + self.lane_at(turn)

    def block_places(self):
        n = lax.iota(jnp.int32, RING * self.width * 2)
        back = lax.div(n, 2 * self.width)
        turn = lax.rem(lax.div(n, 2), self.width)
        ring = (self.at + RING - back) & (RING - 1)
        lane = lax.rem(self.lane + self.width - turn, self.width)
        return (ring * self.width + lane) * 2 + (self.half ^ (n & 1))

    def all_lanes(self, value):
        values = [value]
        while len(values) < self.width:
            values.append(self.lanes(values[-1]))
        return values

    def sum_lanes(self, terms):
        total, *rest = terms
        for term in rest:
            total = (self.lanes(total).astype(F32) + term.astype(F32)).astype(BF16)
        return self.lanes(total)

    def both_cores(self, own):
        other = self.over_core(own)
        first = jnp.where(self.core == 0, own, other)
        second = jnp.where(self.core == 0, other, own)
        return jnp.concatenate([first, second], axis=0)

    def swap_halves(self, total):
        keep = lax.dynamic_index_in_dim(total, self.half, 0, keepdims=False)
        send = lax.dynamic_index_in_dim(total, 1 - self.half, 0, keepdims=False)
        return keep, self.over_half(send.astype(BF16)).astype(F32)

    def side_by_side(self, keep, recv):
        return jnp.concatenate(
            [jnp.where(self.half == 0, keep, recv), jnp.where(self.half == 0, recv, keep)], axis=-1
        )


def slot(values, count, index):
    size = values.shape[1] // count
    return lax.dynamic_slice_in_dim(values, index * size, size, 1)


def in_order(values, index):
    count = len(values)
    ahead = jnp.concatenate(values[::-1], axis=1)
    size = ahead.shape[1]
    first = lax.rem(2 * count - 1 - index, count)
    twice = jnp.concatenate([ahead, ahead], axis=1)
    return lax.dynamic_slice_in_dim(twice, first * (size // count), size, 1)


def on_device(
    mesh,
    inputs,
    conditioning,
    query_matrix,
    key_matrix,
    value_matrix,
    output_matrix,
    cross_query,
    cross_key,
    cross_value,
    cross_output,
    gate_matrix,
    up_matrix,
    down_matrix,
    first_gain,
    second_gain,
    third_gain,
    cotangent,
):
    links = Links(mesh)
    ring, lanes, all_lanes = links.ring, links.lanes, links.all_lanes
    over_half, over_core = links.over_half, links.over_core
    sync = links.sync
    core, half, lane_count = links.core, links.half, links.width
    rows = inputs.shape[1]
    own_rows = rows // 2
    width = inputs.shape[2]
    shard = query_matrix.shape[0]
    cols = query_matrix.shape[1] // 2
    pairs = cols // PAIR
    context_shard = cross_key.shape[0]
    context_width = conditioning.shape[2]
    context_count = conditioning.shape[1]
    hidden = gate_matrix.shape[1] // RING
    blocks = links.fsdp * 2
    places = links.block_places()

    def half_cols(values, index):
        return lax.dynamic_slice_in_dim(values, index * cols, cols, 1)

    def early_part(index):
        parts = [half_cols(w, index) for w in (query_matrix, key_matrix, value_matrix)]
        return jnp.concatenate(
            [p[:, n * PAIR : (n + 1) * PAIR] for n in range(pairs) for p in parts]
            + [half_cols(output_matrix.T, index)],
            axis=1,
        )

    def late_part(index):
        return jnp.concatenate(
            [
                half_cols(w, index)
                for w in (cross_query, cross_output.T, cross_key, cross_value)
            ],
            axis=0,
        )

    def feed_part(index):
        return jnp.concatenate(
            [
                lax.dynamic_slice_in_dim(w, index * hidden, hidden, 1)
                for w in (gate_matrix, up_matrix, down_matrix.T)
            ],
            axis=1,
        )

    def halves_of(left, weights):
        pair = 2 * own_rows
        return mm_nt(left[:pair], weights), mm_nt(left[pair:], weights).astype(BF16)

    def for_half(mine, recv):
        return (mine[own_rows:] + recv[own_rows:].astype(F32)).astype(BF16)

    def spread_cores(own, over):
        pair = jnp.concatenate([own, over], axis=0)
        return jnp.concatenate([pair, over_core(pair)], axis=0)

    own = lax.dynamic_slice_in_dim(inputs[0], core * own_rows, own_rows, 0)
    other = lax.dynamic_slice_in_dim(inputs[0], (1 - core) * own_rows, own_rows, 0)
    upstream = lax.dynamic_slice_in_dim(cotangent[0], core * own_rows, own_rows, 0)
    row = lax.iota(jnp.int32, own_rows)
    position = jnp.concatenate(
        [
            row + (half ^ there) * rows + (core ^ beside) * own_rows
            for beside in (0, 1)
            for there in (0, 1)
        ]
    )
    mark = lax.broadcasted_iota(jnp.int32, (16, width), 1)
    place = (lax.axis_index("fsdp") * 2 + half) * shard
    gains = jnp.pad(jnp.stack([first_gain, second_gain, third_gain]), ((0, 13), (0, 0)))
    gains = jnp.where(
        (mark >= place) & (mark < place + shard), jnp.tile(gains, (1, blocks)), jnp.zeros((), BF16)
    )
    early_send, early_keep = pack_early(
        query_matrix, key_matrix, value_matrix, output_matrix.T, gains, half, cols
    )
    early_recv, cotangent1 = over_half(early_send), ring(upstream, 1)
    early_keep, early_recv, gains = sync(early_keep, early_recv, gains)

    early0 = jnp.concatenate([early_keep, early_recv[:shard], gains + early_recv[shard:]], axis=0)
    early1, lanes0, own_over = ring(early0, 1), all_lanes(early0), over_half(own)
    early1, lanes0, own_over, late_send, late_keep, cotangent1 = sync(
        early1, lanes0, own_over, late_part(1 - half), late_part(half), cotangent1
    )

    early3, lanes1, late_recv = ring(lanes0[0], -1), all_lanes(early1), over_half(late_send)
    other_over = over_core(own_over)
    early3, lanes1, late_recv, other_over, tables, feed0, feed_send = sync(
        early3,
        lanes1,
        late_recv,
        other_over,
        rotary_tables(position),
        feed_part(links.at),
        feed_part(links.ring_at(RING - 1)),
    )

    early2, lanes3, feed0_over = ring(lanes1[0], 1), all_lanes(early3), over_half(feed0)
    late0 = jnp.concatenate([late_keep, late_recv], axis=0)
    early2, lanes3, feed0_over, late0, feed0, feed_sends = sync(
        early2,
        lanes3,
        feed0_over,
        late0,
        feed0,
        [feed_part(links.ring_at(back)) for back in (1, 2)],
    )

    late1, lanes2 = ring(late0, 1), all_lanes(early2)
    context = jnp.pad(conditioning[0], ((0, -context_count % 128), (0, 0)))
    late1, lanes2, context, late_both = sync(
        late1, lanes2, context, jnp.concatenate([late0, late1], axis=0)
    )

    feed1, late2, late3 = ring(feed_send, 1), ring(late1, 1), ring(late0, -1)
    late_lanes01, feed0_lanes = all_lanes(late_both), all_lanes(feed0)
    (
        qkv_low, self_low, self_logsum, partial, send, gains, qkv_full, output_full, normed_one,
    ) = self_forward(
        lanes0 + lanes1 + lanes2 + lanes3, places, (own, own_over, other, other_over), tables, shard
    )
    first_norm_gain, second_norm_gain, third_norm_gain = gains[0:1], gains[1:2], gains[2:3]
    partial, send, feed1, late_lanes01, feed0_lanes, late_both = sync(
        partial, send, feed1, late_lanes01, feed0_lanes, jnp.concatenate([late2, late3], axis=0)
    )

    recv = over_core(send)
    far_term = over_half((partial + recv.astype(F32)).astype(BF16))
    feed2, feed3, late_lanes23 = (
        ring(feed_sends[1], 2),
        ring(feed_sends[0], -1),
        all_lanes(late_both),
    )
    far_term, late_lanes23, feed2, cotangents, x_send, y_send = sync(
        far_term,
        late_lanes23,
        feed2,
        jnp.concatenate([upstream, cotangent1], axis=0),
        jnp.concatenate([feed0_over, feed1], axis=0),
        jnp.concatenate([feed1, feed3], axis=0),
    )
    hidden_one, normed = pair_forward(second_norm_gain, own, own_over, partial, recv, far_term)

    cotangent3, x_recv, y_recv = ring(upstream, -1), all_lanes(x_send), over_half(y_send)
    late_rows = 2 * (shard + context_shard)
    plan = []
    for n in range(blocks):
        first = (n % 2) * 2 * (shard + context_shard)
        for out in range(2):
            plan.append((n // 2, n, first + out * shard, shard, 0, cols, out, 0))
        for out in range(2):
            start = first + 2 * shard + out * context_shard
            plan.append((n // 2, n, start, context_shard, 0, cols, 2, out * cols))
    cross_query_full, cross_output_full, context_full = place_pieces(
        [part[: 2 * late_rows] for part in late_lanes01]
        + [part[2 * late_rows :] for part in late_lanes01]
        + [part[: 2 * late_rows] for part in late_lanes23]
        + [part[2 * late_rows :] for part in late_lanes23],
        plan,
        places,
        [(width, cols)] * 2 + [(context_width, 2 * cols)],
    )
    context_low = mm(context, context_full).astype(BF16)
    normed_two = jnp.concatenate([normed, over_core(normed)], axis=0)
    cross_query_low = mm(normed_two, cross_query_full).astype(BF16) * jnp.asarray(SCALE, BF16)
    cross_low, cross_logsum = cross_forward(cross_query_low, context_low, context_count)
    partial, send = halves_of(cross_low, cross_output_full)
    cotangents_core = over_core(cotangents)
    partial, send, cotangent3, x_recv, y_recv, cotangents_core = sync(
        partial, send, cotangent3, x_recv, y_recv, cotangents_core
    )
    feed0_over_lanes = [part[:shard] for part in x_recv]
    feed1_lanes = [part[shard:] for part in x_recv]
    feed1_over, feed3_over, feed3 = y_recv[:shard], y_recv[shard:], y_send[shard:]

    recv = over_core(send)
    far_term, cotangent2, feed3_lanes = over_half(for_half(partial, recv)), ring(cotangent1, 1), all_lanes(feed3)
    far_term, cotangent2, feed3_lanes, x_send, y_send = sync(
        far_term,
        cotangent2,
        feed3_lanes,
        jnp.concatenate([feed1_over, feed2], axis=0),
        jnp.concatenate([feed2, *feed3_lanes[1:]], axis=0),
    )

    hidden_two, normed0 = norm_forward(
        own_rows, hidden_one, third_norm_gain, partial, recv, far_term
    )
    normed1, normed3 = ring(normed0, 1), ring(normed0, -1)
    x_recv, y_recv = all_lanes(x_send), over_half(y_send)
    core0 = over_core(jnp.concatenate([cotangent3, cotangent2, normed0], axis=0))
    normed1, normed3, x_recv, y_recv, core0 = sync(normed1, normed3, x_recv, y_recv, core0)
    feed1_over_lanes = [part[:shard] for part in x_recv]
    feed2_lanes = [part[shard:] for part in x_recv]
    feed2_over = y_recv[:shard]
    feed3_lanes_over = [feed3_over] + [
        y_recv[shard * n : shard * (n + 1)] for n in range(1, lane_count)
    ]

    normed2 = ring(normed1, 1)
    feed2_lanes_over = [feed2_over] + [over_half(value) for value in feed2_lanes[1:]]
    core1 = over_core(jnp.concatenate([normed1, normed3], axis=0))
    normed2, feed2_lanes_over, core1 = sync(normed2, feed2_lanes_over, core1)

    core2 = over_core(normed2)
    pieces = [
        piece
        for lanes_pieces, over_pieces in (
            (feed0_lanes, feed0_over_lanes),
            (feed1_lanes, feed1_over_lanes),
            (feed2_lanes, feed2_lanes_over),
            (feed3_lanes, feed3_lanes_over),
        )
        for piece in [part for both in zip(lanes_pieces, over_pieces) for part in both]
    ]
    held = [
        core0, core1, core2, normed0, normed1, normed3, normed2,
        cotangents_core, cotangents, cotangent3, cotangent2,
    ]
    feed_low, both_low, send, mine, normed_three, upstream_all, down_full = feed_forward(
        pieces,
        places,
        held,
        [(0, 2), (1, 0), (1, 1), (2, 0), (3, 0), (4, 0), (5, 0), (6, 0)],
        [(7, 0), (7, 1), (0, 0), (0, 1), (8, 0), (8, 1), (9, 0), (10, 0)],
        shard,
        own_rows,
    )
    feed_low, both_low, send, mine, normed_three, upstream_all, down_full = sync(
        feed_low, both_low, send, mine, normed_three, upstream_all, down_full
    )

    def ring_halves(left, weights):
        count = RING * own_rows
        return mm_nt(left[count:], weights), mm_nt(left[:count], weights).astype(BF16)

    def block_of(mine, recv, back):
        spot = (0, 1, 3, 2)[back]
        part = slice(spot * own_rows, (spot + 1) * own_rows)
        return mine[part] + recv[part].astype(F32)

    def lanes_block(grads, turn):
        place = links.lane_at(turn)
        return jnp.concatenate(
            [
                lax.dynamic_slice_in_dim(grads, (z * lane_count + place) * 2 * shard, 2 * shard, 0)
                for z in (0, 1)
            ],
            axis=0,
        )

    def halves_block(grads, index):
        return jnp.concatenate(
            [
                lax.dynamic_slice_in_dim(
                    grads, ((z * lane_count + n) * 2 + index) * shard, shard, 0
                )
                for z in (2, 3)
                for n in range(lane_count)
            ],
            axis=0,
        )

    def lanes_terms(grads):
        return [lanes_block(grads, turn) for turn in range(1, lane_count)]

    def lanes_second(grads, recv):
        total = (lanes_block(grads, 0).astype(F32) + recv.astype(F32)).reshape(2, 2, shard, -1)
        keep = lax.dynamic_index_in_dim(total, half, 1, keepdims=False)
        send = lax.dynamic_index_in_dim(total, 1 - half, 1, keepdims=False)
        return keep, send.astype(BF16)

    def halves_second(grads, recv):
        total = (halves_block(grads, half).astype(F32) + recv.astype(F32)).reshape(
            2, lane_count, shard, -1
        )
        keep, *send = [
            lax.dynamic_index_in_dim(total, links.lane_at(turn), 1, keepdims=False)
            for turn in range(lane_count)
        ]
        return keep, [term.astype(BF16) for term in send]

    def joined(*terms):
        keep, recv, keep_late, recv_late = terms
        return jnp.concatenate(
            [
                (keep + recv.astype(F32)).astype(BF16),
                (keep_late + recv_late.astype(F32)).astype(BF16),
            ],
            axis=0,
        )

    recv = over_core(send)
    down_grad = mm_tn(upstream_all, feed_low).astype(BF16)
    recv, mine, both_low, normed_three, feed_low, down_grad = sync(
        recv, mine, both_low, normed_three, feed_low, down_grad
    )
    mine, recv, both_low, normed_three, down_grad, down_lanes, down_halves, ring_low = sync(
        mine,
        recv,
        both_low,
        normed_three,
        down_grad,
        lanes_terms(down_grad),
        halves_block(down_grad, 1 - half),
        block_of(mine, recv, 2).astype(BF16),
    )

    two = ring(ring_low, -1)
    down_lanes, down_halves = links.sum_lanes(down_lanes), over_half(down_halves)
    both_grad = mm_tn(normed_three, both_low).astype(BF16)
    out_mine, out_send = ring_halves(feed_low, down_full)
    two, both_grad, down_lanes, down_halves, out_mine, out_send, three = sync(
        two,
        both_grad,
        down_lanes,
        down_halves,
        out_mine,
        out_send,
        block_of(mine, recv, 3).astype(BF16),
    )

    three = ring(three, 1)
    one = ring((block_of(mine, recv, 1) + two.astype(F32)).astype(BF16), -1)
    both_lanes = links.sum_lanes(lanes_terms(both_grad))
    both_halves = over_half(halves_block(both_grad, 1 - half))
    out_recv = over_core(out_send)
    down_keep, down_move = lanes_second(down_grad, down_lanes)
    down_late_keep, down_late_move = halves_second(down_grad, down_halves)
    one, three, both_lanes, both_halves, out_recv, out_low, downs = sync(
        one,
        three,
        both_lanes,
        both_halves,
        out_recv,
        [block_of(out_mine, out_recv, back).astype(BF16) for back in (2, 3)],
        (down_keep, down_move, down_late_keep, down_late_move),
    )
    down_keep, down_move, down_late_keep, down_late_move = downs

    hidden_two_grad, low, third_gain_grad = norm_backward(
        hidden_two, third_norm_gain, upstream, mine, recv, one, three
    )
    low_over = over_half(low)
    out_two = ring(out_low[0], -1)
    both_keep, both_move = lanes_second(both_grad, both_lanes)
    both_late_keep, both_late_move = halves_second(both_grad, both_halves)
    low_over, low, out_two, both_keep, both_late_keep, x_send, y_send, out_one = sync(
        low_over,
        low,
        out_two,
        both_keep,
        both_late_keep,
        [jnp.concatenate(pair, axis=-1) for pair in zip(down_late_move, both_late_move)],
        jnp.concatenate([down_move, both_move], axis=-1),
        (block_of(out_mine, out_recv, 1) + out_two.astype(F32)).astype(BF16),
    )

    moved, late_sum, out_three, out_one = (
        over_half(y_send),
        links.sum_lanes(x_send),
        ring(out_low[1], 1),
        ring(out_one, -1),
    )
    branch_two = spread_cores(low, low_over)
    cross_out_grad = mm(branch_two, cross_output_full).astype(BF16)
    cross_query_round, cross_key_back, cross_value_back = cross_backward(
        cross_query_low, context_low, cross_low, cross_out_grad, cross_logsum, context_count
    )
    partial, send = halves_of(cross_query_round, cross_query_full)
    partial, send, moved, late_sum, out_three, out_one, branch_two = sync(
        partial, send, moved, late_sum, out_three, out_one, branch_two
    )
    recv = over_core(send)
    feed_mine = jnp.concatenate(
        [
            joined(down_keep, moved[..., :hidden], down_late_keep, late_sum[..., :hidden]),
            joined(both_keep, moved[..., hidden:], both_late_keep, late_sum[..., hidden:]),
        ],
        axis=2,
    )
    ring_places = jnp.stack(
        [links.place(back, turn) for back in range(RING) for turn in range(lane_count)]
    )

    def by_back(blocks):
        rows = [blocks[back * lane_count : (back + 1) * lane_count] for back in range(RING)]
        return [row[0] for row in rows], [row[1:] for row in rows]

    def below(others, backs):
        return [jnp.concatenate(parts, axis=0) for parts in zip(*[others[back] for back in backs])]

    cross_grads = [
        mm_tn(branch_two, cross_low).astype(BF16),
        mm_tn(normed_two, cross_query_round).astype(BF16),
        mm_tn(context, cross_key_back).astype(BF16),
        mm_tn(context, cross_value_back).astype(BF16),
    ]
    cross_own, cross_other = by_back(split_blocks(cross_grads, ring_places, True))
    recv, feed_mine, feed_send, cross_own, cross_late, cross_most, backs = sync(
        recv,
        feed_mine,
        [
            lax.dynamic_index_in_dim(feed_mine, links.ring_at(back), 0, keepdims=False)
            for back in (1, 2, 3)
        ],
        cross_own,
        below(cross_other, (0, 1)),
        below(cross_other, (2, 3)),
        (cross_key_back, cross_value_back),
    )
    cross_key_back, cross_value_back = backs

    def out_of(values, back):
        return lax.dynamic_index_in_dim(values, links.ring_at(back), 0, keepdims=False)

    far_term = over_half((partial + recv.astype(F32)).astype(BF16))
    feed1_sum, feed3_sum = ring(feed_send[2], 1), ring(feed_send[0], -1)
    cross_most = links.sum_lanes(cross_most)
    block_rows = cross_most.shape[0] // 2
    far_term, feed1_sum, feed3_sum, cross_two, cross_three, cross_late = sync(
        far_term,
        feed1_sum,
        feed3_sum,
        (cross_own[2].astype(F32) + cross_most[:block_rows].astype(F32)).astype(BF16),
        (cross_own[3].astype(F32) + cross_most[block_rows:].astype(F32)).astype(BF16),
        cross_late,
    )
    hidden_one_grad, low, second_gain_grad = pair_backward(
        second_norm_gain, hidden_one, hidden_two_grad, low_over, partial, recv, far_term
    )

    feed2_sum, cross_two = ring(feed_send[1], 2), ring(cross_two, -1)
    cross_late = links.sum_lanes(cross_late)
    branch_one = jnp.concatenate([low, over_core(low)], axis=0)
    self_out_grad = mm(branch_one, output_full).astype(BF16)
    qkv_round = self_backward(qkv_low, self_low, self_out_grad, self_logsum, tables)
    partial, send = halves_of(qkv_round, qkv_full)
    partial, send, feed2_sum, cross_late, cross_two, qkv_round, branch_one = sync(
        partial, send, feed2_sum, cross_late, cross_two, qkv_round, branch_one
    )
    output_grad = mm_tn(branch_one, self_low).astype(BF16)
    qkv_grad = mm_tn(normed_one, qkv_round).astype(BF16)
    self_own, self_other = by_back(split_blocks([output_grad, qkv_grad], ring_places, False))
    cross_zero = cross_own[0].astype(F32) + cross_late[:block_rows].astype(F32)
    cross_one = cross_own[1].astype(F32) + cross_late[block_rows:].astype(F32)
    recv, self_own, self_other, cross_zero, cross_one, backs = sync(
        over_core(send),
        self_own,
        self_other,
        cross_zero,
        (cross_one + cross_two.astype(F32)).astype(BF16),
        (cross_key_back, cross_value_back),
    )
    cross_key_back, cross_value_back = backs

    far_term = over_half(for_half(partial, recv))
    cross_one, cross_three = ring(cross_one, -1), ring(cross_three, 1)
    self2 = links.sum_lanes(self_other[2])
    context_term = (
        mm_nt(cross_key_back, context_full[:, :cols])
        + mm_nt(cross_value_back, context_full[:, cols:])
    )[:context_count]
    context_recv = over_core(context_term.astype(BF16))
    far_term, cross_one, cross_three, self2, context_term, context_recv, self_two = sync(
        far_term,
        cross_one,
        cross_three,
        self2,
        context_term,
        context_recv,
        (self_own[2].astype(F32) + self2.astype(F32)).astype(BF16),
    )

    self3 = links.sum_lanes(self_other[3])
    self_two = ring(self_two, -1)
    context_low_sum = (context_term + context_recv.astype(F32)).astype(BF16)
    context_over = over_half(context_low_sum)
    inputs_grad, _, first_gain_grad = norm_backward(
        own, first_norm_gain, hidden_one_grad, partial, recv, far_term
    )
    layer_result = links.both_cores(
        hidden_two + block_of(out_mine, out_recv, 0) + out_one.astype(F32) + out_three.astype(F32)
    )
    gain_grads = jnp.concatenate([first_gain_grad, second_gain_grad, third_gain_grad], axis=0)
    gate_sum, up_sum, down_sum = spread(
        [out_of(feed_mine, 0), feed1_sum, feed2_sum, feed3_sum],
        jnp.stack([links.ring_at(back) for back in range(RING)]),
    )
    cross_total = cross_zero + cross_one.astype(F32) + cross_three.astype(F32)
    sizes = (shard, shard, context_shard, context_shard)
    starts = [2 * sum(sizes[:n]) for n in range(4)]
    cross_total = jnp.concatenate(
        [
            cross_total[start : start + 2 * size].reshape(2, size, cols)
            for start, size in zip(starts, sizes)
        ],
        axis=1,
    )
    context_grad = context_low_sum.astype(F32) + context_over.astype(F32)
    self3, self_two, context_grad, layer_result, gain_grads, inputs_grad, feed_sums, cross_total, self_three = sync(
        self3,
        self_two,
        context_grad,
        layer_result,
        gain_grads,
        inputs_grad,
        (gate_sum, up_sum, down_sum),
        cross_total,
        (self_own[3].astype(F32) + self3.astype(F32)).astype(BF16),
    )
    gate_sum, up_sum, down_sum = feed_sums

    self1 = links.sum_lanes(self_other[1])
    self_three = ring(self_three, 1)
    gain_grads = gain_grads + over_core(gain_grads)
    gain_grads = gain_grads + over_half(gain_grads)
    cross_keep, cross_recv = links.swap_halves(cross_total)
    self1, self_three, gain_grads, cross_recv, self_one = sync(
        self1,
        self_three,
        gain_grads,
        cross_recv,
        (self_own[1].astype(F32) + self1.astype(F32) + self_two.astype(F32)).astype(BF16),
    )

    self0 = links.sum_lanes(self_other[0])
    self_one = ring(self_one, -1)
    gain_ring = [slot(gain_grads, RING, links.ring_at(back)) for back in range(RING)]
    gain_two, gain_three = ring(gain_ring[2], -1), ring(gain_ring[3], 1)
    inputs_result = links.both_cores(inputs_grad)
    cross_sums = links.side_by_side(cross_keep, cross_recv)
    self0, self_one, gain_two, gain_three, inputs_result, cross_sums = sync(
        self0, self_one, gain_two, gain_three, inputs_result, cross_sums
    )
    gain_one = ring(gain_ring[1] + gain_two, -1)

    self_total = (
        self_own[0].astype(F32) + self0.astype(F32) + self_one.astype(F32) + self_three.astype(F32)
    )
    keep, recv = links.swap_halves(self_total.reshape(2, shard, 4 * cols))
    gain_grads = gain_ring[0] + gain_one + gain_three
    gain_total = slot(gain_grads, lane_count, links.lane_at(1))
    for turn in list(range(2, lane_count)) + [0]:
        gain_total = links.lanes(gain_total) + slot(gain_grads, lane_count, links.lane_at(turn))
    gain_sums = slot(gain_total, 2, half)

    def of_self(values, n):
        if n == 3:
            return values[:, :cols]
        return jnp.concatenate(
            [
                values[:, cols + (3 * pair + n) * PAIR : cols + (3 * pair + n + 1) * PAIR]
                for pair in range(pairs)
            ],
            axis=1,
        )

    query_sum, key_sum, value_sum, output_sum = (
        links.side_by_side(of_self(keep, n), of_self(recv, n)) for n in range(4)
    )
    return (
        layer_result[None],
        inputs_result[None],
        context_grad[None],
        query_sum,
        key_sum,
        value_sum,
        output_sum.T,
        cross_sums[shard : 2 * shard],
        cross_sums[2 * shard : 2 * shard + context_shard],
        cross_sums[2 * shard + context_shard :],
        cross_sums[:shard].T,
        gate_sum,
        up_sum,
        down_sum.T,
        gain_sums[0],
        gain_sums[1],
        gain_sums[2],
    )


def solution(mesh):
    row = P(("fsdp", "ctx"), "tp")
    col = P("tp", ("fsdp", "ctx"))
    gain = P(("fsdp", "ctx"))
    token = P("fsdp", "ctx", None)
    context = P("fsdp", None, None)
    weights = (row, row, row, col, row, row, row, col, row, row, col, gain, gain, gain)
    return jax.shard_map(
        functools.partial(on_device, mesh),
        mesh=mesh,
        in_specs=(token, context) + weights + (token,),
        out_specs=(token, token, context) + weights,
        check_vma=False,
    )
```

```python
import functools
import math

import jax
import jax.numpy as jnp
from jax import lax
from jax.experimental import pallas as pl
from jax.experimental.pallas import tpu as pltpu
from jax.sharding import PartitionSpec as P

HDIM = 64
EPSILON = 1e-05
F32 = jnp.float32
BF16 = jnp.bfloat16
SCALE = HDIM ** (-0.5)
PAIR = 2 * HDIM
VMEM_LIMIT = 48 * 1024 * 1024
VMEM_MOST = 60 * 1024 * 1024


def mm(left, right):
    return lax.dot_general(left, right, (((1,), (0,)), ((), ())), preferred_element_type=F32)


def mm_tn(left, right):
    return lax.dot_general(left, right, (((0,), (0,)), ((), ())), preferred_element_type=F32)


def mm_nt(left, right):
    return lax.dot_general(left, right, (((1,), (1,)), ((), ())), preferred_element_type=F32)


def norm_stats(values):
    center = values - jnp.mean(values, axis=-1, keepdims=True)
    rate = lax.rsqrt(jnp.mean(center * center, axis=-1, keepdims=True) + EPSILON)
    return center * rate, rate


def params(limit=VMEM_LIMIT):
    return pltpu.CompilerParams(vmem_limit_bytes=limit)


def norm_call(kernel, rows, outs, *operands):
    width = operands[0].shape[1]

    def block(count):
        return pl.BlockSpec((count, width), lambda step: (0, 0))

    return pl.pallas_call(
        kernel,
        grid=(1,),
        in_specs=[block(min(rows, operand.shape[0])) for operand in operands],
        out_specs=[block(count) for count, _ in outs],
        out_shape=[jax.ShapeDtypeStruct((count, width), kind) for count, kind in outs],
        compiler_params=params(),
    )(*operands)


def norm_forward_kernel(gain_ref, base_ref, *refs):
    *terms, x_ref, n_ref = refs
    values = base_ref[...].astype(F32)
    for term in terms:
        values = values + term[...].astype(F32)
    x_ref[...] = values
    n_ref[...] = (norm_stats(values)[0] * gain_ref[...]).astype(BF16)


def norm_forward(rows, base, gain, *terms):
    return norm_call(norm_forward_kernel, rows, ((rows, F32), (rows, BF16)), gain, base, *terms)


def pair_forward_kernel(gain_ref, own_ref, over_ref, near_ref, core_ref, far_ref, x_ref, n_ref):
    terms = near_ref[...] + core_ref[...].astype(F32) + far_ref[...].astype(F32)
    base = jnp.where(pl.program_id(0) == 0, own_ref[...].astype(F32), over_ref[...].astype(F32))
    values = base + terms
    x_ref[...] = values
    n_ref[...] = (norm_stats(values)[0] * gain_ref[...]).astype(BF16)


def pair_blocks(rows, width):
    return (
        pl.BlockSpec((rows, width), lambda step: (step, 0)),
        pl.BlockSpec((rows, width), lambda step: (1 - step, 0)),
        pl.BlockSpec((rows, width), lambda step: (0, 0)),
        pl.BlockSpec((1, width), lambda step: (0, 0)),
    )


def pair_forward(gain, own, over, near, core, far):
    rows, width = near.shape
    here, there, fixed, line = pair_blocks(rows // 2, width)
    return pl.pallas_call(
        pair_forward_kernel,
        grid=(2,),
        in_specs=[line, fixed, fixed, here, here, there],
        out_specs=[here, here],
        out_shape=(
            jax.ShapeDtypeStruct((rows, width), F32),
            jax.ShapeDtypeStruct((rows, width), BF16),
        ),
        compiler_params=params(),
    )(gain, own, over, near, core, far)


def pair_backward_kernel(
    gain_ref, x_ref, skip_ref, over_ref, near_ref, core_ref, far_ref, dx_ref, low_ref, dg_ref
):
    upstream = near_ref[...] + core_ref[...].astype(F32) + far_ref[...].astype(F32)
    unit, rate = norm_stats(x_ref[...])
    scaled = upstream * gain_ref[...]
    back = rate * (
        scaled
        - jnp.mean(scaled, axis=-1, keepdims=True)
        - unit * jnp.mean(scaled * unit, axis=-1, keepdims=True)
    )
    first = pl.program_id(0) == 0
    total = jnp.where(first, skip_ref[...], over_ref[...].astype(F32)) + back
    low_ref[...] = total.astype(BF16)

    @pl.when(first)
    def _():
        dx_ref[...] = total
        dg_ref[...] = jnp.sum(upstream * unit, axis=0, keepdims=True)


def pair_backward(gain, values, skip, over, near, core, far):
    rows, width = values.shape
    here, there, fixed, line = pair_blocks(rows // 2, width)
    return pl.pallas_call(
        pair_backward_kernel,
        grid=(2,),
        in_specs=[line, here, fixed, fixed, here, here, there],
        out_specs=[fixed, here, line],
        out_shape=(
            jax.ShapeDtypeStruct((rows // 2, width), F32),
            jax.ShapeDtypeStruct((rows, width), BF16),
            jax.ShapeDtypeStruct((1, width), F32),
        ),
        compiler_params=params(),
    )(gain, values, skip, over, near, core, far)


def norm_backward_kernel(gain_ref, x_ref, skip_ref, *refs):
    *terms, dx_ref, low_ref, dg_ref = refs
    upstream = terms[0][...].astype(F32)
    for term in terms[1:]:
        upstream = upstream + term[...].astype(F32)
    unit, rate = norm_stats(x_ref[...].astype(F32))
    scaled = upstream * gain_ref[...]
    back = rate * (
        scaled
        - jnp.mean(scaled, axis=-1, keepdims=True)
        - unit * jnp.mean(scaled * unit, axis=-1, keepdims=True)
    )
    total = skip_ref[...].astype(F32) + back
    dx_ref[...] = total
    low_ref[...] = total.astype(BF16)
    dg_ref[...] = jnp.sum(upstream * unit, axis=0, keepdims=True)


def norm_backward(values, gain, skip, *terms):
    rows = values.shape[0]
    outs = (rows, F32), (rows, BF16), (1, F32)
    return norm_call(norm_backward_kernel, rows, outs, gain, values, skip, *terms)


def turned(values, cosine, upper, lower):
    width = values.shape[1]
    return (
        values * cosine
        + pltpu.roll(values, width - HDIM // 4, 1) * upper
        + pltpu.roll(values, HDIM // 4, 1) * lower
    )


def chunk_of(rows):
    return 128 if rows % 128 == 0 else rows


def low_half(shape):
    return lax.broadcasted_iota(jnp.int32, shape, len(shape) - 1) < HDIM


def of_head(values, head):
    first = low_half(values.shape)
    keep = first if head == 0 else jnp.logical_not(first)
    return jnp.where(keep, values, jnp.zeros((), values.dtype))


def forward_heads(q_ref, k_ref, v_ref, o_ref, lse_ref, valid):
    rows = q_ref.shape[0]
    step = chunk_of(rows)
    key, value = k_ref[...], v_ref[...]
    first_half = low_half(value.shape)
    ones = jnp.ones((), BF16)
    extended = jnp.where(first_half, value, ones), jnp.where(first_half, ones, value)
    for first in range(0, rows, step):
        part = slice(first, first + step)
        query = q_ref[part, :]
        results = []
        for head in range(2):
            scores = mm_nt(of_head(query, head), key)
            if valid < key.shape[0]:
                column = lax.broadcasted_iota(jnp.int32, scores.shape, 1)
                scores = jnp.where(column < valid, scores, -1e30)
            peak = jnp.max(scores, axis=-1, keepdims=True)
            mixed = mm(jnp.exp(scores - peak).astype(BF16), extended[head])
            total = pltpu.roll(mixed, HDIM, 1)
            results.append((mixed * (1.0 / total), peak + jnp.log(total)))
        lanes = low_half((step, PAIR))
        o_ref[part, :] = jnp.where(lanes, results[0][0], results[1][0]).astype(BF16)
        lse_ref[part, :] = jnp.where(lanes, results[0][1], results[1][1])


def thirds(ref):
    return ref.at[:, :PAIR], ref.at[:, PAIR : 2 * PAIR], ref.at[:, 2 * PAIR :]


def self_forward_kernel(shard, place_ref, *refs):
    n_pieces = len(refs) - 23
    pieces, refs = refs[:n_pieces], refs[n_pieces:]
    parts, refs = refs[:4], refs[4:]
    cos_ref, up_ref, low_ref, *refs = refs
    turned_ref, o_ref, lse_ref, mine_ref, send_ref, gain_ref, *refs = refs
    qkv_out, output_out, normed_out, *refs = refs
    qkv_all, output_all, normed_all, gain_all, o_all = refs[:-2]
    sems, out_sems = refs[-2:]
    pair, cols = pl.program_id(0), qkv_all.shape[1]
    gain_rows = gain_all.shape[0] // n_pieces

    @pl.when(pair == 0)
    def _():
        copies = []
        for n, piece in enumerate(pieces):
            mark = pl.ds(n * gain_rows, gain_rows)
            copies.append((piece.at[pl.ds(2 * shard, gain_rows), pl.ds(0, gain_all.shape[1])], gain_all.at[mark, :]))
        for n, piece in enumerate(pieces):
            for there in (0, 1):
                row = pl.ds(pl.multiple_of(place_ref[2 * n + there] * shard, shard), shard)
                lines = pl.ds(there * shard, shard)
                copies.append((piece.at[lines, pl.ds(0, cols)], qkv_all.at[row, :]))
                copies.append((piece.at[lines, pl.ds(cols, output_all.shape[1])], output_all.at[row, :]))
        copies = [
            pltpu.make_async_copy(source, target, sems.at[n])
            for n, (source, target) in enumerate(copies)
        ]
        for copy in copies:
            copy.start()
        for copy in copies[:n_pieces]:
            copy.wait()
        gains = jnp.zeros((gain_rows, gain_all.shape[1]), F32)
        for n in range(n_pieces):
            gains = gains + gain_all[n * gain_rows : (n + 1) * gain_rows, :].astype(F32)
        gain_ref[...] = gains
        first = 0
        for part in parts:
            unit, _ = norm_stats(part[...].astype(F32))
            normed_all[first : first + part.shape[0], :] = (unit * gains[:1]).astype(BF16)
            first += part.shape[0]
        for copy in copies[n_pieces:]:
            copy.wait()

    exports = [
        pltpu.make_async_copy(source, target, out_sems.at[n])
        for n, (source, target) in enumerate(
            ((qkv_all, qkv_out), (output_all, output_out), (normed_all, normed_out))
        )
    ]

    @pl.when(pair == 0)
    def _():
        for export in exports:
            export.start()

    tables = cos_ref[...], up_ref[...], low_ref[...]
    q_ref, k_ref, v_ref = thirds(turned_ref)
    first = pl.multiple_of(pair * 3 * PAIR, PAIR)
    qkv = mm(normed_all[...], qkv_all[:, pl.ds(first, 3 * PAIR)])
    q_ref[...] = turned(qkv[:, :PAIR], *tables).astype(BF16) * jnp.asarray(SCALE, BF16)
    k_ref[...] = turned(qkv[:, PAIR : 2 * PAIR], *tables).astype(BF16)
    v_ref[...] = qkv[:, 2 * PAIR :].astype(BF16)
    forward_heads(q_ref, k_ref, v_ref, o_ref, lse_ref, k_ref.shape[0])
    o_all[:, pl.ds(pl.multiple_of(pair * PAIR, PAIR), PAIR)] = o_ref[...]

    @pl.when(pair == pl.num_programs(0) - 1)
    def _():
        half = o_all.shape[0] // 2
        mine_ref[...] = mm_nt(o_all[:half, :], output_all[...])
        send_ref[...] = mm_nt(o_all[half:, :], output_all[...]).astype(BF16)
        for export in exports:
            export.wait()


def self_forward(pieces, place, parts, tables, shard):
    width, cols = parts[0].shape[1], pieces[0].shape[1] // 4
    rows, pairs = sum(part.shape[0] for part in parts), cols // PAIR
    gain_rows = pieces[0].shape[0] - 2 * shard
    vmem, anywhere = pl.BlockSpec(memory_space=pltpu.VMEM), pl.BlockSpec(memory_space=pl.ANY)

    def paired(width):
        return pl.BlockSpec((rows, width), lambda pair: (0, pair))

    def whole(shape):
        return pl.BlockSpec(shape, lambda pair: (0, 0))

    return pl.pallas_call(
        functools.partial(self_forward_kernel, shard),
        grid=(pairs,),
        in_specs=[pl.BlockSpec(memory_space=pltpu.SMEM)]
        + [anywhere] * len(pieces)
        + [whole(part.shape) for part in parts]
        + [whole((rows, PAIR))] * 3,
        out_specs=[paired(3 * PAIR), paired(PAIR), paired(PAIR)]
        + [whole((rows // 2, width))] * 2
        + [whole((gain_rows, width))]
        + [anywhere] * 3,
        out_shape=[
            jax.ShapeDtypeStruct((rows, 3 * cols), BF16),
            jax.ShapeDtypeStruct((rows, cols), BF16),
            jax.ShapeDtypeStruct((rows, cols), F32),
            jax.ShapeDtypeStruct((rows // 2, width), F32),
            jax.ShapeDtypeStruct((rows // 2, width), BF16),
            jax.ShapeDtypeStruct((gain_rows, width), F32),
            jax.ShapeDtypeStruct((width, 3 * cols), BF16),
            jax.ShapeDtypeStruct((width, cols), BF16),
            jax.ShapeDtypeStruct((rows, width), BF16),
        ],
        scratch_shapes=[
            pltpu.VMEM((width, 3 * cols), BF16),
            pltpu.VMEM((width, cols), BF16),
            pltpu.VMEM((rows, width), BF16),
            pltpu.VMEM((len(pieces) * gain_rows, width), BF16),
            pltpu.VMEM((rows, cols), BF16),
            pltpu.SemaphoreType.DMA((5 * len(pieces),)),
            pltpu.SemaphoreType.DMA((3,)),
        ],
        compiler_params=params(VMEM_MOST),
        cost_estimate=pl.CostEstimate(
            flops=4 * rows * rows * cols + 2 * rows * width * 4 * cols,
            bytes_accessed=8 * width * cols + 2 * rows * width,
            transcendentals=rows * rows * cols // HDIM,
        ),
    )(place, *pieces, *parts, *tables)


def cross_forward_kernel(valid, q_ref, k_ref, v_ref, o_ref, lse_ref):
    forward_heads(q_ref, k_ref, v_ref, o_ref, lse_ref, valid)


def backward_heads(q_ref, k_ref, v_ref, o_ref, do_ref, lse_ref, dq_ref, dk_ref, dv_ref, valid):
    rows = q_ref.shape[0]
    step = chunk_of(rows)
    key, value = k_ref[...], v_ref[...]
    for first in range(0, rows, step):
        part = slice(first, first + step)
        query, grad = q_ref[part, :], do_ref[part, :]
        lse = lse_ref[part, :].T
        delta = (grad.astype(F32) * o_ref[part, :].astype(F32)).T
        query_terms = []
        for head in range(2):
            query_head, grad_head = of_head(query, head), of_head(grad, head)
            lanes = slice(head * HDIM, (head + 1) * HDIM)
            mean_grad = jnp.sum(delta[lanes, :], axis=0, keepdims=True)
            probability = jnp.exp(mm_nt(key, query_head) - lse[head * HDIM : head * HDIM + 1, :])
            if valid < key.shape[0]:
                line = lax.broadcasted_iota(jnp.int32, probability.shape, 0)
                probability = jnp.where(line < valid, probability, 0.0)
            score_grad = (probability * (mm_nt(value, grad_head) - mean_grad)).astype(BF16)
            query_terms.append(mm_tn(score_grad, key))
            key_term = mm(score_grad, query_head)
            value_term = mm(probability.astype(BF16), grad_head)
            if first == 0 and head == 0:
                dk_ref[...] = key_term
                dv_ref[...] = value_term
            else:
                dk_ref[...] += key_term
                dv_ref[...] += value_term
        dq_ref[part, :] = jnp.where(low_half((step, PAIR)), *query_terms) * SCALE


def self_backward_kernel(
    turned_ref, o_ref, do_ref, lse_ref, cos_ref, up_ref, low_ref, out_ref, dq_acc, dk_acc, dv_acc
):
    q_ref, k_ref, v_ref = thirds(turned_ref)
    backward_heads(
        q_ref, k_ref, v_ref, o_ref, do_ref, lse_ref, dq_acc, dk_acc, dv_acc, k_ref.shape[0]
    )
    tables = cos_ref[...], -up_ref[...], -low_ref[...]
    dq_ref, dk_ref, dv_ref = thirds(out_ref)
    dq_ref[...] = turned(dq_acc[...], *tables).astype(BF16)
    dk_ref[...] = turned(dk_acc[...], *tables).astype(BF16)
    dv_ref[...] = dv_acc[...].astype(BF16)


def cross_backward_kernel(
    valid, q_ref, k_ref, v_ref, o_ref, do_ref, lse_ref, dq_ref, dk_ref, dv_ref, dq_acc, dk_acc, dv_acc
):
    some = -(-valid // 16) * 16
    backward_heads(
        q_ref, k_ref.at[:some, :], v_ref.at[:some, :], o_ref, do_ref, lse_ref,
        dq_acc, dk_acc.at[:some, :], dv_acc.at[:some, :], valid,
    )
    dq_ref[...] = dq_acc[...].astype(BF16)
    for ref, acc in ((dk_ref, dk_acc), (dv_ref, dv_acc)):
        ref[:some, :] = acc[:some, :].astype(BF16)
        if some < ref.shape[0]:
            ref[some:, :] = jnp.zeros((ref.shape[0] - some, PAIR), BF16)


def attention_call(kernel, pairs, ins, outs, scratch, flops):
    return pl.pallas_call(
        kernel,
        grid=(pairs,),
        in_specs=[
            pl.BlockSpec((rows, width), functools.partial(lambda place, pair: (0, place(pair)), place))
            for rows, width, place in ins
        ],
        out_specs=[pl.BlockSpec((rows, width), lambda pair: (0, pair)) for rows, width, _ in outs],
        out_shape=[
            jax.ShapeDtypeStruct((rows, width * pairs), kind) for rows, width, kind in outs
        ],
        scratch_shapes=[pltpu.VMEM((rows, PAIR), F32) for rows in scratch],
        compiler_params=params(),
        cost_estimate=pl.CostEstimate(
            flops=flops,
            bytes_accessed=4 * pairs * sum(rows * width for rows, width, _ in ins),
            transcendentals=flops // 256,
        ),
    )


def here(pair):
    return pair


def always(pair):
    return 0


def self_backward(qkv, out, grad, lse, tables):
    rows, pairs = qkv.shape[0], qkv.shape[1] // (3 * PAIR)
    return attention_call(
        self_backward_kernel,
        pairs,
        [(rows, 3 * PAIR, here)] + [(rows, PAIR, here)] * 3 + [(rows, PAIR, always)] * 3,
        [(rows, 3 * PAIR, BF16)],
        (rows,) * 3,
        10 * rows * rows * pairs * PAIR,
    )(qkv, out, grad, lse, *tables)[0]


def cross_forward(query, context, valid):
    rows, pairs, keys = query.shape[0], query.shape[1] // PAIR, context.shape[0]
    return attention_call(
        functools.partial(cross_forward_kernel, valid),
        pairs,
        [(rows, PAIR, here), (keys, PAIR, here), (keys, PAIR, lambda pair: pairs + pair)],
        [(rows, PAIR, BF16), (rows, PAIR, F32)],
        (),
        4 * rows * keys * pairs * PAIR,
    )(query, context, context)


def cross_backward(query, context, out, grad, lse, valid):
    rows, pairs, keys = query.shape[0], query.shape[1] // PAIR, context.shape[0]
    return attention_call(
        functools.partial(cross_backward_kernel, valid),
        pairs,
        [(rows, PAIR, here), (keys, PAIR, here), (keys, PAIR, lambda pair: pairs + pair)]
        + [(rows, PAIR, here)] * 3,
        [(rows, PAIR, BF16), (keys, PAIR, BF16), (keys, PAIR, BF16)],
        (rows, keys, keys),
        10 * rows * keys * pairs * PAIR,
    )(query, context, context, out, grad, lse)


def rotary_tables(position):
    quarter = HDIM // 4
    lane = lax.broadcasted_iota(jnp.int32, (position.shape[0], PAIR), 1) & (HDIM - 1)
    turn = (lane & (quarter - 1)).astype(F32)
    frequency = jnp.exp(-(2.0 * turn / (2 * quarter)) * math.log(10000.0))
    angles = position.astype(F32)[:, None] * frequency
    cosine, sine = jnp.cos(angles), jnp.sin(angles)
    return (
        jnp.where(lane < 2 * quarter, cosine, 1.0),
        jnp.where(lane < quarter, -sine, 0.0),
        jnp.where((lane >= quarter) & (lane < 2 * quarter), sine, 0.0),
    )


def place_kernel(plan, n_pieces, place_ref, *refs):
    pieces, outs = refs[:n_pieces], refs[n_pieces:]
    for piece, spot, src_row, rows, src_col, cols, out, dst_col in plan:
        row = pl.multiple_of(place_ref[spot] * rows, rows)
        outs[out][pl.ds(row, rows), dst_col : dst_col + cols] = pieces[piece][
            src_row : src_row + rows, src_col : src_col + cols
        ]


def place_pieces(pieces, plan, place, outs):
    if any(entry[2] % 16 or entry[3] % 16 for entry in plan):
        whole = [jnp.zeros(out, BF16) for out in outs]
        for piece, spot, src_row, rows, src_col, cols, out, dst_col in plan:
            part = pieces[piece][src_row : src_row + rows, src_col : src_col + cols]
            whole[out] = lax.dynamic_update_slice(whole[out], part, (place[spot] * rows, dst_col))
        return whole
    vmem = pl.BlockSpec(memory_space=pltpu.VMEM)
    return pl.pallas_call(
        functools.partial(place_kernel, tuple(plan), len(pieces)),
        in_specs=[pl.BlockSpec(memory_space=pltpu.SMEM)] + [vmem] * len(pieces),
        out_specs=[vmem] * len(outs),
        out_shape=[jax.ShapeDtypeStruct(out, BF16) for out in outs],
        compiler_params=params(),
        cost_estimate=pl.CostEstimate(
            flops=0, transcendentals=0, bytes_accessed=4 * sum(math.prod(out) for out in outs)
        ),
    )(place, *pieces)


def feed_kernel(shard, own, n_held, plan, place_ref, *refs):
    n_pieces = len(refs) - 13 - n_held
    pieces, held, refs = refs[:n_pieces], refs[n_pieces : n_pieces + n_held], refs[n_pieces + n_held :]
    tokens, cotangents = [
        [held[n].at[pl.ds(part * own, own), :] for n, part in parts] for parts in plan
    ]
    hid_ref, low_ref, send_ref, mine_ref, n_out, ct_out, down_out, *refs = refs
    gate_up, down, n_all, ct_all, sems, out_sems = refs
    step, steps = pl.program_id(0), pl.num_programs(0)
    hidden = down.shape[1]
    block = n_all.shape[0] // steps
    each = 8 // steps

    def row(n):
        return pl.ds(pl.multiple_of(place_ref[n] * shard, shard), shard)

    def copies_of(sources, target, first):
        return [
            pltpu.make_async_copy(source, target.at[pl.ds(n * own, own), :], sems.at[first + n])
            for n, source in enumerate(sources)
        ]

    inward = copies_of(tokens, n_all, 0), copies_of(cotangents, ct_all, 8)
    weights = [
        pltpu.make_async_copy(piece.at[:, pl.ds(0, 2 * hidden)], gate_up.at[row(n), :], sems.at[16 + n])
        for n, piece in enumerate(pieces)
    ]
    downs = [
        pltpu.make_async_copy(
            piece.at[:, pl.ds(2 * hidden, hidden)], down.at[row(n), :], sems.at[16 + n_pieces + n]
        )
        for n, piece in enumerate(pieces)
    ]

    @pl.when(step == 0)
    def _():
        for copy in inward[0][:each] + weights + inward[1][:each] + downs:
            copy.start()
        for copy in inward[0][each:] + inward[1][each:]:
            copy.start()
        for copy in weights:
            copy.wait()

    @pl.when(step == 0)
    def _():
        for copy in inward[0][:each]:
            copy.wait()

    @pl.when(step == 1)
    def _():
        for copy in inward[0][each:]:
            copy.wait()

    part = pl.ds(pl.multiple_of(step * block, block), block)
    both = mm(n_all[part, :], gate_up[...])
    gate, up = both[:, :hidden], both[:, hidden:]
    sigmoid = 1.0 / (1.0 + jnp.exp(-gate))
    silu = gate * sigmoid
    hid_ref[...] = (silu * up).astype(BF16)
    slope = up * sigmoid * (1.0 + gate * (1.0 - sigmoid))

    @pl.when(step == 0)
    def _():
        for copy in downs:
            copy.wait()

    @pl.when(step == 0)
    def _():
        for copy in inward[1][:each]:
            copy.wait()

    exports = [
        pltpu.make_async_copy(source, target, out_sems.at[n])
        for n, (source, target) in enumerate(((n_all, n_out), (ct_all, ct_out), (down, down_out)))
    ]

    @pl.when(step == 1)
    def _():
        for copy in inward[1][each:]:
            copy.wait()
        for export in exports:
            export.start()

    back = mm(ct_all[part, :], down[...]).astype(BF16).astype(F32)
    gate_low = (back * slope).astype(BF16)
    up_low = (back * silu).astype(BF16)
    low_ref[:, :hidden] = gate_low
    low_ref[:, hidden:] = up_low
    result = mm_nt(low_ref[...], gate_up[...])

    @pl.when(step < steps // 2)
    def _():
        send_ref[...] = result.astype(BF16)

    @pl.when(step >= steps // 2)
    def _():
        mine_ref[...] = result

    @pl.when(step == steps - 1)
    def _():
        for export in exports:
            export.wait()


def feed_forward(pieces, place, held, tokens, cotangents, shard, own):
    width = held[0].shape[1]
    hidden = pieces[0].shape[1] // 3
    rows = 8 * own
    steps = 4
    block = rows // steps
    vmem, anywhere = pl.BlockSpec(memory_space=pltpu.VMEM), pl.BlockSpec(memory_space=pl.ANY)
    half = steps // 2

    def blocks(cols):
        return pl.BlockSpec((block, cols), lambda step: (step, 0))

    return pl.pallas_call(
        functools.partial(
            feed_kernel, shard, own, len(held), (tuple(tokens), tuple(cotangents))
        ),
        grid=(steps,),
        in_specs=[pl.BlockSpec(memory_space=pltpu.SMEM)] + [anywhere] * (len(pieces) + len(held)),
        out_specs=[blocks(hidden), blocks(2 * hidden)]
        + [
            pl.BlockSpec((block, width), lambda step: (jnp.minimum(step, half - 1), 0)),
            pl.BlockSpec((block, width), lambda step: (jnp.maximum(step - half, 0), 0)),
        ]
        + [anywhere] * 3,
        out_shape=[
            jax.ShapeDtypeStruct((rows, hidden), BF16),
            jax.ShapeDtypeStruct((rows, 2 * hidden), BF16),
            jax.ShapeDtypeStruct((rows // 2, width), BF16),
            jax.ShapeDtypeStruct((rows // 2, width), F32),
            jax.ShapeDtypeStruct((rows, width), BF16),
            jax.ShapeDtypeStruct((rows, width), BF16),
            jax.ShapeDtypeStruct((width, hidden), BF16),
        ],
        scratch_shapes=[
            pltpu.VMEM((width, 2 * hidden), BF16),
            pltpu.VMEM((width, hidden), BF16),
            pltpu.VMEM((rows, width), BF16),
            pltpu.VMEM((rows, width), BF16),
            pltpu.SemaphoreType.DMA((16 + 2 * len(pieces),)),
            pltpu.SemaphoreType.DMA((3,)),
        ],
        compiler_params=params(VMEM_MOST),
        cost_estimate=pl.CostEstimate(
            flops=10 * rows * width * hidden,
            bytes_accessed=6 * width * hidden + 8 * rows * width,
            transcendentals=rows * hidden,
        ),
    )(place, *pieces, *held)


def spread_kernel(place_ref, *refs):
    pieces, (down_out, gate_out, up_out) = refs[:RING], refs[RING:]
    cols = pieces[0].shape[1] // 3
    for n, piece in enumerate(pieces):
        spot = pl.ds(pl.multiple_of(place_ref[n] * cols, cols), cols)
        for m, out in enumerate((down_out, gate_out, up_out)):
            out[:, spot] = piece[:, m * cols : (m + 1) * cols].astype(F32)


def spread(pieces, place):
    rows, cols = pieces[0].shape
    vmem = pl.BlockSpec(memory_space=pltpu.VMEM)
    down, gate, up = pl.pallas_call(
        spread_kernel,
        in_specs=[pl.BlockSpec(memory_space=pltpu.SMEM)] + [vmem] * RING,
        out_specs=[vmem] * 3,
        out_shape=[jax.ShapeDtypeStruct((rows, cols // 3 * RING), F32)] * 3,
        compiler_params=params(),
    )(place, *pieces)
    return gate, up, down


def split_kernel(down, place_ref, *refs):
    grads, outs = refs[: len(down)], refs[len(down) :]
    for n, out in enumerate(outs):
        row = col = 0
        for grad, below in zip(grads, down):
            count, cols = grad.shape[0] // len(outs), grad.shape[1]
            line = pl.ds(pl.multiple_of(place_ref[n] * count, count), count)
            out[row : row + count, col : col + cols] = grad[line, :]
            if below:
                row += count
            else:
                col += cols


def split_blocks(grads, place, below):
    count = place.shape[0]
    rows = [grad.shape[0] // count for grad in grads]
    cols = [grad.shape[1] for grad in grads]
    shape = (sum(rows), cols[0]) if below else (rows[0], sum(cols))
    vmem = pl.BlockSpec(memory_space=pltpu.VMEM)
    return pl.pallas_call(
        functools.partial(split_kernel, (below,) * len(grads)),
        in_specs=[pl.BlockSpec(memory_space=pltpu.SMEM)] + [vmem] * len(grads),
        out_specs=[vmem] * count,
        out_shape=[jax.ShapeDtypeStruct(shape, BF16)] * count,
        compiler_params=params(),
    )(place, *grads)


def pack_early_kernel(half_ref, q_any, k_any, v_any, o_any, gain_ref, send_ref, keep_ref, *scratch):
    *held, sems = scratch
    copies = [
        pltpu.make_async_copy(source, target, sems.at[n])
        for n, (source, target) in enumerate(zip((q_any, k_any, v_any, o_any), held))
    ]
    for copy in copies:
        copy.start()
    for copy in copies:
        copy.wait()
    q_ref, k_ref, v_ref, o_ref = held
    rows, cols = o_ref.shape[0], o_ref.shape[1] // 2
    for out, index in ((send_ref, 1 - half_ref[0]), (keep_ref, half_ref[0])):
        first = pl.multiple_of(index * cols, PAIR)
        for pair in range(cols // PAIR):
            for n, ref in enumerate((q_ref, k_ref, v_ref)):
                spot = (3 * pair + n) * PAIR
                out[:rows, spot : spot + PAIR] = ref[:, pl.ds(first + pair * PAIR, PAIR)]
        out[:rows, 3 * cols :] = o_ref[:, pl.ds(first, cols)]
    send_ref[rows:, :] = gain_ref[...]


def pack_early(query, key, value, output, gains, half, cols):
    rows, full = query.shape
    vmem = pl.BlockSpec(memory_space=pltpu.VMEM)
    anywhere = pl.BlockSpec(memory_space=pl.ANY)
    return pl.pallas_call(
        pack_early_kernel,
        in_specs=[pl.BlockSpec(memory_space=pltpu.SMEM)] + [anywhere] * 4 + [vmem],
        out_specs=[vmem] * 2,
        out_shape=[
            jax.ShapeDtypeStruct((rows + gains.shape[0], 4 * cols), BF16),
            jax.ShapeDtypeStruct((rows, 4 * cols), BF16),
        ],
        scratch_shapes=[pltpu.VMEM((rows, full), BF16)] * 4 + [pltpu.SemaphoreType.DMA((4,))],
        compiler_params=params(VMEM_MOST),
    )(half.reshape(1), query, key, value, output, gains)


RING = 4


class Links:
    def __init__(self, mesh):
        self.fsdp = mesh.shape["fsdp"]
        self.width = self.fsdp // RING
        index = lax.axis_index("fsdp")
        self.at = lax.div(index, self.width)
        self.lane = index - self.at * self.width
        self.half = lax.axis_index("ctx")
        self.core = lax.axis_index("tp")
        self.step = jnp.zeros((8, 128), F32)

    def sync(self, *values):
        flat, tree = jax.tree.flatten(values)
        self.step, *flat = lax.optimization_barrier([self.step, *flat])
        return jax.tree.unflatten(tree, flat)

    def begun(self, value):
        return lax.optimization_barrier([value, self.step])[0]

    def ring(self, value, hops):
        z, r = RING, self.width
        pairs = [(a * r + b, (a + hops) % z * r + b) for a in range(z) for b in range(r)]
        return lax.ppermute(self.begun(value), "fsdp", pairs)

    def lanes(self, value):
        z, r = RING, self.width
        pairs = [(a * r + b, a * r + (b + 1) % r) for a in range(z) for b in range(r)]
        return lax.ppermute(self.begun(value), "fsdp", pairs)

    def over_half(self, value):
        return lax.ppermute(self.begun(value), "ctx", [(0, 1), (1, 0)])

    def over_core(self, value):
        return lax.ppermute(self.begun(value), "tp", [(0, 1), (1, 0)])

    def ring_at(self, back):
        return (self.at + (RING - back)) & (RING - 1)

    def lane_at(self, turn):
        return lax.rem(self.lane + (self.width - turn), self.width) if turn else self.lane

    def place(self, back, turn):
        return self.ring_at(back) * self.width + self.lane_at(turn)

    def block_places(self):
        n = lax.iota(jnp.int32, RING * self.width * 2)
        back = lax.div(n, 2 * self.width)
        turn = lax.rem(lax.div(n, 2), self.width)
        ring = (self.at + RING - back) & (RING - 1)
        lane = lax.rem(self.lane + self.width - turn, self.width)
        return (ring * self.width + lane) * 2 + (self.half ^ (n & 1))

    def all_lanes(self, value):
        values = [value]
        while len(values) < self.width:
            values.append(self.lanes(values[-1]))
        return values

    def sum_lanes(self, terms):
        total, *rest = terms
        for term in rest:
            total = (self.lanes(total).astype(F32) + term.astype(F32)).astype(BF16)
        return self.lanes(total)

    def both_cores(self, own):
        other = self.over_core(own)
        first = jnp.where(self.core == 0, own, other)
        second = jnp.where(self.core == 0, other, own)
        return jnp.concatenate([first, second], axis=0)

    def swap_halves(self, total):
        keep = lax.dynamic_index_in_dim(total, self.half, 0, keepdims=False)
        send = lax.dynamic_index_in_dim(total, 1 - self.half, 0, keepdims=False)
        return keep, self.over_half(send.astype(BF16)).astype(F32)

    def side_by_side(self, keep, recv):
        return jnp.concatenate(
            [jnp.where(self.half == 0, keep, recv), jnp.where(self.half == 0, recv, keep)], axis=-1
        )


def slot(values, count, index):
    size = values.shape[1] // count
    return lax.dynamic_slice_in_dim(values, index * size, size, 1)


def in_order(values, index):
    count = len(values)
    ahead = jnp.concatenate(values[::-1], axis=1)
    size = ahead.shape[1]
    first = lax.rem(2 * count - 1 - index, count)
    twice = jnp.concatenate([ahead, ahead], axis=1)
    return lax.dynamic_slice_in_dim(twice, first * (size // count), size, 1)


def on_device(
    mesh,
    inputs,
    conditioning,
    query_matrix,
    key_matrix,
    value_matrix,
    output_matrix,
    cross_query,
    cross_key,
    cross_value,
    cross_output,
    gate_matrix,
    up_matrix,
    down_matrix,
    first_gain,
    second_gain,
    third_gain,
    cotangent,
):
    links = Links(mesh)
    ring, lanes, all_lanes = links.ring, links.lanes, links.all_lanes
    over_half, over_core = links.over_half, links.over_core
    sync = links.sync
    core, half, lane_count = links.core, links.half, links.width
    rows = inputs.shape[1]
    own_rows = rows // 2
    width = inputs.shape[2]
    shard = query_matrix.shape[0]
    cols = query_matrix.shape[1] // 2
    pairs = cols // PAIR
    context_shard = cross_key.shape[0]
    context_width = conditioning.shape[2]
    context_count = conditioning.shape[1]
    hidden = gate_matrix.shape[1] // RING
    blocks = links.fsdp * 2
    places = links.block_places()

    def half_cols(values, index):
        return lax.dynamic_slice_in_dim(values, index * cols, cols, 1)

    def early_part(index):
        parts = [half_cols(w, index) for w in (query_matrix, key_matrix, value_matrix)]
        return jnp.concatenate(
            [p[:, n * PAIR : (n + 1) * PAIR] for n in range(pairs) for p in parts]
            + [half_cols(output_matrix.T, index)],
            axis=1,
        )

    def late_part(index):
        return jnp.concatenate(
            [
                half_cols(w, index)
                for w in (cross_query, cross_output.T, cross_key, cross_value)
            ],
            axis=0,
        )

    def feed_part(index):
        return jnp.concatenate(
            [
                lax.dynamic_slice_in_dim(w, index * hidden, hidden, 1)
                for w in (gate_matrix, up_matrix, down_matrix.T)
            ],
            axis=1,
        )

    def halves_of(left, weights):
        pair = 2 * own_rows
        return mm_nt(left[:pair], weights), mm_nt(left[pair:], weights).astype(BF16)

    def for_half(mine, recv):
        return (mine[own_rows:] + recv[own_rows:].astype(F32)).astype(BF16)

    def spread_cores(own, over):
        pair = jnp.concatenate([own, over], axis=0)
        return jnp.concatenate([pair, over_core(pair)], axis=0)

    own = lax.dynamic_slice_in_dim(inputs[0], core * own_rows, own_rows, 0)
    other = lax.dynamic_slice_in_dim(inputs[0], (1 - core) * own_rows, own_rows, 0)
    upstream = lax.dynamic_slice_in_dim(cotangent[0], core * own_rows, own_rows, 0)
    row = lax.iota(jnp.int32, own_rows)
    position = jnp.concatenate(
        [
            row + (half ^ there) * rows + (core ^ beside) * own_rows
            for beside in (0, 1)
            for there in (0, 1)
        ]
    )
    mark = lax.broadcasted_iota(jnp.int32, (16, width), 1)
    place = (lax.axis_index("fsdp") * 2 + half) * shard
    gains = jnp.pad(jnp.stack([first_gain, second_gain, third_gain]), ((0, 13), (0, 0)))
    gains = jnp.where(
        (mark >= place) & (mark < place + shard), jnp.tile(gains, (1, blocks)), jnp.zeros((), BF16)
    )
    early_send, early_keep = pack_early(
        query_matrix, key_matrix, value_matrix, output_matrix.T, gains, half, cols
    )
    early_recv, cotangent1 = over_half(early_send), ring(upstream, 1)
    early_keep, early_recv, gains = sync(early_keep, early_recv, gains)

    early0 = jnp.concatenate([early_keep, early_recv[:shard], gains + early_recv[shard:]], axis=0)
    early1, lanes0, own_over = ring(early0, 1), all_lanes(early0), over_half(own)
    early1, lanes0, own_over, late_send, late_keep, cotangent1 = sync(
        early1, lanes0, own_over, late_part(1 - half), late_part(half), cotangent1
    )

    early3, lanes1, late_recv = ring(lanes0[0], -1), all_lanes(early1), over_half(late_send)
    other_over = over_core(own_over)
    early3, lanes1, late_recv, other_over, tables, feed0, feed_send = sync(
        early3,
        lanes1,
        late_recv,
        other_over,
        rotary_tables(position),
        feed_part(links.at),
        feed_part(links.ring_at(RING - 1)),
    )

    early2, lanes3, feed0_over = ring(lanes1[0], 1), all_lanes(early3), over_half(feed0)
    late0 = jnp.concatenate([late_keep, late_recv], axis=0)
    early2, lanes3, feed0_over, late0, feed0, feed_sends = sync(
        early2,
        lanes3,
        feed0_over,
        late0,
        feed0,
        [feed_part(links.ring_at(back)) for back in (1, 2)],
    )

    late1, lanes2 = ring(late0, 1), all_lanes(early2)
    context = jnp.pad(conditioning[0], ((0, -context_count % 128), (0, 0)))
    late1, lanes2, context, late_both = sync(
        late1, lanes2, context, jnp.concatenate([late0, late1], axis=0)
    )

    feed1, late2, late3 = ring(feed_send, 1), ring(late1, 1), ring(late0, -1)
    late_lanes01, feed0_lanes = all_lanes(late_both), all_lanes(feed0)
    (
        qkv_low, self_low, self_logsum, partial, send, gains, qkv_full, output_full, normed_one,
    ) = self_forward(
        lanes0 + lanes1 + lanes2 + lanes3, places, (own, own_over, other, other_over), tables, shard
    )
    first_norm_gain, second_norm_gain, third_norm_gain = gains[0:1], gains[1:2], gains[2:3]
    partial, send, feed1, late_lanes01, feed0_lanes, late_both = sync(
        partial, send, feed1, late_lanes01, feed0_lanes, jnp.concatenate([late2, late3], axis=0)
    )

    recv = over_core(send)
    far_term = over_half((partial + recv.astype(F32)).astype(BF16))
    feed2, feed3, late_lanes23 = (
        ring(feed_sends[1], 2),
        ring(feed_sends[0], -1),
        all_lanes(late_both),
    )
    far_term, late_lanes23, feed2, cotangents, x_send, y_send = sync(
        far_term,
        late_lanes23,
        feed2,
        jnp.concatenate([upstream, cotangent1], axis=0),
        jnp.concatenate([feed0_over, feed1], axis=0),
        jnp.concatenate([feed1, feed3], axis=0),
    )
    hidden_one, normed = pair_forward(second_norm_gain, own, own_over, partial, recv, far_term)

    cotangent3, x_recv, y_recv = ring(upstream, -1), all_lanes(x_send), over_half(y_send)
    late_rows = 2 * (shard + context_shard)
    plan = []
    for n in range(blocks):
        first = (n % 2) * 2 * (shard + context_shard)
        for out in range(2):
            plan.append((n // 2, n, first + out * shard, shard, 0, cols, out, 0))
        for out in range(2):
            start = first + 2 * shard + out * context_shard
            plan.append((n // 2, n, start, context_shard, 0, cols, 2, out * cols))
    cross_query_full, cross_output_full, context_full = place_pieces(
        [part[: 2 * late_rows] for part in late_lanes01]
        + [part[2 * late_rows :] for part in late_lanes01]
        + [part[: 2 * late_rows] for part in late_lanes23]
        + [part[2 * late_rows :] for part in late_lanes23],
        plan,
        places,
        [(width, cols)] * 2 + [(context_width, 2 * cols)],
    )
    context_low = mm(context, context_full).astype(BF16)
    normed_two = jnp.concatenate([normed, over_core(normed)], axis=0)
    cross_query_low = mm(normed_two, cross_query_full).astype(BF16) * jnp.asarray(SCALE, BF16)
    cross_low, cross_logsum = cross_forward(cross_query_low, context_low, context_count)
    partial, send = halves_of(cross_low, cross_output_full)
    cotangents_core = over_core(cotangents)
    partial, send, cotangent3, x_recv, y_recv, cotangents_core = sync(
        partial, send, cotangent3, x_recv, y_recv, cotangents_core
    )
    feed0_over_lanes = [part[:shard] for part in x_recv]
    feed1_lanes = [part[shard:] for part in x_recv]
    feed1_over, feed3_over, feed3 = y_recv[:shard], y_recv[shard:], y_send[shard:]

    recv = over_core(send)
    far_term, cotangent2, feed3_lanes = over_half(for_half(partial, recv)), ring(cotangent1, 1), all_lanes(feed3)
    far_term, cotangent2, feed3_lanes, x_send, y_send = sync(
        far_term,
        cotangent2,
        feed3_lanes,
        jnp.concatenate([feed1_over, feed2], axis=0),
        jnp.concatenate([feed2, *feed3_lanes[1:]], axis=0),
    )

    hidden_two, normed0 = norm_forward(
        own_rows, hidden_one, third_norm_gain, partial, recv, far_term
    )
    normed1, normed3 = ring(normed0, 1), ring(normed0, -1)
    x_recv, y_recv = all_lanes(x_send), over_half(y_send)
    core0 = over_core(jnp.concatenate([cotangent3, cotangent2, normed0], axis=0))
    normed1, normed3, x_recv, y_recv, core0 = sync(normed1, normed3, x_recv, y_recv, core0)
    feed1_over_lanes = [part[:shard] for part in x_recv]
    feed2_lanes = [part[shard:] for part in x_recv]
    feed2_over = y_recv[:shard]
    feed3_lanes_over = [feed3_over] + [
        y_recv[shard * n : shard * (n + 1)] for n in range(1, lane_count)
    ]

    normed2 = ring(normed1, 1)
    feed2_lanes_over = [feed2_over] + [over_half(value) for value in feed2_lanes[1:]]
    core1 = over_core(jnp.concatenate([normed1, normed3], axis=0))
    normed2, feed2_lanes_over, core1 = sync(normed2, feed2_lanes_over, core1)

    core2 = over_core(normed2)
    pieces = [
        piece
        for lanes_pieces, over_pieces in (
            (feed0_lanes, feed0_over_lanes),
            (feed1_lanes, feed1_over_lanes),
            (feed2_lanes, feed2_lanes_over),
            (feed3_lanes, feed3_lanes_over),
        )
        for piece in [part for both in zip(lanes_pieces, over_pieces) for part in both]
    ]
    held = [
        core0, core1, core2, normed0, normed1, normed3, normed2,
        cotangents_core, cotangents, cotangent3, cotangent2,
    ]
    feed_low, both_low, send, mine, normed_three, upstream_all, down_full = feed_forward(
        pieces,
        places,
        held,
        [(0, 2), (1, 0), (1, 1), (2, 0), (3, 0), (4, 0), (5, 0), (6, 0)],
        [(7, 0), (7, 1), (0, 0), (0, 1), (8, 0), (8, 1), (9, 0), (10, 0)],
        shard,
        own_rows,
    )
    feed_low, both_low, send, mine, normed_three, upstream_all, down_full = sync(
        feed_low, both_low, send, mine, normed_three, upstream_all, down_full
    )

    def ring_halves(left, weights):
        count = RING * own_rows
        return mm_nt(left[count:], weights), mm_nt(left[:count], weights).astype(BF16)

    def block_of(mine, recv, back):
        spot = (0, 1, 3, 2)[back]
        part = slice(spot * own_rows, (spot + 1) * own_rows)
        return mine[part] + recv[part].astype(F32)

    def lanes_block(grads, turn):
        place = links.lane_at(turn)
        return jnp.concatenate(
            [
                lax.dynamic_slice_in_dim(grads, (z * lane_count + place) * 2 * shard, 2 * shard, 0)
                for z in (0, 1)
            ],
            axis=0,
        )

    def halves_block(grads, index):
        return jnp.concatenate(
            [
                lax.dynamic_slice_in_dim(
                    grads, ((z * lane_count + n) * 2 + index) * shard, shard, 0
                )
                for z in (2, 3)
                for n in range(lane_count)
            ],
            axis=0,
        )

    def lanes_terms(grads):
        return [lanes_block(grads, turn) for turn in range(1, lane_count)]

    def lanes_second(grads, recv):
        total = (lanes_block(grads, 0).astype(F32) + recv.astype(F32)).reshape(2, 2, shard, -1)
        keep = lax.dynamic_index_in_dim(total, half, 1, keepdims=False)
        send = lax.dynamic_index_in_dim(total, 1 - half, 1, keepdims=False)
        return keep, send.astype(BF16)

    def halves_second(grads, recv):
        total = (halves_block(grads, half).astype(F32) + recv.astype(F32)).reshape(
            2, lane_count, shard, -1
        )
        keep, *send = [
            lax.dynamic_index_in_dim(total, links.lane_at(turn), 1, keepdims=False)
            for turn in range(lane_count)
        ]
        return keep, [term.astype(BF16) for term in send]

    def joined(*terms):
        keep, recv, keep_late, recv_late = terms
        return jnp.concatenate(
            [
                (keep + recv.astype(F32)).astype(BF16),
                (keep_late + recv_late.astype(F32)).astype(BF16),
            ],
            axis=0,
        )

    recv = over_core(send)
    down_grad = mm_tn(upstream_all, feed_low).astype(BF16)
    recv, mine, both_low, normed_three, feed_low, down_grad = sync(
        recv, mine, both_low, normed_three, feed_low, down_grad
    )
    mine, recv, both_low, normed_three, down_grad, down_lanes, down_halves, ring_low = sync(
        mine,
        recv,
        both_low,
        normed_three,
        down_grad,
        lanes_terms(down_grad),
        halves_block(down_grad, 1 - half),
        block_of(mine, recv, 2).astype(BF16),
    )

    two = ring(ring_low, -1)
    down_lanes, down_halves = links.sum_lanes(down_lanes), over_half(down_halves)
    both_grad = mm_tn(normed_three, both_low).astype(BF16)
    out_mine, out_send = ring_halves(feed_low, down_full)
    two, both_grad, down_lanes, down_halves, out_mine, out_send, three = sync(
        two,
        both_grad,
        down_lanes,
        down_halves,
        out_mine,
        out_send,
        block_of(mine, recv, 3).astype(BF16),
    )

    three = ring(three, 1)
    one = ring((block_of(mine, recv, 1) + two.astype(F32)).astype(BF16), -1)
    both_lanes = links.sum_lanes(lanes_terms(both_grad))
    both_halves = over_half(halves_block(both_grad, 1 - half))
    out_recv = over_core(out_send)
    down_keep, down_move = lanes_second(down_grad, down_lanes)
    down_late_keep, down_late_move = halves_second(down_grad, down_halves)
    one, three, both_lanes, both_halves, out_recv, out_low, downs = sync(
        one,
        three,
        both_lanes,
        both_halves,
        out_recv,
        [block_of(out_mine, out_recv, back).astype(BF16) for back in (2, 3)],
        (down_keep, down_move, down_late_keep, down_late_move),
    )
    down_keep, down_move, down_late_keep, down_late_move = downs

    hidden_two_grad, low, third_gain_grad = norm_backward(
        hidden_two, third_norm_gain, upstream, mine, recv, one, three
    )
    low, out_send = lax.optimization_barrier((low, out_low[0]))
    low_over = over_half(low)
    out_two = ring(out_send, -1)
    both_keep, both_move = lanes_second(both_grad, both_lanes)
    both_late_keep, both_late_move = halves_second(both_grad, both_halves)
    low_over, low, out_two, both_keep, both_late_keep, x_send, y_send, out_one = sync(
        low_over,
        low,
        out_two,
        both_keep,
        both_late_keep,
        [jnp.concatenate(pair, axis=-1) for pair in zip(down_late_move, both_late_move)],
        jnp.concatenate([down_move, both_move], axis=-1),
        (block_of(out_mine, out_recv, 1) + out_two.astype(F32)).astype(BF16),
    )

    moved, late_sum, out_three, out_one = (
        over_half(y_send),
        links.sum_lanes(x_send),
        ring(out_low[1], 1),
        ring(out_one, -1),
    )
    branch_two = spread_cores(low, low_over)
    cross_out_grad = mm(branch_two, cross_output_full).astype(BF16)
    cross_query_round, cross_key_back, cross_value_back = cross_backward(
        cross_query_low, context_low, cross_low, cross_out_grad, cross_logsum, context_count
    )
    partial, send = halves_of(cross_query_round, cross_query_full)
    partial, send, moved, late_sum, out_three, out_one, branch_two = sync(
        partial, send, moved, late_sum, out_three, out_one, branch_two
    )
    recv = over_core(send)
    feed_mine = jnp.concatenate(
        [
            joined(down_keep, moved[..., :hidden], down_late_keep, late_sum[..., :hidden]),
            joined(both_keep, moved[..., hidden:], both_late_keep, late_sum[..., hidden:]),
        ],
        axis=2,
    )
    ring_places = jnp.stack(
        [links.place(back, turn) for back in range(RING) for turn in range(lane_count)]
    )

    def by_back(blocks):
        rows = [blocks[back * lane_count : (back + 1) * lane_count] for back in range(RING)]
        return [row[0] for row in rows], [row[1:] for row in rows]

    def below(others, backs):
        return [jnp.concatenate(parts, axis=0) for parts in zip(*[others[back] for back in backs])]

    cross_grads = [
        mm_tn(branch_two, cross_low).astype(BF16),
        mm_tn(normed_two, cross_query_round).astype(BF16),
        mm_tn(context, cross_key_back).astype(BF16),
        mm_tn(context, cross_value_back).astype(BF16),
    ]
    cross_own, cross_other = by_back(split_blocks(cross_grads, ring_places, True))
    recv, feed_mine, feed_send, cross_own, cross_late, cross_most, backs = sync(
        recv,
        feed_mine,
        [
            lax.dynamic_index_in_dim(feed_mine, links.ring_at(back), 0, keepdims=False)
            for back in (1, 2, 3)
        ],
        cross_own,
        below(cross_other, (0, 1)),
        below(cross_other, (2, 3)),
        (cross_key_back, cross_value_back),
    )
    cross_key_back, cross_value_back = backs

    def out_of(values, back):
        return lax.dynamic_index_in_dim(values, links.ring_at(back), 0, keepdims=False)

    half_send = (partial + recv.astype(F32)).astype(BF16)
    half_send, feed_send, cross_most = lax.optimization_barrier((half_send, feed_send, cross_most))
    far_term = over_half(half_send)
    feed1_sum, feed3_sum = ring(feed_send[2], 1), ring(feed_send[0], -1)
    cross_most = links.sum_lanes(cross_most)
    block_rows = cross_most.shape[0] // 2
    far_term, feed1_sum, feed3_sum, cross_two, cross_three, cross_late = sync(
        far_term,
        feed1_sum,
        feed3_sum,
        (cross_own[2].astype(F32) + cross_most[:block_rows].astype(F32)).astype(BF16),
        (cross_own[3].astype(F32) + cross_most[block_rows:].astype(F32)).astype(BF16),
        cross_late,
    )
    hidden_one_grad, low, second_gain_grad = pair_backward(
        second_norm_gain, hidden_one, hidden_two_grad, low_over, partial, recv, far_term
    )

    feed2_sum, cross_two = ring(feed_send[1], 2), ring(cross_two, -1)
    cross_late = links.sum_lanes(cross_late)
    branch_one = jnp.concatenate([low, over_core(low)], axis=0)
    self_out_grad = mm(branch_one, output_full).astype(BF16)
    qkv_round = self_backward(qkv_low, self_low, self_out_grad, self_logsum, tables)
    partial, send = halves_of(qkv_round, qkv_full)
    partial, send, feed2_sum, cross_late, cross_two, qkv_round, branch_one = sync(
        partial, send, feed2_sum, cross_late, cross_two, qkv_round, branch_one
    )
    output_grad = mm_tn(branch_one, self_low).astype(BF16)
    qkv_grad = mm_tn(normed_one, qkv_round).astype(BF16)
    self_own, self_other = by_back(split_blocks([output_grad, qkv_grad], ring_places, False))
    cross_zero = cross_own[0].astype(F32) + cross_late[:block_rows].astype(F32)
    cross_one = cross_own[1].astype(F32) + cross_late[block_rows:].astype(F32)
    cross_three = ring(cross_three, 1)
    recv, cross_three, self_own, self_other, cross_zero, cross_one, backs = sync(
        over_core(send),
        cross_three,
        self_own,
        self_other,
        cross_zero,
        (cross_one + cross_two.astype(F32)).astype(BF16),
        (cross_key_back, cross_value_back),
    )
    cross_key_back, cross_value_back = backs

    half_send = for_half(partial, recv)
    half_send, cross_one, self_send = lax.optimization_barrier(
        (half_send, cross_one, self_other[2])
    )
    far_term = over_half(half_send)
    cross_one = ring(cross_one, -1)
    self2 = links.sum_lanes(self_send)
    context_term = (
        mm_nt(cross_key_back, context_full[:, :cols])
        + mm_nt(cross_value_back, context_full[:, cols:])
    )[:context_count]
    context_recv = over_core(context_term.astype(BF16))
    far_term, cross_one, self2, context_term, context_recv, self_two = sync(
        far_term,
        cross_one,
        self2,
        context_term,
        context_recv,
        (self_own[2].astype(F32) + self2.astype(F32)).astype(BF16),
    )

    self3 = links.sum_lanes(self_other[3])
    self_two = ring(self_two, -1)
    context_low_sum = (context_term + context_recv.astype(F32)).astype(BF16)
    context_over = over_half(context_low_sum)
    inputs_grad, _, first_gain_grad = norm_backward(
        own, first_norm_gain, hidden_one_grad, partial, recv, far_term
    )
    layer_result = links.both_cores(
        hidden_two + block_of(out_mine, out_recv, 0) + out_one.astype(F32) + out_three.astype(F32)
    )
    gain_grads = jnp.concatenate([first_gain_grad, second_gain_grad, third_gain_grad], axis=0)
    gate_sum, up_sum, down_sum = spread(
        [out_of(feed_mine, 0), feed1_sum, feed2_sum, feed3_sum],
        jnp.stack([links.ring_at(back) for back in range(RING)]),
    )
    cross_total = cross_zero + cross_one.astype(F32) + cross_three.astype(F32)
    sizes = (shard, shard, context_shard, context_shard)
    starts = [2 * sum(sizes[:n]) for n in range(4)]
    cross_total = jnp.concatenate(
        [
            cross_total[start : start + 2 * size].reshape(2, size, cols)
            for start, size in zip(starts, sizes)
        ],
        axis=1,
    )
    gain_grads = gain_grads + over_core(gain_grads)
    gain_grads = gain_grads + over_half(gain_grads)
    context_grad = context_low_sum.astype(F32) + context_over.astype(F32)
    self3, self_two, context_grad, layer_result, gain_grads, inputs_grad, feed_sums, cross_total, self_three = sync(
        self3,
        self_two,
        context_grad,
        layer_result,
        gain_grads,
        inputs_grad,
        (gate_sum, up_sum, down_sum),
        cross_total,
        (self_own[3].astype(F32) + self3.astype(F32)).astype(BF16),
    )
    gate_sum, up_sum, down_sum = feed_sums

    self1 = links.sum_lanes(self_other[1])
    self_three = ring(self_three, 1)
    gain_lanes = (
        gain_grads.reshape(3, RING, lane_count, -1).swapaxes(1, 2).reshape(3, -1)
    )
    gain_total = slot(gain_lanes, lane_count, links.lane_at(1))
    for turn in list(range(2, lane_count)) + [0]:
        gain_total = links.lanes(gain_total) + slot(gain_lanes, lane_count, links.lane_at(turn))
    gain_ring = [slot(gain_total, RING, links.ring_at(back)) for back in range(RING)]
    gain_two, gain_three = ring(gain_ring[2], -1), ring(gain_ring[3], 1)
    cross_keep, cross_recv = links.swap_halves(cross_total)
    self1, self_three, gain_two, gain_three, cross_recv, self_one = sync(
        self1,
        self_three,
        gain_two,
        gain_three,
        cross_recv,
        (self_own[1].astype(F32) + self1.astype(F32) + self_two.astype(F32)).astype(BF16),
    )

    self0 = links.sum_lanes(self_other[0])
    self_one = ring(self_one, -1)
    gain_one = ring(gain_ring[1] + gain_two, -1)
    inputs_result = links.both_cores(inputs_grad)
    cross_sums = links.side_by_side(cross_keep, cross_recv)
    gain_sums = slot(gain_ring[0] + gain_one + gain_three, 2, half)
    self0, self_one, gain_sums, inputs_result, cross_sums = sync(
        self0, self_one, gain_sums, inputs_result, cross_sums
    )

    self_total = (
        self_own[0].astype(F32) + self0.astype(F32) + self_one.astype(F32) + self_three.astype(F32)
    )
    keep, recv = links.swap_halves(self_total.reshape(2, shard, 4 * cols))

    def of_self(values, n):
        if n == 3:
            return values[:, :cols]
        return jnp.concatenate(
            [
                values[:, cols + (3 * pair + n) * PAIR : cols + (3 * pair + n + 1) * PAIR]
                for pair in range(pairs)
            ],
            axis=1,
        )

    query_sum, key_sum, value_sum, output_sum = (
        links.side_by_side(of_self(keep, n), of_self(recv, n)) for n in range(4)
    )
    return (
        layer_result[None],
        inputs_result[None],
        context_grad[None],
        query_sum,
        key_sum,
        value_sum,
        output_sum.T,
        cross_sums[shard : 2 * shard],
        cross_sums[2 * shard : 2 * shard + context_shard],
        cross_sums[2 * shard + context_shard :],
        cross_sums[:shard].T,
        gate_sum,
        up_sum,
        down_sum.T,
        gain_sums[0],
        gain_sums[1],
        gain_sums[2],
    )


def solution(mesh):
    row = P(("fsdp", "ctx"), "tp")
    col = P("tp", ("fsdp", "ctx"))
    gain = P(("fsdp", "ctx"))
    token = P("fsdp", "ctx", None)
    context = P("fsdp", None, None)
    weights = (row, row, row, col, row, row, row, col, row, row, col, gain, gain, gain)
    return jax.shard_map(
        functools.partial(on_device, mesh),
        mesh=mesh,
        in_specs=(token, context) + weights + (token,),
        out_specs=(token, token, context) + weights,
        check_vma=False,
    )
```

```python
import functools
import math

import jax
import jax.numpy as jnp
from jax import lax
from jax.experimental import pallas as pl
from jax.experimental.pallas import tpu as pltpu
from jax.sharding import PartitionSpec as P

HDIM = 64
EPSILON = 1e-05
F32 = jnp.float32
BF16 = jnp.bfloat16
SCALE = HDIM ** (-0.5)
PAIR = 2 * HDIM
VMEM_LIMIT = 48 * 1024 * 1024
VMEM_MOST = 60 * 1024 * 1024


def mm(left, right):
    return lax.dot_general(left, right, (((1,), (0,)), ((), ())), preferred_element_type=F32)


def mm_tn(left, right):
    return lax.dot_general(left, right, (((0,), (0,)), ((), ())), preferred_element_type=F32)


def mm_nt(left, right):
    return lax.dot_general(left, right, (((1,), (1,)), ((), ())), preferred_element_type=F32)


def norm_stats(values):
    center = values - jnp.mean(values, axis=-1, keepdims=True)
    rate = lax.rsqrt(jnp.mean(center * center, axis=-1, keepdims=True) + EPSILON)
    return center * rate, rate


def params(limit=VMEM_LIMIT):
    return pltpu.CompilerParams(vmem_limit_bytes=limit)


def norm_call(kernel, rows, outs, *operands):
    width = operands[0].shape[1]

    def block(count):
        return pl.BlockSpec((count, width), lambda step: (0, 0))

    return pl.pallas_call(
        kernel,
        grid=(1,),
        in_specs=[block(min(rows, operand.shape[0])) for operand in operands],
        out_specs=[block(count) for count, _ in outs],
        out_shape=[jax.ShapeDtypeStruct((count, width), kind) for count, kind in outs],
        compiler_params=params(),
    )(*operands)


def norm_forward_kernel(gain_ref, base_ref, *refs):
    *terms, x_ref, n_ref = refs
    values = base_ref[...].astype(F32)
    for term in terms:
        values = values + term[...].astype(F32)
    x_ref[...] = values
    n_ref[...] = (norm_stats(values)[0] * gain_ref[...]).astype(BF16)


def norm_forward(rows, base, gain, *terms):
    return norm_call(norm_forward_kernel, rows, ((rows, F32), (rows, BF16)), gain, base, *terms)


def pair_forward_kernel(gain_ref, own_ref, over_ref, near_ref, core_ref, far_ref, x_ref, n_ref):
    terms = near_ref[...] + core_ref[...].astype(F32) + far_ref[...].astype(F32)
    base = jnp.where(pl.program_id(0) == 0, own_ref[...].astype(F32), over_ref[...].astype(F32))
    values = base + terms
    x_ref[...] = values
    n_ref[...] = (norm_stats(values)[0] * gain_ref[...]).astype(BF16)


def pair_blocks(rows, width):
    return (
        pl.BlockSpec((rows, width), lambda step: (step, 0)),
        pl.BlockSpec((rows, width), lambda step: (1 - step, 0)),
        pl.BlockSpec((rows, width), lambda step: (0, 0)),
        pl.BlockSpec((1, width), lambda step: (0, 0)),
    )


def pair_forward(gain, own, over, near, core, far):
    rows, width = near.shape
    here, there, fixed, line = pair_blocks(rows // 2, width)
    return pl.pallas_call(
        pair_forward_kernel,
        grid=(2,),
        in_specs=[line, fixed, fixed, here, here, there],
        out_specs=[here, here],
        out_shape=(
            jax.ShapeDtypeStruct((rows, width), F32),
            jax.ShapeDtypeStruct((rows, width), BF16),
        ),
        compiler_params=params(),
    )(gain, own, over, near, core, far)


def pair_backward_kernel(
    gain_ref, x_ref, skip_ref, over_ref, near_ref, core_ref, far_ref, dx_ref, low_ref, dg_ref
):
    upstream = near_ref[...] + core_ref[...].astype(F32) + far_ref[...].astype(F32)
    unit, rate = norm_stats(x_ref[...])
    scaled = upstream * gain_ref[...]
    back = rate * (
        scaled
        - jnp.mean(scaled, axis=-1, keepdims=True)
        - unit * jnp.mean(scaled * unit, axis=-1, keepdims=True)
    )
    first = pl.program_id(0) == 0
    total = jnp.where(first, skip_ref[...], over_ref[...].astype(F32)) + back
    low_ref[...] = total.astype(BF16)

    @pl.when(first)
    def _():
        dx_ref[...] = total
        dg_ref[...] = jnp.sum(upstream * unit, axis=0, keepdims=True)


def pair_backward(gain, values, skip, over, near, core, far):
    rows, width = values.shape
    here, there, fixed, line = pair_blocks(rows // 2, width)
    return pl.pallas_call(
        pair_backward_kernel,
        grid=(2,),
        in_specs=[line, here, fixed, fixed, here, here, there],
        out_specs=[fixed, here, line],
        out_shape=(
            jax.ShapeDtypeStruct((rows // 2, width), F32),
            jax.ShapeDtypeStruct((rows, width), BF16),
            jax.ShapeDtypeStruct((1, width), F32),
        ),
        compiler_params=params(),
    )(gain, values, skip, over, near, core, far)


def norm_backward_kernel(gain_ref, x_ref, skip_ref, *refs):
    *terms, dx_ref, low_ref, dg_ref = refs
    upstream = terms[0][...].astype(F32)
    for term in terms[1:]:
        upstream = upstream + term[...].astype(F32)
    unit, rate = norm_stats(x_ref[...].astype(F32))
    scaled = upstream * gain_ref[...]
    back = rate * (
        scaled
        - jnp.mean(scaled, axis=-1, keepdims=True)
        - unit * jnp.mean(scaled * unit, axis=-1, keepdims=True)
    )
    total = skip_ref[...].astype(F32) + back
    dx_ref[...] = total
    low_ref[...] = total.astype(BF16)
    dg_ref[...] = jnp.sum(upstream * unit, axis=0, keepdims=True)


def norm_backward(values, gain, skip, *terms):
    rows = values.shape[0]
    outs = (rows, F32), (rows, BF16), (1, F32)
    return norm_call(norm_backward_kernel, rows, outs, gain, values, skip, *terms)


def turned(values, cosine, upper, lower):
    width = values.shape[1]
    return (
        values * cosine
        + pltpu.roll(values, width - HDIM // 4, 1) * upper
        + pltpu.roll(values, HDIM // 4, 1) * lower
    )


def chunk_of(rows):
    return 128 if rows % 128 == 0 else rows


def low_half(shape):
    return lax.broadcasted_iota(jnp.int32, shape, len(shape) - 1) < HDIM


def of_head(values, head):
    first = low_half(values.shape)
    keep = first if head == 0 else jnp.logical_not(first)
    return jnp.where(keep, values, jnp.zeros((), values.dtype))


def forward_heads(q_ref, k_ref, v_ref, o_ref, lse_ref, valid):
    rows = q_ref.shape[0]
    step = chunk_of(rows)
    key, value = k_ref[...], v_ref[...]
    first_half = low_half(value.shape)
    ones = jnp.ones((), BF16)
    extended = jnp.where(first_half, value, ones), jnp.where(first_half, ones, value)
    for first in range(0, rows, step):
        part = slice(first, first + step)
        query = q_ref[part, :]
        results = []
        for head in range(2):
            scores = mm_nt(of_head(query, head), key)
            if valid < key.shape[0]:
                column = lax.broadcasted_iota(jnp.int32, scores.shape, 1)
                scores = jnp.where(column < valid, scores, -1e30)
            peak = jnp.max(scores, axis=-1, keepdims=True)
            mixed = mm(jnp.exp(scores - peak).astype(BF16), extended[head])
            total = pltpu.roll(mixed, HDIM, 1)
            results.append((mixed * (1.0 / total), peak + jnp.log(total)))
        lanes = low_half((step, PAIR))
        o_ref[part, :] = jnp.where(lanes, results[0][0], results[1][0]).astype(BF16)
        lse_ref[part, :] = jnp.where(lanes, results[0][1], results[1][1])


def thirds(ref):
    return ref.at[:, :PAIR], ref.at[:, PAIR : 2 * PAIR], ref.at[:, 2 * PAIR :]


def self_forward_kernel(shard, place_ref, *refs):
    n_pieces = len(refs) - 23
    pieces, refs = refs[:n_pieces], refs[n_pieces:]
    parts, refs = refs[:4], refs[4:]
    cos_ref, up_ref, low_ref, *refs = refs
    turned_ref, o_ref, lse_ref, mine_ref, send_ref, gain_ref, *refs = refs
    qkv_out, output_out, normed_out, *refs = refs
    qkv_all, output_all, normed_all, gain_all, o_all = refs[:-2]
    sems, out_sems = refs[-2:]
    pair, cols = pl.program_id(0), qkv_all.shape[1]
    gain_rows = gain_all.shape[0] // n_pieces

    @pl.when(pair == 0)
    def _():
        copies = []
        for n, piece in enumerate(pieces):
            mark = pl.ds(n * gain_rows, gain_rows)
            copies.append((piece.at[pl.ds(2 * shard, gain_rows), pl.ds(0, gain_all.shape[1])], gain_all.at[mark, :]))
        for n, piece in enumerate(pieces):
            for there in (0, 1):
                row = pl.ds(pl.multiple_of(place_ref[2 * n + there] * shard, shard), shard)
                lines = pl.ds(there * shard, shard)
                copies.append((piece.at[lines, pl.ds(0, cols)], qkv_all.at[row, :]))
                copies.append((piece.at[lines, pl.ds(cols, output_all.shape[1])], output_all.at[row, :]))
        copies = [
            pltpu.make_async_copy(source, target, sems.at[n])
            for n, (source, target) in enumerate(copies)
        ]
        for copy in copies:
            copy.start()
        for copy in copies[:n_pieces]:
            copy.wait()
        gains = jnp.zeros((gain_rows, gain_all.shape[1]), F32)
        for n in range(n_pieces):
            gains = gains + gain_all[n * gain_rows : (n + 1) * gain_rows, :].astype(F32)
        gain_ref[...] = gains
        first = 0
        for part in parts:
            unit, _ = norm_stats(part[...].astype(F32))
            normed_all[first : first + part.shape[0], :] = (unit * gains[:1]).astype(BF16)
            first += part.shape[0]
        for copy in copies[n_pieces:]:
            copy.wait()

    exports = [
        pltpu.make_async_copy(source, target, out_sems.at[n])
        for n, (source, target) in enumerate(
            ((qkv_all, qkv_out), (output_all, output_out), (normed_all, normed_out))
        )
    ]

    @pl.when(pair == 0)
    def _():
        for export in exports:
            export.start()

    tables = cos_ref[...], up_ref[...], low_ref[...]
    q_ref, k_ref, v_ref = thirds(turned_ref)
    first = pl.multiple_of(pair * 3 * PAIR, PAIR)
    qkv = mm(normed_all[...], qkv_all[:, pl.ds(first, 3 * PAIR)])
    q_ref[...] = turned(qkv[:, :PAIR], *tables).astype(BF16) * jnp.asarray(SCALE, BF16)
    k_ref[...] = turned(qkv[:, PAIR : 2 * PAIR], *tables).astype(BF16)
    v_ref[...] = qkv[:, 2 * PAIR :].astype(BF16)
    forward_heads(q_ref, k_ref, v_ref, o_ref, lse_ref, k_ref.shape[0])
    o_all[:, pl.ds(pl.multiple_of(pair * PAIR, PAIR), PAIR)] = o_ref[...]

    @pl.when(pair == pl.num_programs(0) - 1)
    def _():
        half = o_all.shape[0] // 2
        mine_ref[...] = mm_nt(o_all[:half, :], output_all[...])
        send_ref[...] = mm_nt(o_all[half:, :], output_all[...]).astype(BF16)
        for export in exports:
            export.wait()


def self_forward(pieces, place, parts, tables, shard):
    width, cols = parts[0].shape[1], pieces[0].shape[1] // 4
    rows, pairs = sum(part.shape[0] for part in parts), cols // PAIR
    gain_rows = pieces[0].shape[0] - 2 * shard
    vmem, anywhere = pl.BlockSpec(memory_space=pltpu.VMEM), pl.BlockSpec(memory_space=pl.ANY)

    def paired(width):
        return pl.BlockSpec((rows, width), lambda pair: (0, pair))

    def whole(shape):
        return pl.BlockSpec(shape, lambda pair: (0, 0))

    return pl.pallas_call(
        functools.partial(self_forward_kernel, shard),
        grid=(pairs,),
        in_specs=[pl.BlockSpec(memory_space=pltpu.SMEM)]
        + [anywhere] * len(pieces)
        + [whole(part.shape) for part in parts]
        + [whole((rows, PAIR))] * 3,
        out_specs=[paired(3 * PAIR), paired(PAIR), paired(PAIR)]
        + [whole((rows // 2, width))] * 2
        + [whole((gain_rows, width))]
        + [anywhere] * 3,
        out_shape=[
            jax.ShapeDtypeStruct((rows, 3 * cols), BF16),
            jax.ShapeDtypeStruct((rows, cols), BF16),
            jax.ShapeDtypeStruct((rows, cols), F32),
            jax.ShapeDtypeStruct((rows // 2, width), F32),
            jax.ShapeDtypeStruct((rows // 2, width), BF16),
            jax.ShapeDtypeStruct((gain_rows, width), F32),
            jax.ShapeDtypeStruct((width, 3 * cols), BF16),
            jax.ShapeDtypeStruct((width, cols), BF16),
            jax.ShapeDtypeStruct((rows, width), BF16),
        ],
        scratch_shapes=[
            pltpu.VMEM((width, 3 * cols), BF16),
            pltpu.VMEM((width, cols), BF16),
            pltpu.VMEM((rows, width), BF16),
            pltpu.VMEM((len(pieces) * gain_rows, width), BF16),
            pltpu.VMEM((rows, cols), BF16),
            pltpu.SemaphoreType.DMA((5 * len(pieces),)),
            pltpu.SemaphoreType.DMA((3,)),
        ],
        compiler_params=params(VMEM_MOST),
        cost_estimate=pl.CostEstimate(
            flops=4 * rows * rows * cols + 2 * rows * width * 4 * cols,
            bytes_accessed=8 * width * cols + 2 * rows * width,
            transcendentals=rows * rows * cols // HDIM,
        ),
    )(place, *pieces, *parts, *tables)


def cross_forward_kernel(valid, q_ref, k_ref, v_ref, o_ref, lse_ref):
    forward_heads(q_ref, k_ref, v_ref, o_ref, lse_ref, valid)


def backward_heads(q_ref, k_ref, v_ref, o_ref, do_ref, lse_ref, dq_ref, dk_ref, dv_ref, valid):
    rows = q_ref.shape[0]
    step = chunk_of(rows)
    key, value = k_ref[...], v_ref[...]
    for first in range(0, rows, step):
        part = slice(first, first + step)
        query, grad = q_ref[part, :], do_ref[part, :]
        lse = lse_ref[part, :].T
        delta = (grad.astype(F32) * o_ref[part, :].astype(F32)).T
        query_terms = []
        for head in range(2):
            query_head, grad_head = of_head(query, head), of_head(grad, head)
            lanes = slice(head * HDIM, (head + 1) * HDIM)
            mean_grad = jnp.sum(delta[lanes, :], axis=0, keepdims=True)
            probability = jnp.exp(mm_nt(key, query_head) - lse[head * HDIM : head * HDIM + 1, :])
            if valid < key.shape[0]:
                line = lax.broadcasted_iota(jnp.int32, probability.shape, 0)
                probability = jnp.where(line < valid, probability, 0.0)
            score_grad = (probability * (mm_nt(value, grad_head) - mean_grad)).astype(BF16)
            query_terms.append(mm_tn(score_grad, key))
            key_term = mm(score_grad, query_head)
            value_term = mm(probability.astype(BF16), grad_head)
            if first == 0 and head == 0:
                dk_ref[...] = key_term
                dv_ref[...] = value_term
            else:
                dk_ref[...] += key_term
                dv_ref[...] += value_term
        dq_ref[part, :] = jnp.where(low_half((step, PAIR)), *query_terms) * SCALE


def self_backward_kernel(
    turned_ref, o_ref, do_ref, lse_ref, cos_ref, up_ref, low_ref, out_ref, dq_acc, dk_acc, dv_acc
):
    q_ref, k_ref, v_ref = thirds(turned_ref)
    backward_heads(
        q_ref, k_ref, v_ref, o_ref, do_ref, lse_ref, dq_acc, dk_acc, dv_acc, k_ref.shape[0]
    )
    tables = cos_ref[...], -up_ref[...], -low_ref[...]
    dq_ref, dk_ref, dv_ref = thirds(out_ref)
    dq_ref[...] = turned(dq_acc[...], *tables).astype(BF16)
    dk_ref[...] = turned(dk_acc[...], *tables).astype(BF16)
    dv_ref[...] = dv_acc[...].astype(BF16)


def cross_backward_kernel(
    valid, q_ref, k_ref, v_ref, o_ref, do_ref, lse_ref, dq_ref, dk_ref, dv_ref, dq_acc, dk_acc, dv_acc
):
    some = -(-valid // 16) * 16
    backward_heads(
        q_ref, k_ref.at[:some, :], v_ref.at[:some, :], o_ref, do_ref, lse_ref,
        dq_acc, dk_acc.at[:some, :], dv_acc.at[:some, :], valid,
    )
    dq_ref[...] = dq_acc[...].astype(BF16)
    for ref, acc in ((dk_ref, dk_acc), (dv_ref, dv_acc)):
        ref[:some, :] = acc[:some, :].astype(BF16)
        if some < ref.shape[0]:
            ref[some:, :] = jnp.zeros((ref.shape[0] - some, PAIR), BF16)


def attention_call(kernel, pairs, ins, outs, scratch, flops):
    return pl.pallas_call(
        kernel,
        grid=(pairs,),
        in_specs=[
            pl.BlockSpec((rows, width), functools.partial(lambda place, pair: (0, place(pair)), place))
            for rows, width, place in ins
        ],
        out_specs=[pl.BlockSpec((rows, width), lambda pair: (0, pair)) for rows, width, _ in outs],
        out_shape=[
            jax.ShapeDtypeStruct((rows, width * pairs), kind) for rows, width, kind in outs
        ],
        scratch_shapes=[pltpu.VMEM((rows, PAIR), F32) for rows in scratch],
        compiler_params=params(),
        cost_estimate=pl.CostEstimate(
            flops=flops,
            bytes_accessed=4 * pairs * sum(rows * width for rows, width, _ in ins),
            transcendentals=flops // 256,
        ),
    )


def here(pair):
    return pair


def always(pair):
    return 0


def self_backward(qkv, out, grad, lse, tables):
    rows, pairs = qkv.shape[0], qkv.shape[1] // (3 * PAIR)
    return attention_call(
        self_backward_kernel,
        pairs,
        [(rows, 3 * PAIR, here)] + [(rows, PAIR, here)] * 3 + [(rows, PAIR, always)] * 3,
        [(rows, 3 * PAIR, BF16)],
        (rows,) * 3,
        10 * rows * rows * pairs * PAIR,
    )(qkv, out, grad, lse, *tables)[0]


def cross_forward(query, context, valid):
    rows, pairs, keys = query.shape[0], query.shape[1] // PAIR, context.shape[0]
    return attention_call(
        functools.partial(cross_forward_kernel, valid),
        pairs,
        [(rows, PAIR, here), (keys, PAIR, here), (keys, PAIR, lambda pair: pairs + pair)],
        [(rows, PAIR, BF16), (rows, PAIR, F32)],
        (),
        4 * rows * keys * pairs * PAIR,
    )(query, context, context)


def cross_backward(query, context, out, grad, lse, valid):
    rows, pairs, keys = query.shape[0], query.shape[1] // PAIR, context.shape[0]
    return attention_call(
        functools.partial(cross_backward_kernel, valid),
        pairs,
        [(rows, PAIR, here), (keys, PAIR, here), (keys, PAIR, lambda pair: pairs + pair)]
        + [(rows, PAIR, here)] * 3,
        [(rows, PAIR, BF16), (keys, PAIR, BF16), (keys, PAIR, BF16)],
        (rows, keys, keys),
        10 * rows * keys * pairs * PAIR,
    )(query, context, context, out, grad, lse)


def rotary_tables(position):
    quarter = HDIM // 4
    lane = lax.broadcasted_iota(jnp.int32, (position.shape[0], PAIR), 1) & (HDIM - 1)
    turn = (lane & (quarter - 1)).astype(F32)
    frequency = jnp.exp(-(2.0 * turn / (2 * quarter)) * math.log(10000.0))
    angles = position.astype(F32)[:, None] * frequency
    cosine, sine = jnp.cos(angles), jnp.sin(angles)
    return (
        jnp.where(lane < 2 * quarter, cosine, 1.0),
        jnp.where(lane < quarter, -sine, 0.0),
        jnp.where((lane >= quarter) & (lane < 2 * quarter), sine, 0.0),
    )


def place_kernel(plan, n_pieces, place_ref, *refs):
    pieces, outs = refs[:n_pieces], refs[n_pieces:]
    for piece, spot, src_row, rows, src_col, cols, out, dst_col in plan:
        row = pl.multiple_of(place_ref[spot] * rows, rows)
        outs[out][pl.ds(row, rows), dst_col : dst_col + cols] = pieces[piece][
            src_row : src_row + rows, src_col : src_col + cols
        ]


def place_pieces(pieces, plan, place, outs):
    if any(entry[2] % 16 or entry[3] % 16 for entry in plan):
        whole = [jnp.zeros(out, BF16) for out in outs]
        for piece, spot, src_row, rows, src_col, cols, out, dst_col in plan:
            part = pieces[piece][src_row : src_row + rows, src_col : src_col + cols]
            whole[out] = lax.dynamic_update_slice(whole[out], part, (place[spot] * rows, dst_col))
        return whole
    vmem = pl.BlockSpec(memory_space=pltpu.VMEM)
    return pl.pallas_call(
        functools.partial(place_kernel, tuple(plan), len(pieces)),
        in_specs=[pl.BlockSpec(memory_space=pltpu.SMEM)] + [vmem] * len(pieces),
        out_specs=[vmem] * len(outs),
        out_shape=[jax.ShapeDtypeStruct(out, BF16) for out in outs],
        compiler_params=params(),
        cost_estimate=pl.CostEstimate(
            flops=0, transcendentals=0, bytes_accessed=4 * sum(math.prod(out) for out in outs)
        ),
    )(place, *pieces)


def feed_kernel(shard, own, n_held, plan, place_ref, *refs):
    n_pieces = len(refs) - 13 - n_held
    pieces, held, refs = refs[:n_pieces], refs[n_pieces : n_pieces + n_held], refs[n_pieces + n_held :]
    tokens, cotangents = [
        [held[n].at[pl.ds(part * own, own), :] for n, part in parts] for parts in plan
    ]
    hid_ref, low_ref, send_ref, mine_ref, n_out, ct_out, down_out, *refs = refs
    gate_up, down, n_all, ct_all, sems, out_sems = refs
    step, steps = pl.program_id(0), pl.num_programs(0)
    hidden = down.shape[1]
    block = n_all.shape[0] // steps
    each = 8 // steps

    def row(n):
        return pl.ds(pl.multiple_of(place_ref[n] * shard, shard), shard)

    def copies_of(sources, target, first):
        return [
            pltpu.make_async_copy(source, target.at[pl.ds(n * own, own), :], sems.at[first + n])
            for n, source in enumerate(sources)
        ]

    inward = copies_of(tokens, n_all, 0), copies_of(cotangents, ct_all, 8)
    weights = [
        pltpu.make_async_copy(piece.at[:, pl.ds(0, 2 * hidden)], gate_up.at[row(n), :], sems.at[16 + n])
        for n, piece in enumerate(pieces)
    ]
    downs = [
        pltpu.make_async_copy(
            piece.at[:, pl.ds(2 * hidden, hidden)], down.at[row(n), :], sems.at[16 + n_pieces + n]
        )
        for n, piece in enumerate(pieces)
    ]

    @pl.when(step == 0)
    def _():
        for copy in inward[0][:each] + weights + inward[1][:each] + downs:
            copy.start()
        for copy in inward[0][each:] + inward[1][each:]:
            copy.start()
        for copy in weights:
            copy.wait()

    @pl.when(step == 0)
    def _():
        for copy in inward[0][:each]:
            copy.wait()

    @pl.when(step == 1)
    def _():
        for copy in inward[0][each:]:
            copy.wait()

    part = pl.ds(pl.multiple_of(step * block, block), block)
    both = mm(n_all[part, :], gate_up[...])
    gate, up = both[:, :hidden], both[:, hidden:]
    sigmoid = 1.0 / (1.0 + jnp.exp(-gate))
    silu = gate * sigmoid
    hid_ref[...] = (silu * up).astype(BF16)
    slope = up * sigmoid * (1.0 + gate * (1.0 - sigmoid))

    @pl.when(step == 0)
    def _():
        for copy in downs:
            copy.wait()

    @pl.when(step == 0)
    def _():
        for copy in inward[1][:each]:
            copy.wait()

    exports = [
        pltpu.make_async_copy(source, target, out_sems.at[n])
        for n, (source, target) in enumerate(((n_all, n_out), (ct_all, ct_out), (down, down_out)))
    ]

    @pl.when(step == 1)
    def _():
        for copy in inward[1][each:]:
            copy.wait()
        for export in exports:
            export.start()

    back = mm(ct_all[part, :], down[...]).astype(BF16).astype(F32)
    gate_low = (back * slope).astype(BF16)
    up_low = (back * silu).astype(BF16)
    low_ref[:, :hidden] = gate_low
    low_ref[:, hidden:] = up_low
    result = mm_nt(low_ref[...], gate_up[...])

    @pl.when(step < steps // 2)
    def _():
        send_ref[...] = result.astype(BF16)

    @pl.when(step >= steps // 2)
    def _():
        mine_ref[...] = result

    @pl.when(step == steps - 1)
    def _():
        for export in exports:
            export.wait()


def feed_forward(pieces, place, held, tokens, cotangents, shard, own):
    width = held[0].shape[1]
    hidden = pieces[0].shape[1] // 3
    rows = 8 * own
    steps = 4
    block = rows // steps
    vmem, anywhere = pl.BlockSpec(memory_space=pltpu.VMEM), pl.BlockSpec(memory_space=pl.ANY)
    half = steps // 2

    def blocks(cols):
        return pl.BlockSpec((block, cols), lambda step: (step, 0))

    return pl.pallas_call(
        functools.partial(
            feed_kernel, shard, own, len(held), (tuple(tokens), tuple(cotangents))
        ),
        grid=(steps,),
        in_specs=[pl.BlockSpec(memory_space=pltpu.SMEM)] + [anywhere] * (len(pieces) + len(held)),
        out_specs=[blocks(hidden), blocks(2 * hidden)]
        + [
            pl.BlockSpec((block, width), lambda step: (jnp.minimum(step, half - 1), 0)),
            pl.BlockSpec((block, width), lambda step: (jnp.maximum(step - half, 0), 0)),
        ]
        + [anywhere] * 3,
        out_shape=[
            jax.ShapeDtypeStruct((rows, hidden), BF16),
            jax.ShapeDtypeStruct((rows, 2 * hidden), BF16),
            jax.ShapeDtypeStruct((rows // 2, width), BF16),
            jax.ShapeDtypeStruct((rows // 2, width), F32),
            jax.ShapeDtypeStruct((rows, width), BF16),
            jax.ShapeDtypeStruct((rows, width), BF16),
            jax.ShapeDtypeStruct((width, hidden), BF16),
        ],
        scratch_shapes=[
            pltpu.VMEM((width, 2 * hidden), BF16),
            pltpu.VMEM((width, hidden), BF16),
            pltpu.VMEM((rows, width), BF16),
            pltpu.VMEM((rows, width), BF16),
            pltpu.SemaphoreType.DMA((16 + 2 * len(pieces),)),
            pltpu.SemaphoreType.DMA((3,)),
        ],
        compiler_params=params(VMEM_MOST),
        cost_estimate=pl.CostEstimate(
            flops=10 * rows * width * hidden,
            bytes_accessed=6 * width * hidden + 8 * rows * width,
            transcendentals=rows * hidden,
        ),
    )(place, *pieces, *held)


def spread_kernel(place_ref, *refs):
    pieces, (down_out, gate_out, up_out) = refs[:RING], refs[RING:]
    cols = pieces[0].shape[1] // 3
    for n, piece in enumerate(pieces):
        spot = pl.ds(pl.multiple_of(place_ref[n] * cols, cols), cols)
        for m, out in enumerate((down_out, gate_out, up_out)):
            out[:, spot] = piece[:, m * cols : (m + 1) * cols].astype(F32)


def spread(pieces, place):
    rows, cols = pieces[0].shape
    vmem = pl.BlockSpec(memory_space=pltpu.VMEM)
    down, gate, up = pl.pallas_call(
        spread_kernel,
        in_specs=[pl.BlockSpec(memory_space=pltpu.SMEM)] + [vmem] * RING,
        out_specs=[vmem] * 3,
        out_shape=[jax.ShapeDtypeStruct((rows, cols // 3 * RING), F32)] * 3,
        compiler_params=params(),
    )(place, *pieces)
    return gate, up, down


def split_kernel(down, place_ref, *refs):
    grads, outs = refs[: len(down)], refs[len(down) :]
    for n, out in enumerate(outs):
        row = col = 0
        for grad, below in zip(grads, down):
            count, cols = grad.shape[0] // len(outs), grad.shape[1]
            line = pl.ds(pl.multiple_of(place_ref[n] * count, count), count)
            out[row : row + count, col : col + cols] = grad[line, :]
            if below:
                row += count
            else:
                col += cols


def split_blocks(grads, place, below):
    count = place.shape[0]
    rows = [grad.shape[0] // count for grad in grads]
    cols = [grad.shape[1] for grad in grads]
    shape = (sum(rows), cols[0]) if below else (rows[0], sum(cols))
    vmem = pl.BlockSpec(memory_space=pltpu.VMEM)
    return pl.pallas_call(
        functools.partial(split_kernel, (below,) * len(grads)),
        in_specs=[pl.BlockSpec(memory_space=pltpu.SMEM)] + [vmem] * len(grads),
        out_specs=[vmem] * count,
        out_shape=[jax.ShapeDtypeStruct(shape, BF16)] * count,
        compiler_params=params(),
    )(place, *grads)


def pack_early_kernel(half_ref, q_any, k_any, v_any, o_any, gain_ref, send_ref, keep_ref, *scratch):
    *held, sems = scratch
    copies = [
        pltpu.make_async_copy(source, target, sems.at[n])
        for n, (source, target) in enumerate(zip((q_any, k_any, v_any, o_any), held))
    ]
    for copy in copies:
        copy.start()
    for copy in copies:
        copy.wait()
    q_ref, k_ref, v_ref, o_ref = held
    rows, cols = o_ref.shape[0], o_ref.shape[1] // 2
    for out, index in ((send_ref, 1 - half_ref[0]), (keep_ref, half_ref[0])):
        first = pl.multiple_of(index * cols, PAIR)
        for pair in range(cols // PAIR):
            for n, ref in enumerate((q_ref, k_ref, v_ref)):
                spot = (3 * pair + n) * PAIR
                out[:rows, spot : spot + PAIR] = ref[:, pl.ds(first + pair * PAIR, PAIR)]
        out[:rows, 3 * cols :] = o_ref[:, pl.ds(first, cols)]
    send_ref[rows:, :] = gain_ref[...]


def join_early_kernel(keep_ref, recv_ref, gain_ref, out_ref):
    rows = keep_ref.shape[0]
    out_ref[:rows, :] = keep_ref[...]
    out_ref[rows : 2 * rows, :] = recv_ref[:rows, :]
    marks = gain_ref[...].astype(F32) + recv_ref[rows:, :].astype(F32)
    out_ref[2 * rows :, :] = marks.astype(BF16)


def join_early(keep, recv, gains):
    return pl.pallas_call(
        join_early_kernel,
        out_shape=jax.ShapeDtypeStruct((keep.shape[0] + recv.shape[0], keep.shape[1]), BF16),
        compiler_params=params(),
    )(keep, recv, gains)


def pack_early(query, key, value, output, gains, half, cols):
    rows, full = query.shape
    vmem = pl.BlockSpec(memory_space=pltpu.VMEM)
    anywhere = pl.BlockSpec(memory_space=pl.ANY)
    return pl.pallas_call(
        pack_early_kernel,
        in_specs=[pl.BlockSpec(memory_space=pltpu.SMEM)] + [anywhere] * 4 + [vmem],
        out_specs=[vmem] * 2,
        out_shape=[
            jax.ShapeDtypeStruct((rows + gains.shape[0], 4 * cols), BF16),
            jax.ShapeDtypeStruct((rows, 4 * cols), BF16),
        ],
        scratch_shapes=[pltpu.VMEM((rows, full), BF16)] * 4 + [pltpu.SemaphoreType.DMA((4,))],
        compiler_params=params(VMEM_MOST),
    )(half.reshape(1), query, key, value, output, gains)


RING = 4


class Links:
    def __init__(self, mesh):
        self.fsdp = mesh.shape["fsdp"]
        self.width = self.fsdp // RING
        index = lax.axis_index("fsdp")
        self.at = lax.div(index, self.width)
        self.lane = index - self.at * self.width
        self.half = lax.axis_index("ctx")
        self.core = lax.axis_index("tp")
        self.step = jnp.zeros((8, 128), F32)

    def sync(self, *values):
        flat, tree = jax.tree.flatten(values)
        self.step, *flat = lax.optimization_barrier([self.step, *flat])
        return jax.tree.unflatten(tree, flat)

    def begun(self, value):
        return lax.optimization_barrier([value, self.step])[0]

    def ring(self, value, hops):
        z, r = RING, self.width
        pairs = [(a * r + b, (a + hops) % z * r + b) for a in range(z) for b in range(r)]
        return lax.ppermute(self.begun(value), "fsdp", pairs)

    def lanes(self, value):
        z, r = RING, self.width
        pairs = [(a * r + b, a * r + (b + 1) % r) for a in range(z) for b in range(r)]
        return lax.ppermute(self.begun(value), "fsdp", pairs)

    def over_half(self, value):
        return lax.ppermute(self.begun(value), "ctx", [(0, 1), (1, 0)])

    def over_core(self, value):
        return lax.ppermute(self.begun(value), "tp", [(0, 1), (1, 0)])

    def ring_at(self, back):
        return (self.at + (RING - back)) & (RING - 1)

    def lane_at(self, turn):
        return lax.rem(self.lane + (self.width - turn), self.width) if turn else self.lane

    def place(self, back, turn):
        return self.ring_at(back) * self.width + self.lane_at(turn)

    def block_places(self):
        n = lax.iota(jnp.int32, RING * self.width * 2)
        back = lax.div(n, 2 * self.width)
        turn = lax.rem(lax.div(n, 2), self.width)
        ring = (self.at + RING - back) & (RING - 1)
        lane = lax.rem(self.lane + self.width - turn, self.width)
        return (ring * self.width + lane) * 2 + (self.half ^ (n & 1))

    def all_lanes(self, value):
        values = [value]
        while len(values) < self.width:
            values.append(self.lanes(values[-1]))
        return values

    def sum_lanes(self, terms):
        total, *rest = terms
        for term in rest:
            total = (self.lanes(total).astype(F32) + term.astype(F32)).astype(BF16)
        return self.lanes(total)

    def both_cores(self, own):
        other = self.over_core(own)
        first = jnp.where(self.core == 0, own, other)
        second = jnp.where(self.core == 0, other, own)
        return jnp.concatenate([first, second], axis=0)

    def swap_halves(self, total):
        keep = lax.dynamic_index_in_dim(total, self.half, 0, keepdims=False)
        send = lax.dynamic_index_in_dim(total, 1 - self.half, 0, keepdims=False)
        return keep, self.over_half(send.astype(BF16)).astype(F32)

    def side_by_side(self, keep, recv):
        return jnp.concatenate(
            [jnp.where(self.half == 0, keep, recv), jnp.where(self.half == 0, recv, keep)], axis=-1
        )


def slot(values, count, index):
    size = values.shape[1] // count
    return lax.dynamic_slice_in_dim(values, index * size, size, 1)


def in_order(values, index):
    count = len(values)
    ahead = jnp.concatenate(values[::-1], axis=1)
    size = ahead.shape[1]
    first = lax.rem(2 * count - 1 - index, count)
    twice = jnp.concatenate([ahead, ahead], axis=1)
    return lax.dynamic_slice_in_dim(twice, first * (size // count), size, 1)


def on_device(
    mesh,
    inputs,
    conditioning,
    query_matrix,
    key_matrix,
    value_matrix,
    output_matrix,
    cross_query,
    cross_key,
    cross_value,
    cross_output,
    gate_matrix,
    up_matrix,
    down_matrix,
    first_gain,
    second_gain,
    third_gain,
    cotangent,
):
    links = Links(mesh)
    ring, lanes, all_lanes = links.ring, links.lanes, links.all_lanes
    over_half, over_core = links.over_half, links.over_core
    sync = links.sync
    core, half, lane_count = links.core, links.half, links.width
    rows = inputs.shape[1]
    own_rows = rows // 2
    width = inputs.shape[2]
    shard = query_matrix.shape[0]
    cols = query_matrix.shape[1] // 2
    pairs = cols // PAIR
    context_shard = cross_key.shape[0]
    context_width = conditioning.shape[2]
    context_count = conditioning.shape[1]
    hidden = gate_matrix.shape[1] // RING
    blocks = links.fsdp * 2
    places = links.block_places()

    def half_cols(values, index):
        return lax.dynamic_slice_in_dim(values, index * cols, cols, 1)

    def early_part(index):
        parts = [half_cols(w, index) for w in (query_matrix, key_matrix, value_matrix)]
        return jnp.concatenate(
            [p[:, n * PAIR : (n + 1) * PAIR] for n in range(pairs) for p in parts]
            + [half_cols(output_matrix.T, index)],
            axis=1,
        )

    def late_part(index):
        return jnp.concatenate(
            [
                half_cols(w, index)
                for w in (cross_query, cross_output.T, cross_key, cross_value)
            ],
            axis=0,
        )

    def feed_part(index):
        return jnp.concatenate(
            [
                lax.dynamic_slice_in_dim(w, index * hidden, hidden, 1)
                for w in (gate_matrix, up_matrix, down_matrix.T)
            ],
            axis=1,
        )

    def halves_of(left, weights):
        pair = 2 * own_rows
        return mm_nt(left[:pair], weights), mm_nt(left[pair:], weights).astype(BF16)

    def for_half(mine, recv):
        return (mine[own_rows:] + recv[own_rows:].astype(F32)).astype(BF16)

    def spread_cores(own, over):
        pair = jnp.concatenate([own, over], axis=0)
        return jnp.concatenate([pair, over_core(pair)], axis=0)

    own = lax.dynamic_slice_in_dim(inputs[0], core * own_rows, own_rows, 0)
    other = lax.dynamic_slice_in_dim(inputs[0], (1 - core) * own_rows, own_rows, 0)
    upstream = lax.dynamic_slice_in_dim(cotangent[0], core * own_rows, own_rows, 0)
    row = lax.iota(jnp.int32, own_rows)
    position = jnp.concatenate(
        [
            row + (half ^ there) * rows + (core ^ beside) * own_rows
            for beside in (0, 1)
            for there in (0, 1)
        ]
    )
    mark = lax.broadcasted_iota(jnp.int32, (16, width), 1)
    place = (lax.axis_index("fsdp") * 2 + half) * shard
    gains = jnp.pad(jnp.stack([first_gain, second_gain, third_gain]), ((0, 13), (0, 0)))
    gains = jnp.where(
        (mark >= place) & (mark < place + shard), jnp.tile(gains, (1, blocks)), jnp.zeros((), BF16)
    )
    early_send, early_keep = pack_early(
        query_matrix, key_matrix, value_matrix, output_matrix.T, gains, half, cols
    )
    early_recv, cotangent1 = over_half(early_send), ring(upstream, 1)
    early_keep, early_recv, gains = sync(early_keep, early_recv, gains)

    early0 = join_early(early_keep, early_recv, gains)
    early1, lanes0, own_over = ring(early0, 1), all_lanes(early0), over_half(own)
    early1, lanes0, own_over, late_send, late_keep, cotangent1 = sync(
        early1, lanes0, own_over, late_part(1 - half), late_part(half), cotangent1
    )

    early3, lanes1, late_recv = ring(lanes0[0], -1), all_lanes(early1), over_half(late_send)
    other_over = over_core(own_over)
    early3, lanes1, late_recv, other_over, tables, feed0, feed_send = sync(
        early3,
        lanes1,
        late_recv,
        other_over,
        rotary_tables(position),
        feed_part(links.at),
        feed_part(links.ring_at(RING - 1)),
    )

    early2, lanes3, feed0_over = ring(lanes1[0], 1), all_lanes(early3), over_half(feed0)
    late0 = jnp.concatenate([late_keep, late_recv], axis=0)
    early2, lanes3, feed0_over, late0, feed0, feed_sends = sync(
        early2,
        lanes3,
        feed0_over,
        late0,
        feed0,
        [feed_part(links.ring_at(back)) for back in (1, 2)],
    )

    late1, lanes2 = ring(late0, 1), all_lanes(early2)
    context = jnp.pad(conditioning[0], ((0, -context_count % 128), (0, 0)))
    late1, lanes2, context, late_both = sync(
        late1, lanes2, context, jnp.concatenate([late0, late1], axis=0)
    )

    feed1, late2, late3 = ring(feed_send, 1), ring(late1, 1), ring(late0, -1)
    late_lanes01, feed0_lanes = all_lanes(late_both), all_lanes(feed0)
    (
        qkv_low, self_low, self_logsum, partial, send, gains, qkv_full, output_full, normed_one,
    ) = self_forward(
        lanes0 + lanes1 + lanes2 + lanes3, places, (own, own_over, other, other_over), tables, shard
    )
    first_norm_gain, second_norm_gain, third_norm_gain = gains[0:1], gains[1:2], gains[2:3]
    partial, send, feed1, late_lanes01, feed0_lanes, late_both = sync(
        partial, send, feed1, late_lanes01, feed0_lanes, jnp.concatenate([late2, late3], axis=0)
    )

    recv = over_core(send)
    far_term = over_half((partial + recv.astype(F32)).astype(BF16))
    feed2, feed3, late_lanes23 = (
        ring(feed_sends[1], 2),
        ring(feed_sends[0], -1),
        all_lanes(late_both),
    )
    far_term, late_lanes23, feed2, cotangents, x_send, y_send = sync(
        far_term,
        late_lanes23,
        feed2,
        jnp.concatenate([upstream, cotangent1], axis=0),
        jnp.concatenate([feed0_over, feed1], axis=0),
        jnp.concatenate([feed1, feed3], axis=0),
    )
    hidden_one, normed = pair_forward(second_norm_gain, own, own_over, partial, recv, far_term)

    cotangent3, x_recv, y_recv = ring(upstream, -1), all_lanes(x_send), over_half(y_send)
    late_rows = 2 * (shard + context_shard)
    plan = []
    for n in range(blocks):
        first = (n % 2) * 2 * (shard + context_shard)
        for out in range(2):
            plan.append((n // 2, n, first + out * shard, shard, 0, cols, out, 0))
        for out in range(2):
            start = first + 2 * shard + out * context_shard
            plan.append((n // 2, n, start, context_shard, 0, cols, 2, out * cols))
    cross_query_full, cross_output_full, context_full = place_pieces(
        [part[: 2 * late_rows] for part in late_lanes01]
        + [part[2 * late_rows :] for part in late_lanes01]
        + [part[: 2 * late_rows] for part in late_lanes23]
        + [part[2 * late_rows :] for part in late_lanes23],
        plan,
        places,
        [(width, cols)] * 2 + [(context_width, 2 * cols)],
    )
    context_low = mm(context, context_full).astype(BF16)
    normed_two = jnp.concatenate([normed, over_core(normed)], axis=0)
    cross_query_low = mm(normed_two, cross_query_full).astype(BF16) * jnp.asarray(SCALE, BF16)
    cross_low, cross_logsum = cross_forward(cross_query_low, context_low, context_count)
    partial, send = halves_of(cross_low, cross_output_full)
    cotangents_core = over_core(cotangents)
    partial, send, cotangent3, x_recv, y_recv, cotangents_core = sync(
        partial, send, cotangent3, x_recv, y_recv, cotangents_core
    )
    feed0_over_lanes = [part[:shard] for part in x_recv]
    feed1_lanes = [part[shard:] for part in x_recv]
    feed1_over, feed3_over, feed3 = y_recv[:shard], y_recv[shard:], y_send[shard:]

    recv = over_core(send)
    far_term, cotangent2, feed3_lanes = over_half(for_half(partial, recv)), ring(cotangent1, 1), all_lanes(feed3)
    far_term, cotangent2, feed3_lanes, x_send, y_send = sync(
        far_term,
        cotangent2,
        feed3_lanes,
        jnp.concatenate([feed1_over, feed2], axis=0),
        jnp.concatenate([feed2, *feed3_lanes[1:]], axis=0),
    )

    hidden_two, normed0 = norm_forward(
        own_rows, hidden_one, third_norm_gain, partial, recv, far_term
    )
    normed1, normed3 = ring(normed0, 1), ring(normed0, -1)
    x_recv, y_recv = all_lanes(x_send), over_half(y_send)
    core0 = over_core(jnp.concatenate([cotangent3, cotangent2, normed0], axis=0))
    normed1, normed3, x_recv, y_recv, core0 = sync(normed1, normed3, x_recv, y_recv, core0)
    feed1_over_lanes = [part[:shard] for part in x_recv]
    feed2_lanes = [part[shard:] for part in x_recv]
    feed2_over = y_recv[:shard]
    feed3_lanes_over = [feed3_over] + [
        y_recv[shard * n : shard * (n + 1)] for n in range(1, lane_count)
    ]

    normed2 = ring(normed1, 1)
    feed2_lanes_over = [feed2_over] + [over_half(value) for value in feed2_lanes[1:]]
    core1 = over_core(jnp.concatenate([normed1, normed3], axis=0))
    normed2, feed2_lanes_over, core1 = sync(normed2, feed2_lanes_over, core1)

    core2 = over_core(normed2)
    pieces = [
        piece
        for lanes_pieces, over_pieces in (
            (feed0_lanes, feed0_over_lanes),
            (feed1_lanes, feed1_over_lanes),
            (feed2_lanes, feed2_lanes_over),
            (feed3_lanes, feed3_lanes_over),
        )
        for piece in [part for both in zip(lanes_pieces, over_pieces) for part in both]
    ]
    held = [
        core0, core1, core2, normed0, normed1, normed3, normed2,
        cotangents_core, cotangents, cotangent3, cotangent2,
    ]
    feed_low, both_low, send, mine, normed_three, upstream_all, down_full = feed_forward(
        pieces,
        places,
        held,
        [(0, 2), (1, 0), (1, 1), (2, 0), (3, 0), (4, 0), (5, 0), (6, 0)],
        [(7, 0), (7, 1), (0, 0), (0, 1), (8, 0), (8, 1), (9, 0), (10, 0)],
        shard,
        own_rows,
    )
    feed_low, both_low, send, mine, normed_three, upstream_all, down_full = sync(
        feed_low, both_low, send, mine, normed_three, upstream_all, down_full
    )

    def ring_halves(left, weights):
        count = RING * own_rows
        return mm_nt(left[count:], weights), mm_nt(left[:count], weights).astype(BF16)

    def block_of(mine, recv, back):
        spot = (0, 1, 3, 2)[back]
        part = slice(spot * own_rows, (spot + 1) * own_rows)
        return mine[part] + recv[part].astype(F32)

    def lanes_block(grads, turn):
        place = links.lane_at(turn)
        return jnp.concatenate(
            [
                lax.dynamic_slice_in_dim(grads, (z * lane_count + place) * 2 * shard, 2 * shard, 0)
                for z in (0, 1)
            ],
            axis=0,
        )

    def halves_block(grads, index):
        return jnp.concatenate(
            [
                lax.dynamic_slice_in_dim(
                    grads, ((z * lane_count + n) * 2 + index) * shard, shard, 0
                )
                for z in (2, 3)
                for n in range(lane_count)
            ],
            axis=0,
        )

    def lanes_terms(grads):
        return [lanes_block(grads, turn) for turn in range(1, lane_count)]

    def lanes_second(grads, recv):
        total = (lanes_block(grads, 0).astype(F32) + recv.astype(F32)).reshape(2, 2, shard, -1)
        keep = lax.dynamic_index_in_dim(total, half, 1, keepdims=False)
        send = lax.dynamic_index_in_dim(total, 1 - half, 1, keepdims=False)
        return keep, send.astype(BF16)

    def halves_second(grads, recv):
        total = (halves_block(grads, half).astype(F32) + recv.astype(F32)).reshape(
            2, lane_count, shard, -1
        )
        keep, *send = [
            lax.dynamic_index_in_dim(total, links.lane_at(turn), 1, keepdims=False)
            for turn in range(lane_count)
        ]
        return keep, [term.astype(BF16) for term in send]

    def joined(*terms):
        keep, recv, keep_late, recv_late = terms
        return jnp.concatenate(
            [
                (keep + recv.astype(F32)).astype(BF16),
                (keep_late + recv_late.astype(F32)).astype(BF16),
            ],
            axis=0,
        )

    recv = over_core(send)
    down_grad = mm_tn(upstream_all, feed_low).astype(BF16)
    recv, mine, both_low, normed_three, feed_low, down_grad = sync(
        recv, mine, both_low, normed_three, feed_low, down_grad
    )
    mine, recv, both_low, normed_three, down_grad, down_lanes, down_halves, ring_low = sync(
        mine,
        recv,
        both_low,
        normed_three,
        down_grad,
        lanes_terms(down_grad),
        halves_block(down_grad, 1 - half),
        block_of(mine, recv, 2).astype(BF16),
    )

    two = ring(ring_low, -1)
    down_lanes, down_halves = links.sum_lanes(down_lanes), over_half(down_halves)
    both_grad = mm_tn(normed_three, both_low).astype(BF16)
    out_mine, out_send = ring_halves(feed_low, down_full)
    two, both_grad, down_lanes, down_halves, out_mine, out_send, three = sync(
        two,
        both_grad,
        down_lanes,
        down_halves,
        out_mine,
        out_send,
        block_of(mine, recv, 3).astype(BF16),
    )

    three = ring(three, 1)
    one = ring((block_of(mine, recv, 1) + two.astype(F32)).astype(BF16), -1)
    both_lanes = links.sum_lanes(lanes_terms(both_grad))
    both_halves = over_half(halves_block(both_grad, 1 - half))
    out_recv = over_core(out_send)
    down_keep, down_move = lanes_second(down_grad, down_lanes)
    down_late_keep, down_late_move = halves_second(down_grad, down_halves)
    one, three, both_lanes, both_halves, out_recv, out_low, downs = sync(
        one,
        three,
        both_lanes,
        both_halves,
        out_recv,
        [block_of(out_mine, out_recv, back).astype(BF16) for back in (2, 3)],
        (down_keep, down_move, down_late_keep, down_late_move),
    )
    down_keep, down_move, down_late_keep, down_late_move = downs

    hidden_two_grad, low, third_gain_grad = norm_backward(
        hidden_two, third_norm_gain, upstream, mine, recv, one, three
    )
    low, out_send = lax.optimization_barrier((low, out_low[0]))
    low_over = over_half(low)
    out_two = ring(out_send, -1)
    both_keep, both_move = lanes_second(both_grad, both_lanes)
    both_late_keep, both_late_move = halves_second(both_grad, both_halves)
    low_over, low, out_two, both_keep, both_late_keep, x_send, y_send, out_one = sync(
        low_over,
        low,
        out_two,
        both_keep,
        both_late_keep,
        [jnp.concatenate(pair, axis=-1) for pair in zip(down_late_move, both_late_move)],
        jnp.concatenate([down_move, both_move], axis=-1),
        (block_of(out_mine, out_recv, 1) + out_two.astype(F32)).astype(BF16),
    )

    moved, late_sum, out_three, out_one = (
        over_half(y_send),
        links.sum_lanes(x_send),
        ring(out_low[1], 1),
        ring(out_one, -1),
    )
    branch_two = spread_cores(low, low_over)
    cross_out_grad = mm(branch_two, cross_output_full).astype(BF16)
    cross_query_round, cross_key_back, cross_value_back = cross_backward(
        cross_query_low, context_low, cross_low, cross_out_grad, cross_logsum, context_count
    )
    partial, send = halves_of(cross_query_round, cross_query_full)
    partial, send, moved, late_sum, out_three, out_one, branch_two = sync(
        partial, send, moved, late_sum, out_three, out_one, branch_two
    )
    recv = over_core(send)
    feed_mine = jnp.concatenate(
        [
            joined(down_keep, moved[..., :hidden], down_late_keep, late_sum[..., :hidden]),
            joined(both_keep, moved[..., hidden:], both_late_keep, late_sum[..., hidden:]),
        ],
        axis=2,
    )
    ring_places = jnp.stack(
        [links.place(back, turn) for back in range(RING) for turn in range(lane_count)]
    )

    def by_back(blocks):
        rows = [blocks[back * lane_count : (back + 1) * lane_count] for back in range(RING)]
        return [row[0] for row in rows], [row[1:] for row in rows]

    def below(others, backs):
        return [jnp.concatenate(parts, axis=0) for parts in zip(*[others[back] for back in backs])]

    cross_grads = [
        mm_tn(branch_two, cross_low).astype(BF16),
        mm_tn(normed_two, cross_query_round).astype(BF16),
        mm_tn(context, cross_key_back).astype(BF16),
        mm_tn(context, cross_value_back).astype(BF16),
    ]
    cross_own, cross_other = by_back(split_blocks(cross_grads, ring_places, True))
    recv, feed_mine, feed_send, cross_own, cross_late, cross_most, backs = sync(
        recv,
        feed_mine,
        [
            lax.dynamic_index_in_dim(feed_mine, links.ring_at(back), 0, keepdims=False)
            for back in (1, 2, 3)
        ],
        cross_own,
        below(cross_other, (0, 1)),
        below(cross_other, (2, 3)),
        (cross_key_back, cross_value_back),
    )
    cross_key_back, cross_value_back = backs

    def out_of(values, back):
        return lax.dynamic_index_in_dim(values, links.ring_at(back), 0, keepdims=False)

    half_send = (partial + recv.astype(F32)).astype(BF16)
    half_send, feed_send, cross_most = lax.optimization_barrier((half_send, feed_send, cross_most))
    far_term = over_half(half_send)
    feed1_sum, feed3_sum = ring(feed_send[2], 1), ring(feed_send[0], -1)
    cross_most = links.sum_lanes(cross_most)
    block_rows = cross_most.shape[0] // 2
    far_term, feed1_sum, feed3_sum, cross_two, cross_three, cross_late = sync(
        far_term,
        feed1_sum,
        feed3_sum,
        (cross_own[2].astype(F32) + cross_most[:block_rows].astype(F32)).astype(BF16),
        (cross_own[3].astype(F32) + cross_most[block_rows:].astype(F32)).astype(BF16),
        cross_late,
    )
    hidden_one_grad, low, second_gain_grad = pair_backward(
        second_norm_gain, hidden_one, hidden_two_grad, low_over, partial, recv, far_term
    )

    feed2_sum, cross_two = ring(feed_send[1], 2), ring(cross_two, -1)
    cross_late = links.sum_lanes(cross_late)
    branch_one = jnp.concatenate([low, over_core(low)], axis=0)
    self_out_grad = mm(branch_one, output_full).astype(BF16)
    qkv_round = self_backward(qkv_low, self_low, self_out_grad, self_logsum, tables)
    partial, send = halves_of(qkv_round, qkv_full)
    partial, send, feed2_sum, cross_late, cross_two, qkv_round, branch_one = sync(
        partial, send, feed2_sum, cross_late, cross_two, qkv_round, branch_one
    )
    output_grad = mm_tn(branch_one, self_low).astype(BF16)
    qkv_grad = mm_tn(normed_one, qkv_round).astype(BF16)
    self_own, self_other = by_back(split_blocks([output_grad, qkv_grad], ring_places, False))
    cross_zero = cross_own[0].astype(F32) + cross_late[:block_rows].astype(F32)
    cross_one = cross_own[1].astype(F32) + cross_late[block_rows:].astype(F32)
    cross_three = ring(cross_three, 1)
    recv, cross_three, self_own, self_other, cross_zero, cross_one, backs = sync(
        over_core(send),
        cross_three,
        self_own,
        self_other,
        cross_zero,
        (cross_one + cross_two.astype(F32)).astype(BF16),
        (cross_key_back, cross_value_back),
    )
    cross_key_back, cross_value_back = backs

    half_send = for_half(partial, recv)
    half_send, cross_one, self_send = lax.optimization_barrier(
        (half_send, cross_one, self_other[2])
    )
    far_term = over_half(half_send)
    cross_one = ring(cross_one, -1)
    self2 = links.sum_lanes(self_send)
    context_term = (
        mm_nt(cross_key_back, context_full[:, :cols])
        + mm_nt(cross_value_back, context_full[:, cols:])
    )[:context_count]
    context_recv = over_core(context_term.astype(BF16))
    far_term, cross_one, self2, context_term, context_recv, self_two = sync(
        far_term,
        cross_one,
        self2,
        context_term,
        context_recv,
        (self_own[2].astype(F32) + self2.astype(F32)).astype(BF16),
    )

    self3 = links.sum_lanes(self_other[3])
    self_two = ring(self_two, -1)
    context_low_sum = (context_term + context_recv.astype(F32)).astype(BF16)
    context_over = over_half(context_low_sum)
    inputs_grad, _, first_gain_grad = norm_backward(
        own, first_norm_gain, hidden_one_grad, partial, recv, far_term
    )
    layer_result = links.both_cores(
        hidden_two + block_of(out_mine, out_recv, 0) + out_one.astype(F32) + out_three.astype(F32)
    )
    gain_grads = jnp.concatenate([first_gain_grad, second_gain_grad, third_gain_grad], axis=0)
    gate_sum, up_sum, down_sum = spread(
        [out_of(feed_mine, 0), feed1_sum, feed2_sum, feed3_sum],
        jnp.stack([links.ring_at(back) for back in range(RING)]),
    )
    cross_total = cross_zero + cross_one.astype(F32) + cross_three.astype(F32)
    sizes = (shard, shard, context_shard, context_shard)
    starts = [2 * sum(sizes[:n]) for n in range(4)]
    cross_total = jnp.concatenate(
        [
            cross_total[start : start + 2 * size].reshape(2, size, cols)
            for start, size in zip(starts, sizes)
        ],
        axis=1,
    )
    gain_grads = gain_grads + over_core(gain_grads)
    gain_grads = gain_grads + over_half(gain_grads)
    context_grad = context_low_sum.astype(F32) + context_over.astype(F32)
    self3, self_two, context_grad, layer_result, gain_grads, inputs_grad, feed_sums, cross_total, self_three = sync(
        self3,
        self_two,
        context_grad,
        layer_result,
        gain_grads,
        inputs_grad,
        (gate_sum, up_sum, down_sum),
        cross_total,
        (self_own[3].astype(F32) + self3.astype(F32)).astype(BF16),
    )
    gate_sum, up_sum, down_sum = feed_sums

    self1 = links.sum_lanes(self_other[1])
    self_three = ring(self_three, 1)
    gain_lanes = (
        gain_grads.reshape(3, RING, lane_count, -1).swapaxes(1, 2).reshape(3, -1)
    )
    gain_total = slot(gain_lanes, lane_count, links.lane_at(1))
    for turn in list(range(2, lane_count)) + [0]:
        gain_total = links.lanes(gain_total) + slot(gain_lanes, lane_count, links.lane_at(turn))
    gain_ring = [slot(gain_total, RING, links.ring_at(back)) for back in range(RING)]
    gain_two, gain_three = ring(gain_ring[2], -1), ring(gain_ring[3], 1)
    cross_keep, cross_recv = links.swap_halves(cross_total)
    self1, self_three, gain_two, gain_three, cross_recv, self_one = sync(
        self1,
        self_three,
        gain_two,
        gain_three,
        cross_recv,
        (self_own[1].astype(F32) + self1.astype(F32) + self_two.astype(F32)).astype(BF16),
    )

    self0 = links.sum_lanes(self_other[0])
    self_one = ring(self_one, -1)
    inputs_result = links.both_cores(inputs_grad)
    gain_send, inputs_result = lax.optimization_barrier((gain_ring[1] + gain_two, inputs_result))
    gain_one = ring(gain_send, -1)
    cross_sums = links.side_by_side(cross_keep, cross_recv)
    gain_sums = slot(gain_ring[0] + gain_one + gain_three, 2, half)
    self0, self_one, gain_sums, inputs_result, cross_sums = sync(
        self0, self_one, gain_sums, inputs_result, cross_sums
    )

    self_total = (
        self_own[0].astype(F32) + self0.astype(F32) + self_one.astype(F32) + self_three.astype(F32)
    )
    keep, recv = links.swap_halves(self_total.reshape(2, shard, 4 * cols))

    def of_self(values, n):
        if n == 3:
            return values[:, :cols]
        return jnp.concatenate(
            [
                values[:, cols + (3 * pair + n) * PAIR : cols + (3 * pair + n + 1) * PAIR]
                for pair in range(pairs)
            ],
            axis=1,
        )

    query_sum, key_sum, value_sum, output_sum = (
        links.side_by_side(of_self(keep, n), of_self(recv, n)) for n in range(4)
    )
    return (
        layer_result[None],
        inputs_result[None],
        context_grad[None],
        query_sum,
        key_sum,
        value_sum,
        output_sum.T,
        cross_sums[shard : 2 * shard],
        cross_sums[2 * shard : 2 * shard + context_shard],
        cross_sums[2 * shard + context_shard :],
        cross_sums[:shard].T,
        gate_sum,
        up_sum,
        down_sum.T,
        gain_sums[0],
        gain_sums[1],
        gain_sums[2],
    )


def solution(mesh):
    row = P(("fsdp", "ctx"), "tp")
    col = P("tp", ("fsdp", "ctx"))
    gain = P(("fsdp", "ctx"))
    token = P("fsdp", "ctx", None)
    context = P("fsdp", None, None)
    weights = (row, row, row, col, row, row, row, col, row, row, col, gain, gain, gain)
    return jax.shard_map(
        functools.partial(on_device, mesh),
        mesh=mesh,
        in_specs=(token, context) + weights + (token,),
        out_specs=(token, token, context) + weights,
        check_vma=False,
    )
```
